32 devices in a mesh: groups: 2 (over x), mem: 8 (over z, y), tp: 2 (over core).
Axes of the slice: x: 2, y: 2, z: 4, core: 2. Of those that a mesh axis runs over, the one named last changes fastest.
Arguments:
- questions: bfloat16 [16, 32, 2048], P(('groups', 'mem'), None, 'tp'), parts along dimension 0
- memory: bfloat16 [128, 128, 2048], P('mem', None, 'tp')
- retrieved: int32 [16, 12], P(('groups', 'mem')), parts along dimension 0, may hold values from 0 to 127, as said below
- q_len: int32 [16], P(('groups', 'mem')), parts along dimension 0, may hold values from 8 to 32
- p_len: int32 [128], P('mem'), may hold values from 32 to 128
- norm_gain: bfloat16 [2048], replicated, may hold values from 0.099609375 to 1.8984375
- w_query: bfloat16 [2048, 2048], P(None, 'tp')
- w_key: bfloat16 [2048, 2048], P(None, 'tp')
- w_value: bfloat16 [2048, 2048], P(None, 'tp'), may hold values from -0.125 to 0.125
- w_out: bfloat16 [2048, 2048], P('tp'), may hold values from -0.75 to 0.75
Outputs:
- encoded: bfloat16 [16, 12, 160, 2048], P(('groups', 'mem'), None, None, 'tp'), parts along dimension 0
The draws below stay inside these ranges and needn't reach their ends.
There are 2 independent parts, one for each index of `groups`. The reference program is written for one: setup_inputs(seed, part) draws one part's arguments, and reference() takes and returns one part's arrays. A program takes and returns all parts, laid end to end along the dimension named above; an argument that names none is the same for every part. Nothing has to cross between parts.
Inputs may be any that keep to these rules, and one draw needn't show every extreme that they name: `retrieved`: passage i lies on memory shard i // 16. Among the 12 ids of one device's questions, counting repeats, at most 2 lie on any one shard, and every device has 2 on some shard.
All inputs are finite; a program needn't handle non-finite values.
Results may differ from the reference program's by a relative error of at most 0.0075.
Values may be sent and summed in bfloat16 or wider, within the bound.
No kernel may reach another device: no remote copies, remote signals or barrier semaphores. Data moves between devices by JAX's collectives and lax.ppermute only.
A program may use at most 192 MiB of HBM per device.

```python
import math
import jax
import jax.numpy as jnp
from jax import lax

D = 2048
HEADS = 32
HS = 64
LQ = 32
LP = 128
K = 12
QD = 1
P_DEV = 16
CAPM = 2
QUESTIONS = 8
PASSAGES = 128
N_TP = 2


def log_uniform(key, shape, low, high):
    return jnp.exp(jax.random.uniform(key, shape, jnp.float32, math.log(low), math.log(high)))


def draw_questions(key, part):
    key = jax.random.fold_in(key, 22)
    first, second, third = jax.random.split(key, 3)
    shape = (QUESTIONS, LQ, D)
    base = jax.random.normal(first, shape, jnp.float32)
    rows = log_uniform(second, (QUESTIONS, LQ, 1), 0.3, 3.0)
    columns = log_uniform(third, (D,), 0.4, 4.0)
    return (base * rows * columns).astype(jnp.bfloat16)


def draw_memory(key, part):
    key = jax.random.fold_in(key, 21)
    first, second, third = jax.random.split(key, 3)
    shape = (PASSAGES, LP, D)
    base = jax.random.normal(first, shape, jnp.float32)
    rows = log_uniform(second, (PASSAGES, LP, 1), 0.3, 3.0)
    columns = log_uniform(third, (D,), 0.4, 4.0)
    return (base * rows * columns).astype(jnp.bfloat16)


def draw_retrieved(key, part):
    key = jax.random.fold_in(key, 41)
    shard_count = QUESTIONS // QD
    per_device = QD * K
    keys = jax.random.split(key, 4)
    favoured = jax.random.randint(keys[0], (shard_count,), 0, shard_count)

    def one_device(device_key, first_shard):
        spread = jax.random.permutation(device_key, (shard_count - 1) * CAPM)[:per_device - CAPM] // CAPM
        others = (first_shard + 1 + spread) % shard_count
        return jnp.concatenate([jnp.full((CAPM,), first_shard, jnp.int32), others.astype(jnp.int32)])
    shard_ids = jax.vmap(one_device)(jax.random.split(keys[1], shard_count), favoured)
    shuffle = jax.vmap(lambda device_key: jax.random.permutation(device_key, per_device))(jax.random.split(keys[2], shard_count))
    shard_ids = jnp.take_along_axis(shard_ids, shuffle, axis=1)
    local_ids = jax.random.randint(keys[3], (shard_count, per_device), 0, P_DEV)
    return (shard_ids * P_DEV + local_ids).reshape(QUESTIONS, K).astype(jnp.int32)


def draw_q_len(key, part):
    key = jax.random.fold_in(key, 31)
    first, second = jax.random.split(key)
    counts = jax.random.randint(first, (QUESTIONS,), LQ // 4, LQ + 1)
    spots = jax.random.permutation(second, QUESTIONS)
    return counts.at[spots[0]].set(LQ).at[spots[1]].set(LQ // 4).astype(jnp.int32)


def draw_p_len(key, part):
    key = jax.random.fold_in(key, 32)
    first, second = jax.random.split(key)
    counts = jax.random.randint(first, (PASSAGES,), LP // 4, LP + 1)
    spots = jax.random.permutation(second, PASSAGES)
    return counts.at[spots[0]].set(LP).at[spots[1]].set(LP // 4).astype(jnp.int32)


def draw_w_query(key, part):
    key = jax.random.fold_in(key, 51)
    matrix = jax.random.normal(key, (D, HEADS * HS), jnp.float32)
    return (matrix / math.sqrt(D)).astype(jnp.bfloat16)


def draw_w_key(key, part):
    key = jax.random.fold_in(key, 52)
    matrix = jax.random.normal(key, (D, HEADS * HS), jnp.float32)
    return (matrix / math.sqrt(D)).astype(jnp.bfloat16)


def shard_levels(rng, dims, cuts, smallest, largest):
    def one(axis_at, parts):
        heights = jax.random.uniform(jax.random.fold_in(jax.random.fold_in(rng, 6), axis_at), (parts,), jnp.float32, smallest / len(cuts), largest / len(cuts))
        return jnp.repeat(jnp.exp(heights), dims[axis_at] // parts).reshape((-1,) + (1,) * (len(dims) - axis_at - 1))

    factor_of = one(*cuts[0])
    for cut in cuts[1:]:
        factor_of = factor_of * one(*cut)
    return factor_of


def normal_values(own_key, extent, scale, reach, pieces=(), held_as=jnp.bfloat16):
    values = scale * jax.random.normal(own_key, extent, jnp.float32)
    if pieces:
        values = values * shard_levels(own_key, extent, pieces, -0.22, 0.18)
    return jnp.clip(values, -reach, reach).astype(held_as)


def setup_inputs(seed: int = 0, part: int = 0) -> dict:
    seeds = jax.random.split(jax.random.key(seed), 11)
    part_splits = jax.random.split(jax.random.fold_in(seeds[10], part), 11)
    questions = draw_questions(jax.random.fold_in(jax.random.fold_in(seeds[10], part), 71), part)
    memory = draw_memory(jax.random.fold_in(seeds[10], 71), part)
    retrieved = draw_retrieved(jax.random.fold_in(jax.random.fold_in(seeds[10], part), 71), part)
    q_len = draw_q_len(jax.random.fold_in(jax.random.fold_in(seeds[10], part), 71), part)
    p_len = draw_p_len(jax.random.fold_in(seeds[10], 71), part)
    norm_gain = jnp.clip(1.0 + 0.18 * jax.random.normal(seeds[5], (D,), jnp.float32), 0.099609375, 1.8984375).astype(jnp.bfloat16)
    w_query = draw_w_query(jax.random.fold_in(seeds[10], 71), part)
    w_key = draw_w_key(jax.random.fold_in(seeds[10], 71), part)
    w_value = normal_values(seeds[8], (D, HEADS * HS), D ** -0.5, 0.125, ((1, 2),))
    w_out = normal_values(seeds[9], (HEADS * HS, D), HS ** -0.5, 0.75, ((0, 2),))
    return {"questions": questions, "memory": memory, "retrieved": retrieved, "q_len": q_len, "p_len": p_len, "norm_gain": norm_gain, "w_query": w_query, "w_key": w_key, "w_value": w_value, "w_out": w_out}


def encode_block(pair_rows, qlen_pair, plen_pair, norm_gain, w_query, w_key, w_value, w_out):
    count, total_len, width = pair_rows.shape
    spots = jnp.arange(total_len, dtype=jnp.int32)[None, :]
    usable = jnp.where(spots < LQ, spots < qlen_pair[:, None], spots - LQ < plen_pair[:, None])
    widened = pair_rows.astype(jnp.float32)
    scale_sq = lax.optimization_barrier(jnp.mean(widened * widened, axis=2, keepdims=True))
    normed = (widened * lax.rsqrt(scale_sq + 1e-06) * norm_gain.astype(jnp.float32)).astype(jnp.bfloat16)
    flat_rows = normed.reshape(count * total_len, width)

    def project(weight):
        made = jnp.dot(flat_rows, weight, preferred_element_type=jnp.float32).astype(jnp.bfloat16)
        return made.reshape(count, total_len, HEADS, HS)
    query_heads = project(w_query)
    key_heads = project(w_key)
    value_heads = project(w_value)
    scores = jnp.einsum('bqhd,bkhd->bhqk', query_heads.astype(jnp.float32), key_heads.astype(jnp.float32))
    scores = scores * (1.0 / math.sqrt(HS))
    scores = jnp.where(usable[:, None, None, :], scores, -1e+30)
    row_max = lax.optimization_barrier(jnp.max(scores, axis=3, keepdims=True))
    raised = jnp.exp(scores - row_max)
    attention_weights = (raised / lax.optimization_barrier(jnp.sum(raised, axis=3, keepdims=True))).astype(jnp.bfloat16)
    attended = jnp.einsum('bhqk,bkhd->bqhd', attention_weights.astype(jnp.float32), value_heads.astype(jnp.float32))
    attended = attended.astype(jnp.bfloat16).reshape(count * total_len, HEADS * HS)
    group_cols = HEADS * HS // N_TP
    branch = jnp.zeros((count * total_len, width), jnp.float32)
    for group in range(N_TP):
        term = jnp.dot(attended[:, group * group_cols:(group + 1) * group_cols], w_out[group * group_cols:(group + 1) * group_cols], preferred_element_type=jnp.float32).astype(jnp.bfloat16)
        term = lax.optimization_barrier(term)
        branch = branch + term.astype(jnp.float32)
    branch = branch.reshape(count, total_len, width)
    return ((widened + branch) * usable[:, :, None].astype(jnp.float32)).astype(jnp.bfloat16)

def reference(questions, memory, retrieved, q_len, p_len, norm_gain, w_query, w_key, w_value, w_out):

    def one_question(question):
        chosen = retrieved[question]
        passage_rows = memory[chosen]
        question_rows = jnp.broadcast_to(questions[question][None], (K, LQ, D))
        pair_rows = jnp.concatenate([question_rows, passage_rows], axis=1)
        qlen_pair = jnp.broadcast_to(q_len[question], (K,))
        return encode_block(pair_rows, qlen_pair, p_len[chosen], norm_gain, w_query, w_key, w_value, w_out)
    return lax.map(one_question, jnp.arange(QUESTIONS, dtype=jnp.int32))
```

```python
import functools

import jax
import jax.numpy as jnp
from jax import lax
from jax.experimental import pallas as pl
from jax.experimental.pallas import tpu as pltpu
from jax.sharding import PartitionSpec as P

HS = 64
CAPM = 2
EPS = 1e-06
MASKED = -1e30
LANES = 128
VMEM_LIMIT = 56 * 1024 * 1024

ANY = pl.BlockSpec(memory_space=pl.ANY)
SMEM = pl.BlockSpec(memory_space=pltpu.SMEM)
VMEM = pl.BlockSpec(memory_space=pltpu.VMEM)


def pick_kernel(shards, pass_dev, wants, own_ref, *refs):
    metas = refs[:shards]
    memory = refs[shards]
    outs = refs[shards + 1 : 2 * shards + 1]
    table = refs[2 * shards + 1]
    sems = refs[2 * shards + 2]
    me = own_ref[0, 1]
    low = me * pass_dev
    counts = []
    for k in range(shards):

        def ask(j, count):
            local = metas[k][0, j] - low
            mine = jnp.logical_and(local >= 0, local < pass_dev)

            @pl.when(mine)
            def _():
                pltpu.make_async_copy(
                    memory.at[local], outs[k].at[count], sems.at[k, count]
                ).start()

            return count + mine.astype(jnp.int32)

        counts.append(lax.fori_loop(0, wants, ask, jnp.int32(0)))
    for k in range(shards):
        partner_low = lax.bitwise_xor(me, k) * pass_dev
        for r in range(CAPM):
            table[0, CAPM * k + r] = jnp.int32(-1)
            table[1, CAPM * k + r] = jnp.int32(0)

        def place(j, count):
            local = metas[0][0, j] - partner_low
            theirs = jnp.logical_and(local >= 0, local < pass_dev)

            @pl.when(theirs)
            def _():
                table[0, CAPM * k + count] = j
                table[1, CAPM * k + count] = metas[k][0, wants + local]

            return count + theirs.astype(jnp.int32)

        lax.fori_loop(0, wants, place, jnp.int32(0))
    for k in range(shards):
        for r in range(CAPM):

            @pl.when(r < counts[k])
            def _():
                pltpu.make_async_copy(memory.at[0], outs[k].at[r], sems.at[k, r]).wait()


def pick(own, metas, memory, wants):
    shards = len(metas)
    pass_dev, p_tokens, half = memory.shape
    slot = jax.ShapeDtypeStruct((CAPM, p_tokens, half), memory.dtype)
    result = pl.pallas_call(
        functools.partial(pick_kernel, shards, pass_dev, wants),
        out_shape=[slot] * shards + [jax.ShapeDtypeStruct((2, LANES), jnp.int32)],
        in_specs=[SMEM] * (shards + 1) + [ANY],
        out_specs=[ANY] * shards + [SMEM],
        scratch_shapes=[pltpu.SemaphoreType.DMA((shards, CAPM))],
        cost_estimate=pl.CostEstimate(
            flops=0, bytes_accessed=2 * shards * CAPM * p_tokens * half * 2, transcendentals=0
        ),
        name="pick",
    )(own, *metas, memory)
    return result[:shards], result[shards]


def normed_halves(own, other, gain_own, gain_other):
    own = own.astype(jnp.float32)
    other = other.astype(jnp.float32)
    total = jnp.sum(own * own + other * other, axis=-1, keepdims=True)
    scale = lax.rsqrt(total / (2 * own.shape[-1]) + EPS)
    return (
        (own * scale * gain_own).astype(jnp.bfloat16),
        (other * scale * gain_other).astype(jnp.bfloat16),
    )


def weight_copies(c, half, sources, targets, sems):
    copies = []
    for i, (source, target) in enumerate(zip(sources, targets)):
        pieces = []
        for part, core in enumerate((c, 1 - c)):
            start = pl.multiple_of(core * half, half)
            pieces.append(
                pltpu.make_async_copy(
                    source.at[pl.ds(start, half), :],
                    target.at[pl.ds(part * half, half), :],
                    sems.at[i, part],
                )
            )
        copies.append(pieces)
    return copies


def question_kernel(own_ref, mine, theirs, gain, wq, wk, wv, out, vq, vk, vv, sems):
    c = own_ref[0, 0]
    half = mine.shape[-1]
    copies = weight_copies(c, half, (wq, wk, wv), (vq, vk, vv), sems)
    for pieces in copies:
        for piece in pieces:
            piece.start()
    g_own = gain[c].astype(jnp.float32)
    g_other = gain[1 - c].astype(jnp.float32)
    first, second = normed_halves(mine[0], theirs[0], g_own, g_other)
    rows = jnp.concatenate([first, second], axis=1)
    for i, weight in enumerate((vq, vk, vv)):
        for piece in copies[i]:
            piece.wait()
        made = jnp.dot(rows, weight[...], preferred_element_type=jnp.float32)
        made = made.astype(jnp.bfloat16)
        if i == 0:
            made = made * jnp.bfloat16(1.0 / 8.0)
        out[i] = made


def project_question(own, mine, theirs, gain, wq, wk, wv):
    _, q_tokens, half = mine.shape
    width, cols = wq.shape
    weight = pltpu.VMEM((width, cols), jnp.bfloat16)
    return pl.pallas_call(
        question_kernel,
        out_shape=jax.ShapeDtypeStruct((3, q_tokens, cols), jnp.bfloat16),
        in_specs=[SMEM, VMEM, VMEM, VMEM, ANY, ANY, ANY],
        out_specs=VMEM,
        scratch_shapes=[weight] * 3 + [pltpu.SemaphoreType.DMA((3, 2))],
        compiler_params=pltpu.CompilerParams(vmem_limit_bytes=VMEM_LIMIT),
        cost_estimate=pl.CostEstimate(
            flops=6 * q_tokens * width * cols, bytes_accessed=6 * width * cols, transcendentals=0
        ),
        name="question_projections",
    )(own, mine, theirs, gain, wq, wk, wv)


def layer_kernel(ks, own_ref, table, question, gain, *refs):
    n = len(ks)
    mine, theirs = refs[:n], refs[n : 2 * n]
    wq, wk, wv, wo = refs[2 * n : 2 * n + 4]
    out_own, out_other = refs[2 * n + 4 : 2 * n + 6]
    vq, vk, vv, vo, rows, query, key, value, attended, sems, sems_out = refs[2 * n + 6 :]
    slots, total, cols = query.shape
    q_tokens = question.shape[1]
    p_tokens = total - q_tokens
    half = mine[0].shape[-1]
    c = own_ref[0, 0]
    q_len = own_ref[0, 2]
    copies = weight_copies(c, half, (wq, wk, wv), (vq, vk, vv), sems)
    out_copies = []
    for part, core in enumerate((1 - c, c)):
        start = pl.multiple_of(core * half, half)
        out_copies.append(
            pltpu.make_async_copy(wo.at[:, pl.ds(start, half)], vo.at[part], sems_out.at[part])
        )
    for pieces in copies + [out_copies]:
        for piece in pieces:
            piece.start()
    g_own = gain[c].astype(jnp.float32)
    g_other = gain[1 - c].astype(jnp.float32)
    for i in range(n):
        for r in range(CAPM):
            first, second = normed_halves(mine[i][r], theirs[i][r], g_own, g_other)
            at = pl.ds((CAPM * i + r) * p_tokens, p_tokens)
            rows[at, :half] = first
            rows[at, half:] = second
    for i, (weight, target) in enumerate(((vq, query), (vk, key), (vv, value))):
        for piece in copies[i]:
            piece.wait()
        for s in range(slots):
            target[s, :q_tokens, :] = question[i]
        for left in range(0, cols, 256):
            span = slice(left, left + 256)
            made = jnp.dot(rows[...], weight[:, span], preferred_element_type=jnp.float32)
            made = made.astype(jnp.bfloat16)
            if i == 0:
                made = made * jnp.bfloat16(1.0 / 8.0)
            for s in range(slots):
                target[s, q_tokens:, span] = made[s * p_tokens : (s + 1) * p_tokens]

    lane = lax.broadcasted_iota(jnp.int32, (1, 2 * HS), 1)
    in_first = lane < HS
    spot = lax.broadcasted_iota(jnp.int32, (1, total), 1)
    ones = jnp.ones((total, 2 * HS), jnp.bfloat16)

    def attend(s, carry):
        slot = CAPM * ks[0] + s
        p_len = table[1, slot]

        @pl.when(p_len > 0)
        def _():
            end = jnp.where(spot < q_tokens, q_len, q_tokens + p_len)
            bias = jnp.where(spot < end, 0.0, MASKED)
            for left in range(0, cols, 2 * HS):
                span = slice(left, left + 2 * HS)
                q2 = query[s, :, span]
                zero = jnp.zeros_like(q2)
                q2 = jnp.concatenate(
                    [jnp.where(in_first, q2, zero), jnp.where(in_first, zero, q2)], axis=0
                )
                scores = lax.dot_general(
                    q2,
                    key[s, :, span],
                    (((1,), (1,)), ((), ())),
                    preferred_element_type=jnp.float32,
                )
                scores = scores + bias
                raised = jnp.exp(scores - jnp.max(scores, axis=1, keepdims=True))
                with_sum = jnp.dot(
                    raised.astype(jnp.bfloat16),
                    jnp.concatenate([value[s, :, span], ones], axis=1),
                    preferred_element_type=jnp.float32,
                )
                mixed = with_sum[:, : 2 * HS] / with_sum[:, 2 * HS :]
                attended[s, :, span] = jnp.where(
                    in_first, mixed[:total], mixed[total:]
                ).astype(jnp.bfloat16)

        return carry

    lax.fori_loop(0, slots, attend, 0)
    for part, out in enumerate((out_other, out_own)):
        out_copies[part].wait()
        flat = attended[...].reshape(slots * total, cols)
        for left in range(0, half, 256):
            span = slice(left, left + 256)
            made = jnp.dot(flat, vo[part, :, span], preferred_element_type=jnp.float32)
            out[:, :, span] = made.astype(jnp.bfloat16).reshape(slots, total, 256)


def layer(ks, own, table, question, gain, mine, theirs, wq, wk, wv, wo):
    _, p_tokens, half = mine[0].shape
    _, q_tokens, cols = question.shape
    width = wq.shape[0]
    slots = CAPM * len(ks)
    total = q_tokens + p_tokens
    weight = pltpu.VMEM((width, cols), jnp.bfloat16)
    split = pltpu.VMEM((slots, total, cols), jnp.bfloat16)
    out = jax.ShapeDtypeStruct((slots, total, half), jnp.bfloat16)
    return pl.pallas_call(
        functools.partial(layer_kernel, ks),
        out_shape=[out, out],
        in_specs=[SMEM, SMEM, VMEM, VMEM] + [VMEM] * (2 * len(ks)) + [ANY] * 4,
        out_specs=[VMEM, VMEM],
        scratch_shapes=[weight] * 3
        + [
            pltpu.VMEM((2, cols, half), jnp.bfloat16),
            pltpu.VMEM((slots * p_tokens, width), jnp.bfloat16),
            split,
            split,
            split,
            split,
            pltpu.SemaphoreType.DMA((3, 2)),
            pltpu.SemaphoreType.DMA((2,)),
        ],
        compiler_params=pltpu.CompilerParams(vmem_limit_bytes=VMEM_LIMIT),
        cost_estimate=pl.CostEstimate(
            flops=slots * (6 * p_tokens * width * cols + 4 * total * cols * half),
            bytes_accessed=8 * width * cols,
            transcendentals=slots * total * total * cols // HS,
        ),
        name="layer",
    )(own, table, question, gain, *mine, *theirs, wq, wk, wv, wo)


def combine_kernel(ks, first, own_ref, table, questions, *refs):
    n = len(ks)
    mine = refs[:n]
    ours, arrived = refs[n : n + 2]
    encoded, staged, sems = refs[n + 2 if first else n + 3 :]
    slots, total, _ = ours.shape
    q_tokens = questions.shape[1]
    q_len = own_ref[0, 2]

    def copy(s, pair):
        return pltpu.make_async_copy(staged.at[s], encoded.at[0, pair], sems.at[s])

    for s in range(slots):
        pair = table[0, CAPM * ks[0] + s]
        p_len = table[1, CAPM * ks[0] + s]

        @pl.when(pair >= 0)
        def _():
            for rows, at, length in (
                (questions[0], slice(0, q_tokens), q_len),
                (mine[s // CAPM][s % CAPM], slice(q_tokens, total), p_len),
            ):
                spot = lax.broadcasted_iota(jnp.int32, (rows.shape[0], 1), 0)
                branch = ours[s, at].astype(jnp.float32) + arrived[s, at].astype(jnp.float32)
                made = rows.astype(jnp.float32) + branch
                staged[s, at] = jnp.where(spot < length, made, 0.0).astype(jnp.bfloat16)
            copy(s, pair).start()

    for s in range(slots):

        @pl.when(table[0, CAPM * ks[0] + s] >= 0)
        def _():
            copy(s, 0).wait()


def combine(ks, encoded, shape, own, table, questions, mine, ours, arrived):
    first = encoded is None
    operands = [own, table, questions, *mine, ours, arrived] + ([] if first else [encoded])
    return pl.pallas_call(
        functools.partial(combine_kernel, ks, first),
        out_shape=jax.ShapeDtypeStruct(shape, jnp.bfloat16),
        in_specs=[SMEM, SMEM, VMEM] + [VMEM] * (len(ks) + 2) + ([] if first else [ANY]),
        out_specs=ANY,
        scratch_shapes=[
            pltpu.VMEM(ours.shape, jnp.bfloat16),
            pltpu.SemaphoreType.DMA((ours.shape[0],)),
        ],
        input_output_aliases={} if first else {len(operands) - 1: 0},
        compiler_params=pltpu.CompilerParams(vmem_limit_bytes=VMEM_LIMIT),
        cost_estimate=pl.CostEstimate(
            flops=0, bytes_accessed=8 * ours.size, transcendentals=0
        ),
        name="combine",
    )(*operands)


def body(questions, memory, retrieved, q_len, p_len, norm_gain, w_query, w_key, w_value, w_out):
    shards = lax.axis_size("mem")
    cores = lax.axis_size("tp")
    _, q_tokens, half = questions.shape
    pass_dev, p_tokens, _ = memory.shape
    wants = retrieved.shape[1]

    def swap(x):
        return lax.ppermute(x, "tp", [(i, (i + 1) % cores) for i in range(cores)])

    def exchange(x, k):
        return lax.ppermute(x, "mem", [(i, i ^ k) for i in range(shards)])

    meta = jnp.concatenate(
        [retrieved[0], p_len, jnp.zeros((LANES - wants - pass_dev,), jnp.int32)]
    )[None]
    metas = [meta] + [exchange(meta, k) for k in range(1, shards)]
    own = jnp.concatenate(
        [
            lax.axis_index("tp").astype(jnp.int32)[None],
            lax.axis_index("mem").astype(jnp.int32)[None],
            q_len,
            jnp.zeros((LANES - 3,), jnp.int32),
        ]
    )[None]
    gain = norm_gain.reshape(cores, 1, half)
    question = project_question(
        own, questions, swap(questions), gain, w_query, w_key, w_value
    )
    sends, table = pick(own, metas, memory, wants)
    mine = [sends[0]] + [exchange(sends[k], k) for k in range(1, shards)]
    encoded = None
    shape = (1, wants, q_tokens + p_tokens, half)
    for low in range(0, shards, 2):
        ks = tuple(range(low, low + 2))
        rows = [mine[k] for k in ks]
        theirs = [swap(x) for x in rows]
        ours, other = layer(
            ks, own, table, question, gain, rows, theirs, w_query, w_key, w_value, w_out
        )
        encoded = combine(ks, encoded, shape, own, table, questions, rows, ours, swap(other))
    return encoded


def solution(mesh):
    in_specs = (
        P(("groups", "mem"), None, "tp"),
        P("mem", None, "tp"),
        P(("groups", "mem"), None),
        P(("groups", "mem")),
        P("mem"),
        P(),
        P(None, "tp"),
        P(None, "tp"),
        P(None, "tp"),
        P("tp", None),
    )
    out_specs = P(("groups", "mem"), None, None, "tp")
    return jax.shard_map(body, mesh=mesh, in_specs=in_specs, out_specs=out_specs, check_vma=False)
```

```python
import functools

import jax
import jax.numpy as jnp
from jax import lax
from jax.experimental import pallas as pl
from jax.experimental.pallas import tpu as pltpu
from jax.sharding import PartitionSpec as P

HS = 64
CAPM = 2
EPS = 1e-06
MASKED = -1e30
LANES = 128
PACK = 16
VMEM_LARGE = 40 * 1024 * 1024
VMEM_SMALL = 20 * 1024 * 1024

ANY = pl.BlockSpec(memory_space=pl.ANY)
SMEM = pl.BlockSpec(memory_space=pltpu.SMEM)
VMEM = pl.BlockSpec(memory_space=pltpu.VMEM)


def pick_kernel(shards, pass_dev, wants, own_ref, metas, memory, *refs):
    outs = refs[:shards]
    table, sems = refs[shards:]
    me = own_ref[0, 1]
    low = me * pass_dev
    counts = []
    for k in range(shards):
        partner = lax.bitwise_xor(me, k)

        def ask(j, count):
            local = metas[partner, 0, j] - low
            mine = jnp.logical_and(local >= 0, local < pass_dev)

            @pl.when(mine)
            def _():
                pltpu.make_async_copy(
                    memory.at[local], outs[k].at[count], sems.at[k, count]
                ).start()

            return count + mine.astype(jnp.int32)

        counts.append(lax.fori_loop(0, wants, ask, jnp.int32(0)))
    for k in range(shards):
        partner = lax.bitwise_xor(me, k)
        for r in range(CAPM):
            table[0, CAPM * k + r] = jnp.int32(-1)
            table[1, CAPM * k + r] = jnp.int32(0)

        def place(j, count):
            local = metas[me, 0, j] - partner * pass_dev
            theirs = jnp.logical_and(local >= 0, local < pass_dev)

            @pl.when(theirs)
            def _():
                table[0, CAPM * k + count] = j
                table[1, CAPM * k + count] = metas[partner, 0, wants + local]

            return count + theirs.astype(jnp.int32)

        lax.fori_loop(0, wants, place, jnp.int32(0))
    for k in range(shards):
        for r in range(CAPM):

            @pl.when(r < counts[k])
            def _():
                pltpu.make_async_copy(memory.at[0], outs[k].at[r], sems.at[k, r]).wait()


def pick(own, metas, memory, wants):
    shards = metas.shape[0]
    pass_dev, p_tokens, half = memory.shape
    slot = jax.ShapeDtypeStruct((CAPM, p_tokens, half), memory.dtype)
    result = pl.pallas_call(
        functools.partial(pick_kernel, shards, pass_dev, wants),
        out_shape=[slot] * shards + [jax.ShapeDtypeStruct((2, LANES), jnp.int32)],
        in_specs=[SMEM, SMEM, ANY],
        out_specs=[VMEM] * shards + [SMEM],
        scratch_shapes=[pltpu.SemaphoreType.DMA((shards, CAPM))],
        compiler_params=pltpu.CompilerParams(vmem_limit_bytes=VMEM_SMALL),
        cost_estimate=pl.CostEstimate(
            flops=0, bytes_accessed=2 * shards * CAPM * p_tokens * half * 2, transcendentals=0
        ),
        name="pick",
    )(own, metas, memory)
    return result[:shards], result[shards]


def normed_halves(own, other, gain_own, gain_other):
    own = own.astype(jnp.float32)
    other = other.astype(jnp.float32)
    total = jnp.sum(own * own + other * other, axis=-1, keepdims=True)
    scale = lax.rsqrt(total / (2 * own.shape[-1]) + EPS)
    return (
        (own * scale * gain_own).astype(jnp.bfloat16),
        (other * scale * gain_other).astype(jnp.bfloat16),
    )


def weight_copies(c, half, sources, targets, sems):
    copies = []
    for i, (source, target) in enumerate(zip(sources, targets)):
        pieces = []
        for part, core in enumerate((c, 1 - c)):
            start = pl.multiple_of(core * half, half)
            pieces.append(
                pltpu.make_async_copy(
                    source.at[pl.ds(start, half), :],
                    target.at[pl.ds(part * half, half), :],
                    sems.at[i, part],
                )
            )
        copies.append(pieces)
    return copies


def question_kernel(own_ref, mine, theirs, gain, wq, wk, wv, out, vq, vk, vv, sems):
    c = own_ref[0, 0]
    half = mine.shape[-1]
    copies = weight_copies(c, half, (wq, wk, wv), (vq, vk, vv), sems)
    for pieces in copies:
        for piece in pieces:
            piece.start()
    g_own = gain[c].astype(jnp.float32)
    g_other = gain[1 - c].astype(jnp.float32)
    first, second = normed_halves(mine[0], theirs[0], g_own, g_other)
    rows = jnp.concatenate([first, second], axis=1)
    for i, weight in enumerate((vq, vk, vv)):
        for piece in copies[i]:
            piece.wait()
        made = jnp.dot(rows, weight[...], preferred_element_type=jnp.float32)
        made = made.astype(jnp.bfloat16)
        if i == 0:
            made = made * jnp.bfloat16(1.0 / 8.0)
        out[i] = made


def project_question(own, mine, theirs, gain, wq, wk, wv):
    _, q_tokens, half = mine.shape
    width, cols = wq.shape
    weight = pltpu.VMEM((width, cols), jnp.bfloat16)
    return pl.pallas_call(
        question_kernel,
        out_shape=jax.ShapeDtypeStruct((3, q_tokens, cols), jnp.bfloat16),
        in_specs=[SMEM, VMEM, VMEM, VMEM, ANY, ANY, ANY],
        out_specs=VMEM,
        scratch_shapes=[weight] * 3 + [pltpu.SemaphoreType.DMA((3, 2))],
        compiler_params=pltpu.CompilerParams(vmem_limit_bytes=VMEM_SMALL),
        cost_estimate=pl.CostEstimate(
            flops=6 * q_tokens * width * cols, bytes_accessed=6 * width * cols, transcendentals=0
        ),
        name="question_projections",
    )(own, mine, theirs, gain, wq, wk, wv)


def compact(table, first, slots, q_tokens):
    places = []
    start = jnp.int32(0)
    start_out = jnp.int32(0)
    for s in range(slots):
        p_len = table[1, first + s]
        room = lax.bitwise_and(p_len + (PACK - 1), ~(PACK - 1))
        places.append((p_len, pl.multiple_of(start, PACK), pl.multiple_of(start_out, PACK)))
        start = start + room
        start_out = start_out + jnp.where(p_len > 0, room + q_tokens, 0)
    return places, start_out


def pick_span(p_len, spans):
    span = jnp.int32(spans[-1])
    for candidate in reversed(spans[:-1]):
        span = jnp.where(p_len <= candidate, candidate, span)
    return span


def for_rows(needed, most, run):
    least = 0
    for count in [c for c in range(256, most, 128)] + [most]:

        @pl.when(jnp.logical_and(needed > least, needed <= count))
        def _():
            run(count)

        least = count


def layer_kernel(ks, own_ref, table, question, gain, *refs):
    n = len(ks)
    mine, theirs = refs[:n], refs[n : 2 * n]
    wq, wk, wv, wo = refs[2 * n : 2 * n + 4]
    out_own, out_other = refs[2 * n + 4 : 2 * n + 6]
    vq, vk, vv, vo, rows, query, key, value, attended, sems, sems_out = refs[2 * n + 6 :]
    cols = query.shape[1]
    q_tokens = question.shape[1]
    _, p_tokens, half = mine[0].shape
    slots = CAPM * n
    total = q_tokens + p_tokens
    spans = (p_tokens // 2, 3 * p_tokens // 4, p_tokens)
    c = own_ref[0, 0]
    q_len = own_ref[0, 2]
    copies = weight_copies(c, half, (wq, wk, wv), (vq, vk, vv), sems)
    out_copies = []
    for part, core in enumerate((1 - c, c)):
        start = pl.multiple_of(core * half, half)
        out_copies.append(
            pltpu.make_async_copy(wo.at[:, pl.ds(start, half)], vo.at[part], sems_out.at[part])
        )
    for pieces in copies + [out_copies]:
        for piece in pieces:
            piece.start()
    places, used_out = compact(table, CAPM * ks[0], slots, q_tokens)
    used = jnp.int32(0)
    for p_len, start, _ in places:
        used = jnp.where(p_len > 0, jnp.maximum(used, start + pick_span(p_len, spans)), used)
    g_own = gain[c].astype(jnp.float32)
    g_other = gain[1 - c].astype(jnp.float32)
    for s, (p_len, start, _) in enumerate(places):

        @pl.when(p_len > 0)
        def _():
            first, second = normed_halves(
                mine[s // CAPM][s % CAPM], theirs[s // CAPM][s % CAPM], g_own, g_other
            )
            rows[pl.ds(start, p_tokens), :half] = first
            rows[pl.ds(start, p_tokens), half:] = second

    for i, (weight, target) in enumerate(((vq, query), (vk, key), (vv, value))):
        for piece in copies[i]:
            piece.wait()

        def project(count):
            for left in range(0, cols, 256):
                span = slice(left, left + 256)
                made = jnp.dot(
                    rows[:count], weight[:, span], preferred_element_type=jnp.float32
                ).astype(jnp.bfloat16)
                if i == 0:
                    made = made * jnp.bfloat16(1.0 / 8.0)
                target[:count, span] = made

        for_rows(used, slots * p_tokens, project)

    lane = lax.broadcasted_iota(jnp.int32, (1, 2 * HS), 1)
    in_first = lane < HS

    def attend(p_len, start, start_out, length):
        both = q_tokens + length
        spot = lax.broadcasted_iota(jnp.int32, (1, both), 1)
        end = jnp.where(spot < q_tokens, q_len, q_tokens + p_len)
        bias = jnp.where(spot < end, 0.0, MASKED)
        ones = jnp.ones((both, 2 * HS), jnp.bfloat16)

        def pair_rows(i, source, span):
            return jnp.concatenate(
                [question[i, :, span], source[pl.ds(start, length), span]], axis=0
            )

        def score(left):
            span = slice(left, left + 2 * HS)
            q2 = pair_rows(0, query, span)
            zero = jnp.zeros_like(q2)
            q2 = jnp.concatenate(
                [jnp.where(in_first, q2, zero), jnp.where(in_first, zero, q2)], axis=0
            )
            return lax.dot_general(
                q2,
                pair_rows(1, key, span),
                (((1,), (1,)), ((), ())),
                preferred_element_type=jnp.float32,
            )

        ahead = score(0)
        for left in range(0, cols, 2 * HS):
            span = slice(left, left + 2 * HS)
            scores = ahead + bias
            if left + 2 * HS < cols:
                ahead = score(left + 2 * HS)
            raised = jnp.exp(scores - jnp.max(scores, axis=1, keepdims=True))
            with_sum = jnp.dot(
                raised.astype(jnp.bfloat16),
                jnp.concatenate([pair_rows(2, value, span), ones], axis=1),
                preferred_element_type=jnp.float32,
            )
            top, bottom = with_sum[:both], with_sum[both:]
            mixed = jnp.where(in_first, top[:, : 2 * HS], bottom[:, : 2 * HS])
            weight_sum = jnp.where(in_first, top[:, 2 * HS :], bottom[:, 2 * HS :])
            attended[pl.ds(start_out, both), span] = (mixed / weight_sum).astype(jnp.bfloat16)

    for s, (p_len, start, start_out) in enumerate(places):
        least = 0
        for length in spans:

            @pl.when(jnp.logical_and(p_len > least, p_len <= length))
            def _():
                attend(p_len, start, start_out, length)

            least = length

    for part, out in enumerate((out_other, out_own)):
        out_copies[part].wait()

        def put_out(count):
            for left in range(0, half, 256):
                span = slice(left, left + 256)
                out[:count, span] = jnp.dot(
                    attended[:count], vo[part, :, span], preferred_element_type=jnp.float32
                ).astype(jnp.bfloat16)

        for_rows(used_out, slots * total, put_out)


def layer(ks, own, table, question, gain, mine, theirs, wq, wk, wv, wo):
    _, p_tokens, half = mine[0].shape
    _, q_tokens, cols = question.shape
    width = wq.shape[0]
    slots = CAPM * len(ks)
    total = q_tokens + p_tokens
    weight = pltpu.VMEM((width, cols), jnp.bfloat16)
    packed = pltpu.VMEM((slots * p_tokens, cols), jnp.bfloat16)
    out = jax.ShapeDtypeStruct((slots * total, half), jnp.bfloat16)
    return pl.pallas_call(
        functools.partial(layer_kernel, ks),
        out_shape=[out, out],
        in_specs=[SMEM, SMEM, VMEM, VMEM] + [VMEM] * (2 * len(ks)) + [ANY] * 4,
        out_specs=[VMEM, VMEM],
        scratch_shapes=[weight] * 3
        + [
            pltpu.VMEM((2, cols, half), jnp.bfloat16),
            pltpu.VMEM((slots * p_tokens, width), jnp.bfloat16),
            packed,
            packed,
            packed,
            pltpu.VMEM((slots * total, cols), jnp.bfloat16),
            pltpu.SemaphoreType.DMA((3, 2)),
            pltpu.SemaphoreType.DMA((2,)),
        ],
        compiler_params=pltpu.CompilerParams(vmem_limit_bytes=VMEM_LARGE),
        cost_estimate=pl.CostEstimate(
            flops=slots * (6 * p_tokens * width * cols + 4 * total * cols * half),
            bytes_accessed=8 * width * cols,
            transcendentals=slots * total * total * cols // HS,
        ),
        name="layer",
    )(own, table, question, gain, *mine, *theirs, wq, wk, wv, wo)


def combine_kernel(ks, first, own_ref, table, questions, *refs):
    n = len(ks)
    mine = refs[:n]
    ours, arrived = refs[n : n + 2]
    encoded, staged, sems = refs[n + 2 if first else n + 3 :]
    slots, total, _ = staged.shape
    q_tokens = questions.shape[1]
    q_len = own_ref[0, 2]
    places, _ = compact(table, CAPM * ks[0], slots, q_tokens)

    def copy(s, pair):
        return pltpu.make_async_copy(staged.at[s], encoded.at[0, pair], sems.at[s])

    for s, (p_len, _, start) in enumerate(places):
        pair = table[0, CAPM * ks[0] + s]

        @pl.when(pair >= 0)
        def _():
            for rows, low, length in (
                (questions[0], 0, q_len),
                (mine[s // CAPM][s % CAPM], q_tokens, p_len),
            ):
                count = rows.shape[0]
                spot = lax.broadcasted_iota(jnp.int32, (count, 1), 0)
                at = pl.ds(pl.multiple_of(start + low, PACK), count)
                branch = ours[at].astype(jnp.float32) + arrived[at].astype(jnp.float32)
                made = rows.astype(jnp.float32) + branch
                staged[s, low : low + count] = jnp.where(spot < length, made, 0.0).astype(
                    jnp.bfloat16
                )
            copy(s, pair).start()

    for s in range(slots):

        @pl.when(table[0, CAPM * ks[0] + s] >= 0)
        def _():
            copy(s, 0).wait()


def combine(ks, encoded, shape, own, table, questions, mine, ours, arrived):
    first = encoded is None
    slots = CAPM * len(ks)
    operands = [own, table, questions, *mine, ours, arrived] + ([] if first else [encoded])
    return pl.pallas_call(
        functools.partial(combine_kernel, ks, first),
        out_shape=jax.ShapeDtypeStruct(shape, jnp.bfloat16),
        in_specs=[SMEM, SMEM, VMEM] + [VMEM] * (len(ks) + 2) + ([] if first else [ANY]),
        out_specs=ANY,
        scratch_shapes=[
            pltpu.VMEM((slots, *shape[2:]), jnp.bfloat16),
            pltpu.SemaphoreType.DMA((slots,)),
        ],
        input_output_aliases={} if first else {len(operands) - 1: 0},
        compiler_params=pltpu.CompilerParams(vmem_limit_bytes=VMEM_SMALL),
        cost_estimate=pl.CostEstimate(
            flops=0, bytes_accessed=8 * ours.size, transcendentals=0
        ),
        name="combine",
    )(*operands)


def body(questions, memory, retrieved, q_len, p_len, norm_gain, w_query, w_key, w_value, w_out):
    shards = lax.axis_size("mem")
    cores = lax.axis_size("tp")
    _, q_tokens, half = questions.shape
    pass_dev, p_tokens, _ = memory.shape
    wants = retrieved.shape[1]

    def swap(x):
        return lax.ppermute(x, "tp", [(i, (i + 1) % cores) for i in range(cores)])

    def exchange(x, k):
        return lax.ppermute(x, "mem", [(i, i ^ k) for i in range(shards)])

    meta = jnp.concatenate(
        [retrieved[0], p_len, jnp.zeros((LANES - wants - pass_dev,), jnp.int32)]
    )[None]
    metas = lax.all_to_all(
        jnp.broadcast_to(meta[None], (shards, 1, LANES)), "mem", 0, 0, tiled=True
    )
    own = jnp.concatenate(
        [
            lax.axis_index("tp").astype(jnp.int32)[None],
            lax.axis_index("mem").astype(jnp.int32)[None],
            q_len,
            jnp.zeros((LANES - 3,), jnp.int32),
        ]
    )[None]
    gain = norm_gain.reshape(cores, 1, half)
    question = project_question(
        own, questions, swap(questions), gain, w_query, w_key, w_value
    )
    sends, table = pick(own, metas, memory, wants)
    mine = [sends[0]] + [exchange(sends[k], k) for k in range(1, shards)]
    encoded = None
    shape = (1, wants, q_tokens + p_tokens, half)
    waiting = None
    for low in range(0, shards, 2):
        ks = tuple(range(low, low + 2))
        rows = [mine[k] for k in ks]
        if waiting is not None:
            *rows, ours, other = lax.optimization_barrier((*rows, *waiting[3:]))
        theirs = [swap(x) for x in rows]
        if waiting is not None:
            encoded = combine(waiting[0], encoded, shape, own, table, questions, waiting[1], ours, swap(other))
            theirs[0], encoded = lax.optimization_barrier((theirs[0], encoded))
        made = layer(
            ks, own, table, question, gain, rows, theirs, w_query, w_key, w_value, w_out
        )
        waiting = (ks, rows, None, *made)
    ks, rows, _, ours, other = waiting
    encoded = combine(ks, encoded, shape, own, table, questions, rows, ours, swap(other))
    return encoded


def solution(mesh):
    in_specs = (
        P(("groups", "mem"), None, "tp"),
        P("mem", None, "tp"),
        P(("groups", "mem"), None),
        P(("groups", "mem")),
        P("mem"),
        P(),
        P(None, "tp"),
        P(None, "tp"),
        P(None, "tp"),
        P("tp", None),
    )
    out_specs = P(("groups", "mem"), None, None, "tp")
    return jax.shard_map(body, mesh=mesh, in_specs=in_specs, out_specs=out_specs, check_vma=False)
```

```python
import functools

import jax
import jax.numpy as jnp
from jax import lax
from jax.experimental import pallas as pl
from jax.experimental.pallas import tpu as pltpu
from jax.sharding import PartitionSpec as P

HS = 64
CAPM = 2
EPS = 1e-06
MASKED = -1e30
LANES = 128
PACK = 16
VMEM_ALL = 60 * 1024 * 1024
VMEM_LAYER = 44 * 1024 * 1024

ANY = pl.BlockSpec(memory_space=pl.ANY)
HBM = pl.BlockSpec(memory_space=pltpu.HBM)
SMEM = pl.BlockSpec(memory_space=pltpu.SMEM)
VMEM = pl.BlockSpec(memory_space=pltpu.VMEM)
LITTLE = pl.CostEstimate(flops=1, bytes_accessed=1, transcendentals=0)


def pick_kernel(shards, pass_dev, wants, own_ref, metas, memory, *refs):
    outs = refs[:shards]
    table, sems = refs[shards:]
    me = own_ref[0, 1]
    low = me * pass_dev
    counts = []
    for k in range(shards):
        partner = lax.bitwise_xor(me, k)

        def ask(j, count):
            local = metas[partner, 0, j] - low
            mine = jnp.logical_and(local >= 0, local < pass_dev)

            @pl.when(mine)
            def _():
                pltpu.make_async_copy(
                    memory.at[local], outs[k].at[count], sems.at[k, count]
                ).start()

            return count + mine.astype(jnp.int32)

        counts.append(lax.fori_loop(0, wants, ask, jnp.int32(0)))
    for k in range(shards):
        partner = lax.bitwise_xor(me, k)
        for r in range(CAPM):
            table[0, CAPM * k + r] = jnp.int32(-1)
            table[1, CAPM * k + r] = jnp.int32(0)

        def place(j, count):
            local = metas[me, 0, j] - partner * pass_dev
            theirs = jnp.logical_and(local >= 0, local < pass_dev)

            @pl.when(theirs)
            def _():
                table[0, CAPM * k + count] = j
                table[1, CAPM * k + count] = metas[partner, 0, wants + local]

            return count + theirs.astype(jnp.int32)

        lax.fori_loop(0, wants, place, jnp.int32(0))
    for k in range(shards):
        for r in range(CAPM):

            @pl.when(r < counts[k])
            def _():
                pltpu.make_async_copy(memory.at[0], outs[k].at[r], sems.at[k, r]).wait()


def pick(own, metas, memory, wants):
    shards = metas.shape[0]
    pass_dev, p_tokens, half = memory.shape
    slot = jax.ShapeDtypeStruct((CAPM, p_tokens, half), memory.dtype)
    result = pl.pallas_call(
        functools.partial(pick_kernel, shards, pass_dev, wants),
        out_shape=[slot] * shards + [jax.ShapeDtypeStruct((2, LANES), jnp.int32)],
        in_specs=[SMEM, SMEM, HBM],
        out_specs=[VMEM] * shards + [SMEM],
        scratch_shapes=[pltpu.SemaphoreType.DMA((shards, CAPM))],
        compiler_params=pltpu.CompilerParams(vmem_limit_bytes=VMEM_ALL),
        cost_estimate=LITTLE,
        name="pick",
    )(own, metas, memory)
    return result[:shards], result[shards]


def normed_halves(own, other, gain_own, gain_other):
    own = own.astype(jnp.float32)
    other = other.astype(jnp.float32)
    total = jnp.sum(own * own + other * other, axis=-1, keepdims=True)
    scale = lax.rsqrt(total / (2 * own.shape[-1]) + EPS)
    return (
        (own * scale * gain_own).astype(jnp.bfloat16),
        (other * scale * gain_other).astype(jnp.bfloat16),
    )


def weight_copies(c, half, sources, targets, sems):
    copies = []
    for i, (source, target) in enumerate(zip(sources, targets)):
        pieces = []
        for part, core in enumerate((c, 1 - c)):
            start = pl.multiple_of(core * half, half)
            pieces.append(
                pltpu.make_async_copy(
                    source.at[pl.ds(start, half), :],
                    target.at[pl.ds(part * half, half), :],
                    sems.at[i, part],
                )
            )
        copies.append(pieces)
    return copies


def question_kernel(own_ref, mine, theirs, gain, wq, wk, wv, out, vq, vk, vv, sems):
    c = own_ref[0, 0]
    half = mine.shape[-1]
    copies = weight_copies(c, half, (wq, wk, wv), (vq, vk, vv), sems)
    for pieces in copies:
        for piece in pieces:
            piece.start()
    g_own = gain[c].astype(jnp.float32)
    g_other = gain[1 - c].astype(jnp.float32)
    first, second = normed_halves(mine[0], theirs[0], g_own, g_other)
    rows = jnp.concatenate([first, second], axis=1)
    for i, weight in enumerate((vq, vk, vv)):
        for piece in copies[i]:
            piece.wait()
        made = jnp.dot(rows, weight[...], preferred_element_type=jnp.float32)
        made = made.astype(jnp.bfloat16)
        if i == 0:
            made = made * jnp.bfloat16(1.0 / 8.0)
        out[i] = made


def project_question(own, mine, theirs, gain, wq, wk, wv):
    _, q_tokens, half = mine.shape
    width, cols = wq.shape
    weight = pltpu.VMEM((width, cols), jnp.bfloat16)
    return pl.pallas_call(
        question_kernel,
        out_shape=jax.ShapeDtypeStruct((3, q_tokens, cols), jnp.bfloat16),
        in_specs=[SMEM, VMEM, VMEM, VMEM, HBM, HBM, HBM],
        out_specs=VMEM,
        scratch_shapes=[weight] * 3 + [pltpu.SemaphoreType.DMA((3, 2))],
        compiler_params=pltpu.CompilerParams(vmem_limit_bytes=VMEM_ALL),
        cost_estimate=LITTLE,
        name="question_projections",
    )(own, mine, theirs, gain, wq, wk, wv)


def place_of(ks, s):
    return CAPM * ks[s // CAPM] + s % CAPM


def compact(table, ks, q_tokens):
    places = []
    start = jnp.int32(0)
    start_out = jnp.int32(0)
    for s in range(CAPM * len(ks)):
        p_len = table[1, place_of(ks, s)]
        room = lax.bitwise_and(p_len + (PACK - 1), ~(PACK - 1))
        places.append((p_len, pl.multiple_of(start, PACK), pl.multiple_of(start_out, PACK)))
        start = start + room
        start_out = start_out + jnp.where(p_len > 0, room + q_tokens, 0)
    return places, start_out


def pick_span(p_len, spans):
    span = jnp.int32(spans[-1])
    for candidate in reversed(spans[:-1]):
        span = jnp.where(p_len <= candidate, candidate, span)
    return span


def for_rows(needed, most, run):
    least = 0
    for count in [c for c in range(256, most, 128)] + [most]:

        @pl.when(jnp.logical_and(needed > least, needed <= count))
        def _():
            run(count)

        least = count


def layer_kernel(ks, own_ref, table, question, gain, *refs):
    n = len(ks)
    mine, theirs = refs[:n], refs[n : 2 * n]
    wq, wk, wv, wo = refs[2 * n : 2 * n + 4]
    out_own, out_other = refs[2 * n + 4 : 2 * n + 6]
    vq, vk, vv, vo, rows, query, key, value, attended, sems, sems_out = refs[2 * n + 6 :]
    cols = query.shape[1]
    q_tokens = question.shape[1]
    _, p_tokens, half = mine[0].shape
    slots = CAPM * n
    total = q_tokens + p_tokens
    spans = (p_tokens // 2, 3 * p_tokens // 4, p_tokens)
    c = own_ref[0, 0]
    q_len = own_ref[0, 2]
    copies = weight_copies(c, half, (wq, wk, wv), (vq, vk, vv), sems)
    out_copies = []
    for part, core in enumerate((1 - c, c)):
        start = pl.multiple_of(core * half, half)
        out_copies.append(
            pltpu.make_async_copy(wo.at[:, pl.ds(start, half)], vo.at[part], sems_out.at[part])
        )
    for pieces in copies + [out_copies]:
        for piece in pieces:
            piece.start()
    places, used_out = compact(table, ks, q_tokens)
    used = jnp.int32(0)
    for p_len, start, _ in places:
        used = jnp.where(p_len > 0, jnp.maximum(used, start + pick_span(p_len, spans)), used)
    g_own = gain[c].astype(jnp.float32)
    g_other = gain[1 - c].astype(jnp.float32)
    for s, (p_len, start, _) in enumerate(places):

        @pl.when(p_len > 0)
        def _():
            first, second = normed_halves(
                mine[s // CAPM][s % CAPM], theirs[s // CAPM][s % CAPM], g_own, g_other
            )
            rows[pl.ds(start, p_tokens), :half] = first
            rows[pl.ds(start, p_tokens), half:] = second

    for i, (weight, target) in enumerate(((vq, query), (vk, key), (vv, value))):
        for piece in copies[i]:
            piece.wait()

        def project(count):
            for left in range(0, cols, 256):
                span = slice(left, left + 256)
                made = jnp.dot(
                    rows[:count], weight[:, span], preferred_element_type=jnp.float32
                ).astype(jnp.bfloat16)
                if i == 0:
                    made = made * jnp.bfloat16(1.0 / 8.0)
                target[:count, span] = made

        for_rows(used, slots * p_tokens, project)

    lane = lax.broadcasted_iota(jnp.int32, (1, 2 * HS), 1)
    in_first = lane < HS

    def attend(p_len, start, start_out, length):
        both = q_tokens + length
        spot = lax.broadcasted_iota(jnp.int32, (1, both), 1)
        end = jnp.where(spot < q_tokens, q_len, q_tokens + p_len)
        bias = jnp.where(spot < end, 0.0, MASKED)
        ones = jnp.ones((both, 2 * HS), jnp.bfloat16)

        def pair_rows(i, source, span):
            return jnp.concatenate(
                [question[i, :, span], source[pl.ds(start, length), span]], axis=0
            )

        def score(left):
            span = slice(left, left + 2 * HS)
            q2 = pair_rows(0, query, span)
            zero = jnp.zeros_like(q2)
            q2 = jnp.concatenate(
                [jnp.where(in_first, q2, zero), jnp.where(in_first, zero, q2)], axis=0
            )
            return lax.dot_general(
                q2,
                pair_rows(1, key, span),
                (((1,), (1,)), ((), ())),
                preferred_element_type=jnp.float32,
            )

        lefts = range(0, cols, 2 * HS)
        scores = [score(left) + bias for left in lefts]
        largest = [jnp.max(x, axis=1, keepdims=True) for x in scores]
        raised = [jnp.exp(x - m).astype(jnp.bfloat16) for x, m in zip(scores, largest)]
        with_sums = [
            jnp.dot(
                x,
                jnp.concatenate([pair_rows(2, value, slice(left, left + 2 * HS)), ones], axis=1),
                preferred_element_type=jnp.float32,
            )
            for x, left in zip(raised, lefts)
        ]
        for with_sum, left in zip(with_sums, lefts):
            top, bottom = with_sum[:both], with_sum[both:]
            mixed = jnp.where(in_first, top[:, : 2 * HS], bottom[:, : 2 * HS])
            weight_sum = jnp.where(in_first, top[:, 2 * HS :], bottom[:, 2 * HS :])
            attended[pl.ds(start_out, both), left : left + 2 * HS] = (
                mixed / weight_sum
            ).astype(jnp.bfloat16)

    for s, (p_len, start, start_out) in enumerate(places):
        least = 0
        for length in spans:

            @pl.when(jnp.logical_and(p_len > least, p_len <= length))
            def _():
                attend(p_len, start, start_out, length)

            least = length

    for part, out in enumerate((out_other, out_own)):
        out_copies[part].wait()

        def put_out(count):
            for left in range(0, half, 256):
                span = slice(left, left + 256)
                out[:count, span] = jnp.dot(
                    attended[:count], vo[part, :, span], preferred_element_type=jnp.float32
                ).astype(jnp.bfloat16)

        for_rows(used_out, slots * total, put_out)


def layer(ks, own, table, question, gain, mine, theirs, wq, wk, wv, wo):
    _, p_tokens, half = mine[0].shape
    _, q_tokens, cols = question.shape
    width = wq.shape[0]
    slots = CAPM * len(ks)
    total = q_tokens + p_tokens
    weight = pltpu.VMEM((width, cols), jnp.bfloat16)
    packed = pltpu.VMEM((slots * p_tokens, cols), jnp.bfloat16)
    out = jax.ShapeDtypeStruct((slots * total, half), jnp.bfloat16)
    return pl.pallas_call(
        functools.partial(layer_kernel, ks),
        out_shape=[out, out],
        in_specs=[SMEM, SMEM, VMEM, VMEM] + [VMEM] * (2 * len(ks)) + [HBM] * 4,
        out_specs=[VMEM, VMEM],
        scratch_shapes=[weight] * 3
        + [
            pltpu.VMEM((2, cols, half), jnp.bfloat16),
            pltpu.VMEM((slots * p_tokens, width), jnp.bfloat16),
            packed,
            packed,
            packed,
            pltpu.VMEM((slots * total, cols), jnp.bfloat16),
            pltpu.SemaphoreType.DMA((3, 2)),
            pltpu.SemaphoreType.DMA((2,)),
        ],
        compiler_params=pltpu.CompilerParams(vmem_limit_bytes=VMEM_LAYER),
        cost_estimate=LITTLE,
        name="layer",
    )(own, table, question, gain, *mine, *theirs, wq, wk, wv, wo)


def combine_kernel(ks, first, own_ref, table, questions, *refs):
    n = len(ks)
    mine = refs[:n]
    ours, arrived = refs[n : n + 2]
    encoded, staged, sems = refs[n + 2 if first else n + 3 :]
    slots, total, _ = staged.shape
    q_tokens = questions.shape[1]
    q_len = own_ref[0, 2]
    places, _ = compact(table, ks, q_tokens)

    def copy(s, pair):
        return pltpu.make_async_copy(staged.at[s], encoded.at[0, pair], sems.at[s])

    for s, (p_len, _, start) in enumerate(places):
        pair = table[0, place_of(ks, s)]

        @pl.when(pair >= 0)
        def _():
            for rows, low, length in (
                (questions[0], 0, q_len),
                (mine[s // CAPM][s % CAPM], q_tokens, p_len),
            ):
                count = rows.shape[0]
                spot = lax.broadcasted_iota(jnp.int32, (count, 1), 0)
                at = pl.ds(pl.multiple_of(start + low, PACK), count)
                branch = ours[at].astype(jnp.float32) + arrived[at].astype(jnp.float32)
                made = rows.astype(jnp.float32) + branch
                staged[s, low : low + count] = jnp.where(spot < length, made, 0.0).astype(
                    jnp.bfloat16
                )
            copy(s, pair).start()

    for s in range(slots):

        @pl.when(table[0, place_of(ks, s)] >= 0)
        def _():
            copy(s, 0).wait()


def combine(ks, encoded, shape, own, table, questions, mine, ours, arrived):
    first = encoded is None
    slots = CAPM * len(ks)
    operands = [own, table, questions, *mine, ours, arrived] + ([] if first else [encoded])
    return pl.pallas_call(
        functools.partial(combine_kernel, ks, first),
        out_shape=jax.ShapeDtypeStruct(shape, jnp.bfloat16),
        in_specs=[SMEM, SMEM, VMEM] + [VMEM] * (len(ks) + 2) + ([] if first else [ANY]),
        out_specs=ANY,
        scratch_shapes=[
            pltpu.VMEM((slots, *shape[2:]), jnp.bfloat16),
            pltpu.SemaphoreType.DMA((slots,)),
        ],
        input_output_aliases={} if first else {len(operands) - 1: 0},
        compiler_params=pltpu.CompilerParams(vmem_limit_bytes=VMEM_LAYER),
        cost_estimate=LITTLE,
        name="combine",
    )(*operands)


def body(questions, memory, retrieved, q_len, p_len, norm_gain, w_query, w_key, w_value, w_out):
    shards = lax.axis_size("mem")
    cores = lax.axis_size("tp")
    _, q_tokens, half = questions.shape
    pass_dev, p_tokens, _ = memory.shape
    wants = retrieved.shape[1]

    def swap(x):
        return lax.ppermute(x, "tp", [(i, (i + 1) % cores) for i in range(cores)])

    def exchange(x, k):
        return lax.ppermute(x, "mem", [(i, i ^ k) for i in range(shards)])

    meta = jnp.concatenate(
        [retrieved[0], p_len, jnp.zeros((LANES - wants - pass_dev,), jnp.int32)]
    )[None]
    metas = lax.all_to_all(
        jnp.broadcast_to(meta[None], (shards, 1, LANES)), "mem", 0, 0, tiled=True
    )
    own = jnp.concatenate(
        [
            lax.axis_index("tp").astype(jnp.int32)[None],
            lax.axis_index("mem").astype(jnp.int32)[None],
            q_len,
            jnp.zeros((LANES - 3,), jnp.int32),
        ]
    )[None]
    gain = norm_gain.reshape(cores, 1, half)
    question = project_question(
        own, questions, swap(questions), gain, w_query, w_key, w_value
    )
    sends, table = pick(own, metas, memory, wants)
    mine = [sends[0]] + [exchange(sends[k], k) for k in range(1, shards)]
    encoded = None
    shape = (1, wants, q_tokens + p_tokens, half)
    waiting = None
    near = shards // 2
    chunks = [(0,)] + [(k, near - 1 + k) for k in range(1, near)] + [(shards - 1,)]
    for ks in chunks:
        rows = [mine[k] for k in ks]
        if waiting is not None:
            *rows, ours, other = lax.optimization_barrier((*rows, *waiting[3:]))
        theirs = [swap(x) for x in rows]
        if waiting is not None:
            encoded = combine(waiting[0], encoded, shape, own, table, questions, waiting[1], ours, swap(other))
            theirs[0], encoded = lax.optimization_barrier((theirs[0], encoded))
        made = layer(
            ks, own, table, question, gain, rows, theirs, w_query, w_key, w_value, w_out
        )
        waiting = (ks, rows, None, *made)
    ks, rows, _, ours, other = waiting
    encoded = combine(ks, encoded, shape, own, table, questions, rows, ours, swap(other))
    return encoded


def solution(mesh):
    in_specs = (
        P(("groups", "mem"), None, "tp"),
        P("mem", None, "tp"),
        P(("groups", "mem"), None),
        P(("groups", "mem")),
        P("mem"),
        P(),
        P(None, "tp"),
        P(None, "tp"),
        P(None, "tp"),
        P("tp", None),
    )
    out_specs = P(("groups", "mem"), None, None, "tp")
    return jax.shard_map(body, mesh=mesh, in_specs=in_specs, out_specs=out_specs, check_vma=False)
```

```python
import functools

import jax
import jax.numpy as jnp
from jax import lax
from jax.experimental import pallas as pl
from jax.experimental.pallas import tpu as pltpu
from jax.sharding import PartitionSpec as P

HS = 64
CAPM = 2
EPS = 1e-06
MASKED = -1e30
LANES = 128
PACK = 16
TILE = 256
MOST = 5
VMEM_ALL = 60 * 1024 * 1024
VMEM_LAYER = 54 * 1024 * 1024

ANY = pl.BlockSpec(memory_space=pl.ANY)
HBM = pl.BlockSpec(memory_space=pltpu.HBM)
SMEM = pl.BlockSpec(memory_space=pltpu.SMEM)
VMEM = pl.BlockSpec(memory_space=pltpu.VMEM)
LITTLE = pl.CostEstimate(flops=1, bytes_accessed=1, transcendentals=0)


def pick_kernel(ks, pass_dev, wants, own_ref, metas, memory, *refs):
    n = len(ks)
    outs = refs[:n]
    table = refs[n] if len(refs) > n + 1 else None
    sems = refs[-1]
    shards = metas.shape[0]
    me = own_ref[0, 1]
    low = me * pass_dev
    counts = []
    for i, k in enumerate(ks):
        partner = lax.bitwise_xor(me, k)

        def ask(j, count):
            local = metas[partner, 0, j] - low
            mine = jnp.logical_and(local >= 0, local < pass_dev)

            @pl.when(mine)
            def _():
                pltpu.make_async_copy(
                    memory.at[local], outs[i].at[count], sems.at[i, count]
                ).start()

            return count + mine.astype(jnp.int32)

        counts.append(lax.fori_loop(0, wants, ask, jnp.int32(0)))
    if table is not None:

        def list_partner(k, carry):
            partner = lax.bitwise_xor(me, k)
            for r in range(CAPM):
                table[0, CAPM * k + r] = jnp.int32(-1)
                table[1, CAPM * k + r] = jnp.int32(0)

            def place(j, count):
                local = metas[me, 0, j] - partner * pass_dev
                theirs = jnp.logical_and(local >= 0, local < pass_dev)

                @pl.when(theirs)
                def _():
                    table[0, CAPM * k + count] = j
                    table[1, CAPM * k + count] = metas[partner, 0, wants + local]

                return count + theirs.astype(jnp.int32)

            lax.fori_loop(0, wants, place, jnp.int32(0))
            return carry

        lax.fori_loop(0, shards, list_partner, 0)
    for i in range(n):
        for r in range(CAPM):

            @pl.when(r < counts[i])
            def _():
                pltpu.make_async_copy(memory.at[0], outs[i].at[r], sems.at[i, r]).wait()


def pick(ks, with_table, own, metas, memory, wants):
    n = len(ks)
    pass_dev, p_tokens, half = memory.shape
    slot = jax.ShapeDtypeStruct((CAPM, p_tokens, half), memory.dtype)
    tables = [jax.ShapeDtypeStruct((2, LANES), jnp.int32)] * with_table
    result = pl.pallas_call(
        functools.partial(pick_kernel, ks, pass_dev, wants),
        out_shape=[slot] * n + tables,
        in_specs=[SMEM, SMEM, HBM],
        out_specs=[VMEM] * n + [SMEM] * with_table,
        scratch_shapes=[pltpu.SemaphoreType.DMA((n, CAPM))],
        compiler_params=pltpu.CompilerParams(vmem_limit_bytes=VMEM_ALL),
        cost_estimate=LITTLE,
        name="pick",
    )(own, metas, memory)
    return dict(zip(ks, result)), result[n:]


def normed_halves(own, other, gain_own, gain_other):
    own = own.astype(jnp.float32)
    other = other.astype(jnp.float32)
    total = jnp.sum(own * own + other * other, axis=-1, keepdims=True)
    scale = lax.rsqrt(total / (2 * own.shape[-1]) + EPS)
    return (
        (own * scale * gain_own).astype(jnp.bfloat16),
        (other * scale * gain_other).astype(jnp.bfloat16),
    )


def weight_copies(c, half, sources, target, sems):
    copies = []
    for i, source in enumerate(sources):
        for part, core in enumerate((c, 1 - c)):
            start = pl.multiple_of(core * half, half)
            copies.append(
                pltpu.make_async_copy(
                    source.at[pl.ds(start, half), :],
                    target.at[i, pl.ds(part * half, half), :],
                    sems.at[i, part],
                )
            )
    return copies


def project_rows(rows, weights, sems, out, counts, needed):
    _, width, cols = weights.shape
    half = width // 2
    tiles = cols // TILE

    def step(t, carry):
        i = lax.div(t, tiles)
        tile = lax.rem(t, tiles)

        @pl.when(tile == 0)
        def _():
            for part in range(2):
                at = pl.ds(part * half, half)
                pltpu.make_async_copy(
                    weights.at[i, at, :], weights.at[i, at, :], sems.at[i, part]
                ).wait()

        span = pl.ds(pl.multiple_of(tile * TILE, TILE), TILE)
        scale = jnp.where(i == 0, 1.0 / 8.0, 1.0)

        def run(count):
            made = jnp.dot(
                rows[0, :count], weights[i, :half, span], preferred_element_type=jnp.float32
            ) + jnp.dot(
                rows[1, :count], weights[i, half:, span], preferred_element_type=jnp.float32
            )
            out[i, :count, span] = (made * scale).astype(jnp.bfloat16)

        for_rows(needed, counts, run)
        return carry

    lax.fori_loop(0, 3 * tiles, step, 0)


def for_rows(needed, counts, run):
    if needed is None:
        run(counts[0])
        return
    least = 0
    for count in counts:

        @pl.when(jnp.logical_and(needed > least, needed <= count))
        def _():
            run(count)

        least = count


def row_counts(most):
    return list(range(256, min(most, 512), 64)) + list(range(512, most, 128)) + [most]


def question_kernel(own_ref, mine, theirs, gain, wq, wk, wv, out, weights, rows, sems):
    c = own_ref[0, 0]
    _, q_tokens, half = mine.shape
    for copy in weight_copies(c, half, (wq, wk, wv), weights, sems):
        copy.start()
    g_own = gain[c].astype(jnp.float32)
    g_other = gain[1 - c].astype(jnp.float32)
    rows[0], rows[1] = normed_halves(mine[0], theirs[0], g_own, g_other)
    project_rows(rows, weights, sems, out, [q_tokens], None)


def project_question(own, mine, theirs, gain, wq, wk, wv):
    _, q_tokens, half = mine.shape
    width, cols = wq.shape
    return pl.pallas_call(
        question_kernel,
        out_shape=jax.ShapeDtypeStruct((3, q_tokens, cols), jnp.bfloat16),
        in_specs=[SMEM, VMEM, VMEM, VMEM, HBM, HBM, HBM],
        out_specs=VMEM,
        scratch_shapes=[
            pltpu.VMEM((3, width, cols), jnp.bfloat16),
            pltpu.VMEM((2, q_tokens, half), jnp.bfloat16),
            pltpu.SemaphoreType.DMA((3, 2)),
        ],
        compiler_params=pltpu.CompilerParams(vmem_limit_bytes=VMEM_ALL),
        cost_estimate=LITTLE,
        name="question_projections",
    )(own, mine, theirs, gain, wq, wk, wv)


def place_of(ks, s):
    return CAPM * ks[s // CAPM] + s % CAPM


def compact(table, ks, q_tokens):
    places = []
    start = jnp.int32(0)
    start_out = jnp.int32(0)
    for s in range(CAPM * len(ks)):
        p_len = table[1, place_of(ks, s)]
        room = lax.bitwise_and(p_len + (PACK - 1), ~(PACK - 1))
        places.append((p_len, pl.multiple_of(start, PACK), pl.multiple_of(start_out, PACK)))
        start = start + room
        start_out = start_out + jnp.where(p_len > 0, room + q_tokens, 0)
    return places, start_out


def pick_span(p_len, spans):
    span = jnp.int32(spans[-1])
    for candidate in reversed(spans[:-1]):
        span = jnp.where(p_len <= candidate, candidate, span)
    return span


def layer_kernel(ks, own_ref, table, question, gain, *refs):
    n = len(ks)
    mine, theirs = refs[:n], refs[n : 2 * n]
    wq, wk, wv, wo = refs[2 * n : 2 * n + 4]
    out_own, out_other = refs[2 * n + 4 : 2 * n + 6]
    weights, vo, rows, packed, listed, sems, sems_out = refs[2 * n + 6 :]
    attended = rows.at[0]
    cols = packed.shape[2]
    q_tokens = question.shape[1]
    _, p_tokens, half = mine[0].shape
    slots = CAPM * n
    total = q_tokens + p_tokens
    spans = (p_tokens // 2, 3 * p_tokens // 4, p_tokens)
    c = own_ref[0, 0]
    q_len = own_ref[0, 2]
    out_copies = []
    for part, core in enumerate((1 - c, c)):
        start = pl.multiple_of(core * half, half)
        out_copies.append(
            pltpu.make_async_copy(wo.at[:, pl.ds(start, half)], vo.at[part], sems_out.at[part])
        )
    for copy in weight_copies(c, half, (wq, wk, wv), weights, sems) + out_copies:
        copy.start()
    places, used_out = compact(table, ks, q_tokens)
    used = jnp.int32(0)
    g_own = gain[c].astype(jnp.float32)
    g_other = gain[1 - c].astype(jnp.float32)
    for s, (p_len, start, start_out) in enumerate(places):
        used = jnp.where(p_len > 0, jnp.maximum(used, start + pick_span(p_len, spans)), used)
        listed[0, s] = p_len
        listed[1, s] = start
        listed[2, s] = start_out

        @pl.when(p_len > 0)
        def _():
            at = pl.ds(start, p_tokens)
            rows[0, at], rows[1, at] = normed_halves(
                mine[s // CAPM][s % CAPM], theirs[s // CAPM][s % CAPM], g_own, g_other
            )

    project_rows(rows, weights, sems, packed, row_counts(slots * p_tokens), used)

    lane = lax.broadcasted_iota(jnp.int32, (1, 2 * HS), 1)
    in_first = lane < HS

    def attend(p_len, start, start_out, length):
        both = q_tokens + length
        spot = lax.broadcasted_iota(jnp.int32, (1, both), 1)
        end = jnp.where(spot < q_tokens, q_len, q_tokens + p_len)
        bias = jnp.where(spot < end, 0.0, MASKED)
        ones = jnp.ones((both, 2 * HS), jnp.bfloat16)

        def pair_rows(i, span):
            return jnp.concatenate(
                [question[i, :, span], packed[i, pl.ds(start, length), span]], axis=0
            )

        def score(span):
            q2 = pair_rows(0, span)
            zero = jnp.zeros_like(q2)
            q2 = jnp.concatenate(
                [jnp.where(in_first, q2, zero), jnp.where(in_first, zero, q2)], axis=0
            )
            return lax.dot_general(
                q2,
                pair_rows(1, span),
                (((1,), (1,)), ((), ())),
                preferred_element_type=jnp.float32,
            )

        spans_here = [slice(left, left + 2 * HS) for left in range(0, cols, 2 * HS)]
        scores = [score(span) + bias for span in spans_here]
        largest = [jnp.max(x, axis=1, keepdims=True) for x in scores]
        raised = [jnp.exp(x - m).astype(jnp.bfloat16) for x, m in zip(scores, largest)]
        with_sums = [
            jnp.dot(
                x,
                jnp.concatenate([pair_rows(2, span), ones], axis=1),
                preferred_element_type=jnp.float32,
            )
            for x, span in zip(raised, spans_here)
        ]
        for with_sum, span in zip(with_sums, spans_here):
            top, bottom = with_sum[:both], with_sum[both:]
            mixed = jnp.where(in_first, top[:, : 2 * HS], bottom[:, : 2 * HS])
            weight_sum = jnp.where(in_first, top[:, 2 * HS :], bottom[:, 2 * HS :])
            attended[pl.ds(start_out, both), span] = (mixed / weight_sum).astype(jnp.bfloat16)

    def attend_slot(s, carry):
        p_len = listed[0, s]
        start = pl.multiple_of(listed[1, s], PACK)
        start_out = pl.multiple_of(listed[2, s], PACK)
        least = 0
        for length in spans:

            @pl.when(jnp.logical_and(p_len > least, p_len <= length))
            def _():
                attend(p_len, start, start_out, length)

            least = length
        return carry

    lax.fori_loop(0, slots, attend_slot, 0)

    for part, out in enumerate((out_other, out_own)):
        out_copies[part].wait()

        def put_out(t, carry):
            span = pl.ds(pl.multiple_of(t * TILE, TILE), TILE)

            def run(count):
                out[:count, span] = jnp.dot(
                    attended[:count], vo[part, :, span], preferred_element_type=jnp.float32
                ).astype(jnp.bfloat16)

            for_rows(used_out, row_counts(slots * total), run)
            return carry

        lax.fori_loop(0, half // TILE, put_out, 0)


def layer(ks, own, table, question, gain, mine, theirs, wq, wk, wv, wo):
    _, p_tokens, half = mine[0].shape
    _, q_tokens, cols = question.shape
    width = wq.shape[0]
    slots = CAPM * len(ks)
    total = q_tokens + p_tokens
    out = jax.ShapeDtypeStruct((slots * total, half), jnp.bfloat16)
    return pl.pallas_call(
        functools.partial(layer_kernel, ks),
        out_shape=[out, out],
        in_specs=[SMEM, SMEM, VMEM, VMEM] + [VMEM] * (2 * len(ks)) + [HBM] * 4,
        out_specs=[VMEM, VMEM],
        scratch_shapes=[
            pltpu.VMEM((3, width, cols), jnp.bfloat16),
            pltpu.VMEM((2, cols, half), jnp.bfloat16),
            pltpu.VMEM((2, slots * total, half), jnp.bfloat16),
            pltpu.VMEM((3, slots * p_tokens, cols), jnp.bfloat16),
            pltpu.SMEM((3, slots), jnp.int32),
            pltpu.SemaphoreType.DMA((3, 2)),
            pltpu.SemaphoreType.DMA((2,)),
        ],
        compiler_params=pltpu.CompilerParams(vmem_limit_bytes=VMEM_LAYER),
        cost_estimate=LITTLE,
        name="layer",
    )(own, table, question, gain, *mine, *theirs, wq, wk, wv, wo)


def combine_kernel(ks, first, own_ref, table, questions, *refs):
    n = len(ks)
    mine = refs[:n]
    ours, arrived = refs[n : n + 2]
    encoded, staged, sems = refs[n + 2 if first else n + 3 :]
    slots, total, _ = staged.shape
    q_tokens = questions.shape[1]
    q_len = own_ref[0, 2]
    places, _ = compact(table, ks, q_tokens)

    def copy(s, pair):
        return pltpu.make_async_copy(staged.at[s], encoded.at[0, pair], sems.at[s])

    for s, (p_len, _, start) in enumerate(places):
        pair = table[0, place_of(ks, s)]

        @pl.when(pair >= 0)
        def _():
            for rows, low, length in (
                (questions[0], 0, q_len),
                (mine[s // CAPM][s % CAPM], q_tokens, p_len),
            ):
                count = rows.shape[0]
                spot = lax.broadcasted_iota(jnp.int32, (count, 1), 0)
                at = pl.ds(pl.multiple_of(start + low, PACK), count)
                branch = ours[at].astype(jnp.float32) + arrived[at].astype(jnp.float32)
                made = rows.astype(jnp.float32) + branch
                staged[s, low : low + count] = jnp.where(spot < length, made, 0.0).astype(
                    jnp.bfloat16
                )
            copy(s, pair).start()

    for s in range(slots):

        @pl.when(table[0, place_of(ks, s)] >= 0)
        def _():
            copy(s, 0).wait()


def combine(ks, encoded, shape, own, table, questions, mine, ours, arrived):
    first = encoded is None
    slots = CAPM * len(ks)
    operands = [own, table, questions, *mine, ours, arrived] + ([] if first else [encoded])
    return pl.pallas_call(
        functools.partial(combine_kernel, ks, first),
        out_shape=jax.ShapeDtypeStruct(shape, jnp.bfloat16),
        in_specs=[SMEM, SMEM, VMEM] + [VMEM] * (len(ks) + 2) + ([] if first else [ANY]),
        out_specs=ANY,
        scratch_shapes=[
            pltpu.VMEM((slots, *shape[2:]), jnp.bfloat16),
            pltpu.SemaphoreType.DMA((slots,)),
        ],
        input_output_aliases={} if first else {len(operands) - 1: 0},
        compiler_params=pltpu.CompilerParams(vmem_limit_bytes=VMEM_LAYER),
        cost_estimate=LITTLE,
        name="combine",
    )(*operands)


def body(questions, memory, retrieved, q_len, p_len, norm_gain, w_query, w_key, w_value, w_out):
    shards = lax.axis_size("mem")
    cores = lax.axis_size("tp")
    _, q_tokens, half = questions.shape
    pass_dev, p_tokens, _ = memory.shape
    wants = retrieved.shape[1]

    def swap(x):
        return lax.ppermute(x, "tp", [(i, (i + 1) % cores) for i in range(cores)])

    def exchange(x, k):
        return lax.ppermute(x, "mem", [(i, i ^ k) for i in range(shards)])

    meta = jnp.concatenate(
        [retrieved[0], p_len, jnp.zeros((LANES - wants - pass_dev,), jnp.int32)]
    )[None]
    metas = lax.all_to_all(
        jnp.broadcast_to(meta[None], (shards, 1, LANES)), "mem", 0, 0, tiled=True
    )
    own = jnp.concatenate(
        [
            lax.axis_index("tp").astype(jnp.int32)[None],
            lax.axis_index("mem").astype(jnp.int32)[None],
            q_len,
            jnp.zeros((LANES - 3,), jnp.int32),
        ]
    )[None]
    gain = norm_gain.reshape(cores, 1, half)
    question = project_question(
        own, questions, swap(questions), gain, w_query, w_key, w_value
    )
    near = shards // 2
    first = (near, 1)
    rest = tuple(k for k in range(shards) if k not in first)
    sends, _ = pick(first, False, own, metas, memory, wants)
    later, *ready = lax.optimization_barrier((metas, *sends.values()))
    sends = dict(zip(first, ready))
    others, (table,) = pick(rest, True, own, later, memory, wants)
    sends.update(others)
    mine = {k: exchange(sends[k], k) if k else sends[0] for k in range(shards)}
    split = near + near // 2
    arrivals = [
        [here[i : i + MOST] for i in range(0, len(here), MOST)]
        for here in ((0,), tuple(range(1, split)), tuple(range(split, shards)))
    ]
    encoded = None
    shape = (1, wants, q_tokens + p_tokens, half)
    done = None
    for chunks in arrivals:
        here = [k for ks in chunks for k in ks]
        rows = [mine[k] for k in here]
        if done is not None:
            ks, kept, ours, other = done
            *rows, ours, other = lax.optimization_barrier((*rows, ours, other))
            done = (ks, kept, ours, other)
        mine.update(zip(here, rows))
        theirs = {k: swap(mine[k]) for k in here}
        for i, ks in enumerate(chunks):
            if done is not None:
                last, kept, ours, other = done
                ahead = theirs[ks[0]]
                if i:
                    held = () if encoded is None else (encoded,)
                    ahead, ours, other, *held = lax.optimization_barrier(
                        (ahead, ours, other, *held)
                    )
                    encoded = held[0] if held else None
                encoded = combine(
                    last, encoded, shape, own, table, questions, kept, ours, swap(other)
                )
                if not i:
                    ahead, encoded = lax.optimization_barrier((ahead, encoded))
                theirs[ks[0]] = ahead
            kept = [mine[k] for k in ks]
            done = (
                ks,
                kept,
                *layer(
                    ks, own, table, question, gain, kept, [theirs[k] for k in ks],
                    w_query, w_key, w_value, w_out,
                ),
            )
    last, kept, ours, other = done
    encoded = combine(last, encoded, shape, own, table, questions, kept, ours, swap(other))
    return encoded


def solution(mesh):
    in_specs = (
        P(("groups", "mem"), None, "tp"),
        P("mem", None, "tp"),
        P(("groups", "mem"), None),
        P(("groups", "mem")),
        P("mem"),
        P(),
        P(None, "tp"),
        P(None, "tp"),
        P(None, "tp"),
        P("tp", None),
    )
    out_specs = P(("groups", "mem"), None, None, "tp")
    return jax.shard_map(body, mesh=mesh, in_specs=in_specs, out_specs=out_specs, check_vma=False)
```

```python
import functools

import jax
import jax.numpy as jnp
from jax import lax
from jax.experimental import pallas as pl
from jax.experimental.pallas import tpu as pltpu
from jax.sharding import PartitionSpec as P

HS = 64
CAPM = 2
EPS = 1e-06
MASKED = -1e30
LANES = 128
PACK = 16
VMEM_ALL = 60 * 1024 * 1024
VMEM_LAYER = 44 * 1024 * 1024

ANY = pl.BlockSpec(memory_space=pl.ANY)
HBM = pl.BlockSpec(memory_space=pltpu.HBM)
SMEM = pl.BlockSpec(memory_space=pltpu.SMEM)
VMEM = pl.BlockSpec(memory_space=pltpu.VMEM)
LITTLE = pl.CostEstimate(flops=1, bytes_accessed=1, transcendentals=0)


def ask_kernel(pass_dev, wants, position, retrieved, p_len, q_len, metas, own_ref):
    shards = metas.shape[0]
    own_ref[0, 0] = position[0]
    own_ref[0, 1] = position[1]
    own_ref[0, 2] = q_len[0]
    for shard in range(shards):
        for r in range(CAPM):
            metas[shard, 0, r] = jnp.int32(-1)
            own_ref[1, CAPM * shard + r] = jnp.int32(-1)
        for i in range(pass_dev):
            metas[shard, 0, CAPM + i] = p_len[i]

    def place(j, carry):
        wanted = retrieved[0, j]
        shard = lax.div(wanted, pass_dev)
        taken = (metas[shard, 0, 0] >= 0).astype(jnp.int32)
        metas[shard, 0, taken] = wanted - shard * pass_dev
        own_ref[1, CAPM * shard + taken] = j
        return carry

    lax.fori_loop(0, wants, place, 0)


def ask(retrieved, p_len, q_len, shards):
    position = jnp.stack([lax.axis_index("tp"), lax.axis_index("mem")]).astype(jnp.int32)
    return pl.pallas_call(
        functools.partial(ask_kernel, p_len.shape[0], retrieved.shape[1]),
        out_shape=[
            jax.ShapeDtypeStruct((shards, 1, LANES), jnp.int32),
            jax.ShapeDtypeStruct((2, LANES), jnp.int32),
        ],
        in_specs=[SMEM] * 4,
        out_specs=[SMEM] * 2,
        cost_estimate=LITTLE,
        name="ask",
    )(position, retrieved, p_len, q_len)


def pick_kernel(own_ref, asked, metas, memory, *refs):
    shards = metas.shape[0]
    outs = refs[:shards]
    table, sems = refs[shards:]
    me = own_ref[0, 1]
    found = []
    for k in range(shards):
        partner = lax.bitwise_xor(me, k)
        for r in range(CAPM):
            local = metas[partner, 0, r]
            found.append((local, pltpu.make_async_copy(
                memory.at[jnp.maximum(local, 0)], outs[k].at[r], sems.at[k, r]
            )))

            @pl.when(local >= 0)
            def _():
                found[-1][1].start()

    for k in range(shards):
        partner = lax.bitwise_xor(me, k)
        for r in range(CAPM):
            pair = own_ref[1, CAPM * partner + r]
            local = jnp.maximum(asked[partner, 0, r], 0)
            table[0, CAPM * k + r] = pair
            table[1, CAPM * k + r] = jnp.where(pair >= 0, metas[partner, 0, CAPM + local], 0)
    for local, copy in found:

        @pl.when(local >= 0)
        def _():
            copy.wait()


def pick(own, asked, metas, memory):
    shards = metas.shape[0]
    _, p_tokens, half = memory.shape
    slot = jax.ShapeDtypeStruct((CAPM, p_tokens, half), memory.dtype)
    result = pl.pallas_call(
        pick_kernel,
        out_shape=[slot] * shards + [jax.ShapeDtypeStruct((2, LANES), jnp.int32)],
        in_specs=[SMEM, SMEM, SMEM, HBM],
        out_specs=[VMEM] * shards + [SMEM],
        scratch_shapes=[pltpu.SemaphoreType.DMA((shards, CAPM))],
        compiler_params=pltpu.CompilerParams(vmem_limit_bytes=VMEM_ALL),
        cost_estimate=LITTLE,
        name="pick",
    )(own, asked, metas, memory)
    return result[:shards], result[shards]


def normed_halves(own, other, gain_own, gain_other):
    own = own.astype(jnp.float32)
    other = other.astype(jnp.float32)
    total = jnp.sum(own * own + other * other, axis=-1, keepdims=True)
    scale = lax.rsqrt(total / (2 * own.shape[-1]) + EPS)
    return (
        (own * scale * gain_own).astype(jnp.bfloat16),
        (other * scale * gain_other).astype(jnp.bfloat16),
    )


def weight_copies(c, half, sources, targets, sems):
    copies = []
    for i, (source, target) in enumerate(zip(sources, targets)):
        pieces = []
        for part, core in enumerate((c, 1 - c)):
            start = pl.multiple_of(core * half, half)
            pieces.append(
                pltpu.make_async_copy(
                    source.at[pl.ds(start, half), :],
                    target.at[pl.ds(part * half, half), :],
                    sems.at[i, part],
                )
            )
        copies.append(pieces)
    return copies


def question_kernel(own_ref, mine, theirs, gain, wq, wk, wv, out, vq, vk, vv, sems):
    c = own_ref[0, 0]
    half = mine.shape[-1]
    copies = weight_copies(c, half, (wq, wk, wv), (vq, vk, vv), sems)
    for pieces in copies:
        for piece in pieces:
            piece.start()
    g_own = gain[c].astype(jnp.float32)
    g_other = gain[1 - c].astype(jnp.float32)
    first, second = normed_halves(mine[0], theirs[0], g_own, g_other)
    rows = jnp.concatenate([first, second], axis=1)
    for i, weight in enumerate((vq, vk, vv)):
        for piece in copies[i]:
            piece.wait()
        made = jnp.dot(rows, weight[...], preferred_element_type=jnp.float32)
        made = made.astype(jnp.bfloat16)
        if i == 0:
            made = made * jnp.bfloat16(1.0 / 8.0)
        out[i] = made


def project_question(own, mine, theirs, gain, wq, wk, wv):
    _, q_tokens, half = mine.shape
    width, cols = wq.shape
    weight = pltpu.VMEM((width, cols), jnp.bfloat16)
    return pl.pallas_call(
        question_kernel,
        out_shape=jax.ShapeDtypeStruct((3, q_tokens, cols), jnp.bfloat16),
        in_specs=[SMEM, VMEM, VMEM, VMEM, HBM, HBM, HBM],
        out_specs=VMEM,
        scratch_shapes=[weight] * 3 + [pltpu.SemaphoreType.DMA((3, 2))],
        compiler_params=pltpu.CompilerParams(vmem_limit_bytes=VMEM_ALL),
        cost_estimate=LITTLE,
        name="question_projections",
    )(own, mine, theirs, gain, wq, wk, wv)


def place_of(ks, s):
    return CAPM * ks[s // CAPM] + s % CAPM


def compact(table, ks, q_tokens):
    places = []
    start = jnp.int32(0)
    start_out = jnp.int32(0)
    for s in range(CAPM * len(ks)):
        p_len = table[1, place_of(ks, s)]
        room = lax.bitwise_and(p_len + (PACK - 1), ~(PACK - 1))
        places.append((p_len, pl.multiple_of(start, PACK), pl.multiple_of(start_out, PACK)))
        start = start + room
        start_out = start_out + jnp.where(p_len > 0, room + q_tokens, 0)
    return places, start_out


def pick_span(p_len, spans):
    span = jnp.int32(spans[-1])
    for candidate in reversed(spans[:-1]):
        span = jnp.where(p_len <= candidate, candidate, span)
    return span


def for_rows(needed, most, run):
    least = 0
    for count in [c for c in range(128, most, 128)] + [most]:

        @pl.when(jnp.logical_and(needed > least, needed <= count))
        def _():
            run(count)

        least = count


def layer_kernel(ks, own_ref, table, question, gain, *refs):
    n = len(ks)
    mine, theirs = refs[:n], refs[n : 2 * n]
    wq, wk, wv, wo = refs[2 * n : 2 * n + 4]
    out_own, out_other = refs[2 * n + 4 : 2 * n + 6]
    vq, vk, vv, vo, rows, query, key, value, attended, sems, sems_out = refs[2 * n + 6 :]
    cols = query.shape[1]
    q_tokens = question.shape[1]
    _, p_tokens, half = mine[0].shape
    slots = CAPM * n
    total = q_tokens + p_tokens
    spans = (p_tokens // 2, 3 * p_tokens // 4, p_tokens)
    c = own_ref[0, 0]
    q_len = own_ref[0, 2]
    copies = weight_copies(c, half, (wq, wk, wv), (vq, vk, vv), sems)
    out_copies = []
    for part, core in enumerate((1 - c, c)):
        start = pl.multiple_of(core * half, half)
        out_copies.append(
            pltpu.make_async_copy(wo.at[:, pl.ds(start, half)], vo.at[part], sems_out.at[part])
        )
    for pieces in copies + [out_copies]:
        for piece in pieces:
            piece.start()
    places, used_out = compact(table, ks, q_tokens)
    used = jnp.int32(0)
    for p_len, start, _ in places:
        used = jnp.where(p_len > 0, jnp.maximum(used, start + pick_span(p_len, spans)), used)
    g_own = gain[c].astype(jnp.float32)
    g_other = gain[1 - c].astype(jnp.float32)
    for s, (p_len, start, _) in enumerate(places):

        @pl.when(p_len > 0)
        def _():
            first, second = normed_halves(
                mine[s // CAPM][s % CAPM], theirs[s // CAPM][s % CAPM], g_own, g_other
            )
            rows[pl.ds(start, p_tokens), :half] = first
            rows[pl.ds(start, p_tokens), half:] = second

    for i, (weight, target) in enumerate(((vq, query), (vk, key), (vv, value))):
        for piece in copies[i]:
            piece.wait()

        def project(count):
            for left in range(0, cols, 256):
                span = slice(left, left + 256)
                made = jnp.dot(
                    rows[:count], weight[:, span], preferred_element_type=jnp.float32
                ).astype(jnp.bfloat16)
                if i == 0:
                    made = made * jnp.bfloat16(1.0 / 8.0)
                target[:count, span] = made

        for_rows(used, slots * p_tokens, project)

    lane = lax.broadcasted_iota(jnp.int32, (1, 2 * HS), 1)
    in_first = lane < HS

    def attend(p_len, start, start_out, length):
        both = q_tokens + length
        spot = lax.broadcasted_iota(jnp.int32, (1, both), 1)
        end = jnp.where(spot < q_tokens, q_len, q_tokens + p_len)
        bias = jnp.where(spot < end, 0.0, MASKED)
        ones = jnp.ones((both, 2 * HS), jnp.bfloat16)

        def pair_rows(i, source, span):
            return jnp.concatenate(
                [question[i, :, span], source[pl.ds(start, length), span]], axis=0
            )

        def score(left):
            span = slice(left, left + 2 * HS)
            q2 = pair_rows(0, query, span)
            zero = jnp.zeros_like(q2)
            q2 = jnp.concatenate(
                [jnp.where(in_first, q2, zero), jnp.where(in_first, zero, q2)], axis=0
            )
            return lax.dot_general(
                q2,
                pair_rows(1, key, span),
                (((1,), (1,)), ((), ())),
                preferred_element_type=jnp.float32,
            )

        lefts = range(0, cols, 2 * HS)
        scores = [score(left) + bias for left in lefts]
        largest = [jnp.max(x, axis=1, keepdims=True) for x in scores]
        raised = [jnp.exp(x - m).astype(jnp.bfloat16) for x, m in zip(scores, largest)]
        with_sums = [
            jnp.dot(
                x,
                jnp.concatenate([pair_rows(2, value, slice(left, left + 2 * HS)), ones], axis=1),
                preferred_element_type=jnp.float32,
            )
            for x, left in zip(raised, lefts)
        ]
        for with_sum, left in zip(with_sums, lefts):
            top, bottom = with_sum[:both], with_sum[both:]
            mixed = jnp.where(in_first, top[:, : 2 * HS], bottom[:, : 2 * HS])
            weight_sum = jnp.where(in_first, top[:, 2 * HS :], bottom[:, 2 * HS :])
            attended[pl.ds(start_out, both), left : left + 2 * HS] = (
                mixed / weight_sum
            ).astype(jnp.bfloat16)

    for s, (p_len, start, start_out) in enumerate(places):
        least = 0
        for length in spans:

            @pl.when(jnp.logical_and(p_len > least, p_len <= length))
            def _():
                attend(p_len, start, start_out, length)

            least = length

    for part, out in enumerate((out_other, out_own)):
        out_copies[part].wait()

        def put_out(count):
            for left in range(0, half, 256):
                span = slice(left, left + 256)
                out[:count, span] = jnp.dot(
                    attended[:count], vo[part, :, span], preferred_element_type=jnp.float32
                ).astype(jnp.bfloat16)

        for_rows(used_out, slots * total, put_out)


def layer(ks, own, table, question, gain, mine, theirs, wq, wk, wv, wo):
    _, p_tokens, half = mine[0].shape
    _, q_tokens, cols = question.shape
    width = wq.shape[0]
    slots = CAPM * len(ks)
    total = q_tokens + p_tokens
    weight = pltpu.VMEM((width, cols), jnp.bfloat16)
    packed = pltpu.VMEM((slots * p_tokens, cols), jnp.bfloat16)
    out = jax.ShapeDtypeStruct((slots * total, half), jnp.bfloat16)
    return pl.pallas_call(
        functools.partial(layer_kernel, ks),
        out_shape=[out, out],
        in_specs=[SMEM, SMEM, VMEM, VMEM] + [VMEM] * (2 * len(ks)) + [HBM] * 4,
        out_specs=[VMEM, VMEM],
        scratch_shapes=[weight] * 3
        + [
            pltpu.VMEM((2, cols, half), jnp.bfloat16),
            pltpu.VMEM((slots * p_tokens, width), jnp.bfloat16),
            packed,
            packed,
            packed,
            pltpu.VMEM((slots * total, cols), jnp.bfloat16),
            pltpu.SemaphoreType.DMA((3, 2)),
            pltpu.SemaphoreType.DMA((2,)),
        ],
        compiler_params=pltpu.CompilerParams(vmem_limit_bytes=VMEM_LAYER),
        cost_estimate=LITTLE,
        name="layer",
    )(own, table, question, gain, *mine, *theirs, wq, wk, wv, wo)


def combine_kernel(ks, first, own_ref, table, questions, *refs):
    n = len(ks)
    mine = refs[:n]
    ours, arrived = refs[n : n + 2]
    encoded, staged, sems = refs[n + 2 if first else n + 3 :]
    slots, total, _ = staged.shape
    q_tokens = questions.shape[1]
    q_len = own_ref[0, 2]
    places, _ = compact(table, ks, q_tokens)

    def copy(s, pair):
        return pltpu.make_async_copy(staged.at[s], encoded.at[0, pair], sems.at[s])

    for s, (p_len, _, start) in enumerate(places):
        pair = table[0, place_of(ks, s)]

        @pl.when(pair >= 0)
        def _():
            for rows, low, length in (
                (questions[0], 0, q_len),
                (mine[s // CAPM][s % CAPM], q_tokens, p_len),
            ):
                count = rows.shape[0]
                spot = lax.broadcasted_iota(jnp.int32, (count, 1), 0)
                at = pl.ds(pl.multiple_of(start + low, PACK), count)
                branch = ours[at].astype(jnp.float32) + arrived[at].astype(jnp.float32)
                made = rows.astype(jnp.float32) + branch
                staged[s, low : low + count] = jnp.where(spot < length, made, 0.0).astype(
                    jnp.bfloat16
                )
            copy(s, pair).start()

    for s in range(slots):

        @pl.when(table[0, place_of(ks, s)] >= 0)
        def _():
            copy(s, 0).wait()


def combine(ks, encoded, shape, own, table, questions, mine, ours, arrived):
    first = encoded is None
    slots = CAPM * len(ks)
    operands = [own, table, questions, *mine, ours, arrived] + ([] if first else [encoded])
    return pl.pallas_call(
        functools.partial(combine_kernel, ks, first),
        out_shape=jax.ShapeDtypeStruct(shape, jnp.bfloat16),
        in_specs=[SMEM, SMEM, VMEM] + [VMEM] * (len(ks) + 2) + ([] if first else [ANY]),
        out_specs=ANY,
        scratch_shapes=[
            pltpu.VMEM((slots, *shape[2:]), jnp.bfloat16),
            pltpu.SemaphoreType.DMA((slots,)),
        ],
        input_output_aliases={} if first else {len(operands) - 1: 0},
        compiler_params=pltpu.CompilerParams(vmem_limit_bytes=VMEM_LAYER),
        cost_estimate=LITTLE,
        name="combine",
    )(*operands)


def body(questions, memory, retrieved, q_len, p_len, norm_gain, w_query, w_key, w_value, w_out):
    shards = lax.axis_size("mem")
    cores = lax.axis_size("tp")
    _, q_tokens, half = questions.shape
    p_tokens = memory.shape[1]
    wants = retrieved.shape[1]

    def swap(x):
        return lax.ppermute(x, "tp", [(i, (i + 1) % cores) for i in range(cores)])

    def exchange(x, k):
        return lax.ppermute(x, "mem", [(i, i ^ k) for i in range(shards)])

    asked, own = ask(retrieved, p_len, q_len, shards)
    metas = lax.all_to_all(asked, "mem", 0, 0, tiled=True)
    gain = norm_gain.reshape(cores, 1, half)
    question = project_question(
        own, questions, swap(questions), gain, w_query, w_key, w_value
    )
    sends, table = pick(own, asked, metas, memory)
    mine = [sends[0]] + [exchange(sends[k], k) for k in range(1, shards)]
    encoded = None
    shape = (1, wants, q_tokens + p_tokens, half)
    waiting = None
    near = shards // 2
    chunks = [(0,)] + [(k, near - 1 + k) for k in range(1, near)] + [(shards - 1,)]
    for i, ks in enumerate(chunks):
        here = range(1, near + 1) if i == 1 else ks[-1:]
        if waiting is not None:
            rows = [mine[k] for k in here]
            *rows, ours, other = lax.optimization_barrier((*rows, *waiting[2:]))
            for k, x in zip(here, rows):
                mine[k] = x
        rows = [mine[k] for k in ks]
        theirs = [swap(x) for x in rows]
        if waiting is not None:
            encoded = combine(
                waiting[0], encoded, shape, own, table, questions, waiting[1], ours, swap(other)
            )
            theirs[0], encoded = lax.optimization_barrier((theirs[0], encoded))
        made = layer(
            ks, own, table, question, gain, rows, theirs, w_query, w_key, w_value, w_out
        )
        waiting = (ks, rows, *made)
    ks, rows, ours, other = waiting
    encoded = combine(ks, encoded, shape, own, table, questions, rows, ours, swap(other))
    return encoded


def solution(mesh):
    in_specs = (
        P(("groups", "mem"), None, "tp"),
        P("mem", None, "tp"),
        P(("groups", "mem"), None),
        P(("groups", "mem")),
        P("mem"),
        P(),
        P(None, "tp"),
        P(None, "tp"),
        P(None, "tp"),
        P("tp", None),
    )
    out_specs = P(("groups", "mem"), None, None, "tp")
    return jax.shard_map(body, mesh=mesh, in_specs=in_specs, out_specs=out_specs, check_vma=False)
```

```python
import functools

import jax
import jax.numpy as jnp
from jax import lax
from jax.experimental import pallas as pl
from jax.experimental.pallas import tpu as pltpu
from jax.sharding import PartitionSpec as P

HS = 64
CAPM = 2
EPS = 1e-06
MASKED = -1e30
LANES = 128
PACK = 16
VMEM_ALL = 60 * 1024 * 1024
VMEM_LAYER = 48 * 1024 * 1024

ANY = pl.BlockSpec(memory_space=pl.ANY)
HBM = pl.BlockSpec(memory_space=pltpu.HBM)
SMEM = pl.BlockSpec(memory_space=pltpu.SMEM)
VMEM = pl.BlockSpec(memory_space=pltpu.VMEM)
LITTLE = pl.CostEstimate(flops=1, bytes_accessed=1, transcendentals=0)


def ask_kernel(pass_dev, wants, position, retrieved, p_len, q_len, metas, own_ref):
    shards = metas.shape[0]
    own_ref[0, 0] = position[0]
    own_ref[0, 1] = position[1]
    own_ref[0, 2] = q_len[0]
    for shard in range(shards):
        for r in range(CAPM):
            metas[shard, 0, r] = jnp.int32(-1)
            own_ref[1, CAPM * shard + r] = jnp.int32(-1)
        for i in range(pass_dev):
            metas[shard, 0, CAPM + i] = p_len[i]

    def place(j, carry):
        wanted = retrieved[0, j]
        shard = lax.div(wanted, pass_dev)
        taken = (metas[shard, 0, 0] >= 0).astype(jnp.int32)
        metas[shard, 0, taken] = wanted - shard * pass_dev
        own_ref[1, CAPM * shard + taken] = j
        return carry

    lax.fori_loop(0, wants, place, 0)


def ask(retrieved, p_len, q_len, shards):
    position = jnp.stack([lax.axis_index("tp"), lax.axis_index("mem")]).astype(jnp.int32)
    return pl.pallas_call(
        functools.partial(ask_kernel, p_len.shape[0], retrieved.shape[1]),
        out_shape=[
            jax.ShapeDtypeStruct((shards, 1, LANES), jnp.int32),
            jax.ShapeDtypeStruct((2, LANES), jnp.int32),
        ],
        in_specs=[SMEM] * 4,
        out_specs=[SMEM] * 2,
        cost_estimate=LITTLE,
        name="ask",
    )(position, retrieved, p_len, q_len)


def pick_kernel(ks, own_ref, asked, metas, memory, *refs):
    n = len(ks)
    outs = refs[:n]
    table = refs[n] if len(refs) > n + 2 else None
    staged, sems = refs[-2:]
    shards = metas.shape[0]
    me = own_ref[0, 1]
    found = []
    for i, k in enumerate(ks):
        partner = lax.bitwise_xor(me, k)
        for r in range(CAPM):
            local = metas[partner, 0, r]
            found.append(
                (
                    local,
                    pltpu.make_async_copy(
                        memory.at[jnp.maximum(local, 0)], staged.at[i, r], sems.at[0, i, r]
                    ),
                    pltpu.make_async_copy(staged.at[i, r], outs[i].at[r], sems.at[1, i, r]),
                )
            )

            @pl.when(local >= 0)
            def _():
                found[-1][1].start()

    if table is not None:
        for k in range(shards):
            partner = lax.bitwise_xor(me, k)
            for r in range(CAPM):
                pair = own_ref[1, CAPM * partner + r]
                local = jnp.maximum(asked[partner, 0, r], 0)
                table[0, CAPM * k + r] = pair
                table[1, CAPM * k + r] = jnp.where(
                    pair >= 0, metas[partner, 0, CAPM + local], 0
                )
    for local, come, go in found:

        @pl.when(local >= 0)
        def _():
            come.wait()
            go.start()

    for local, _, go in found:

        @pl.when(local >= 0)
        def _():
            go.wait()


def pick(ks, with_table, own, asked, metas, memory):
    n = len(ks)
    _, p_tokens, half = memory.shape
    slot = jax.ShapeDtypeStruct((CAPM, p_tokens, half), memory.dtype)
    result = pl.pallas_call(
        functools.partial(pick_kernel, ks),
        out_shape=[slot] * n + [jax.ShapeDtypeStruct((2, LANES), jnp.int32)] * with_table,
        in_specs=[SMEM, SMEM, SMEM, HBM],
        out_specs=[ANY] * n + [SMEM] * with_table,
        scratch_shapes=[
            pltpu.VMEM((n, CAPM, p_tokens, half), memory.dtype),
            pltpu.SemaphoreType.DMA((2, n, CAPM)),
        ],
        compiler_params=pltpu.CompilerParams(vmem_limit_bytes=VMEM_ALL),
        cost_estimate=LITTLE,
        name="pick",
    )(own, asked, metas, memory)
    return dict(zip(ks, result)), result[n:]


def normed_halves(own, other, gain_own, gain_other):
    own = own.astype(jnp.float32)
    other = other.astype(jnp.float32)
    total = jnp.sum(own * own + other * other, axis=-1, keepdims=True)
    scale = lax.rsqrt(total / (2 * own.shape[-1]) + EPS)
    return (
        (own * scale * gain_own).astype(jnp.bfloat16),
        (other * scale * gain_other).astype(jnp.bfloat16),
    )


def weight_copies(c, half, sources, targets, sems):
    copies = []
    for i, (source, target) in enumerate(zip(sources, targets)):
        pieces = []
        for part, core in enumerate((c, 1 - c)):
            start = pl.multiple_of(core * half, half)
            pieces.append(
                pltpu.make_async_copy(
                    source.at[pl.ds(start, half), :],
                    target.at[pl.ds(part * half, half), :],
                    sems.at[i, part],
                )
            )
        copies.append(pieces)
    return copies


def question_kernel(own_ref, mine, theirs, gain, wq, wk, wv, out, vq, vk, vv, sems):
    c = own_ref[0, 0]
    half = mine.shape[-1]
    copies = weight_copies(c, half, (wq, wk, wv), (vq, vk, vv), sems)
    for pieces in copies:
        for piece in pieces:
            piece.start()
    g_own = gain[c].astype(jnp.float32)
    g_other = gain[1 - c].astype(jnp.float32)
    first, second = normed_halves(mine[0], theirs[0], g_own, g_other)
    rows = jnp.concatenate([first, second], axis=1)
    for i, weight in enumerate((vq, vk, vv)):
        for piece in copies[i]:
            piece.wait()
        made = jnp.dot(rows, weight[...], preferred_element_type=jnp.float32)
        made = made.astype(jnp.bfloat16)
        if i == 0:
            made = made * jnp.bfloat16(1.0 / 8.0)
        out[i] = made


def project_question(own, mine, theirs, gain, wq, wk, wv):
    _, q_tokens, half = mine.shape
    width, cols = wq.shape
    weight = pltpu.VMEM((width, cols), jnp.bfloat16)
    return pl.pallas_call(
        question_kernel,
        out_shape=jax.ShapeDtypeStruct((3, q_tokens, cols), jnp.bfloat16),
        in_specs=[SMEM, VMEM, VMEM, VMEM, HBM, HBM, HBM],
        out_specs=VMEM,
        scratch_shapes=[weight] * 3 + [pltpu.SemaphoreType.DMA((3, 2))],
        compiler_params=pltpu.CompilerParams(vmem_limit_bytes=VMEM_ALL),
        cost_estimate=LITTLE,
        name="question_projections",
    )(own, mine, theirs, gain, wq, wk, wv)


def place_of(ks, s):
    return CAPM * ks[s // CAPM] + s % CAPM


def compact(table, ks, q_tokens):
    places = []
    start = jnp.int32(0)
    start_out = jnp.int32(0)
    for s in range(CAPM * len(ks)):
        p_len = table[1, place_of(ks, s)]
        room = lax.bitwise_and(p_len + (PACK - 1), ~(PACK - 1))
        places.append((p_len, pl.multiple_of(start, PACK), pl.multiple_of(start_out, PACK)))
        start = start + room
        start_out = start_out + jnp.where(p_len > 0, room + q_tokens, 0)
    return places, start_out


def pick_span(p_len, spans):
    span = jnp.int32(spans[-1][1])
    for queries, keys in reversed(spans[:-1]):
        span = jnp.where(p_len <= queries, keys, span)
    return span


def for_rows(needed, most, run):
    least = 0
    for count in [c for c in range(128, most, 128)] + [most]:

        @pl.when(jnp.logical_and(needed > least, needed <= count))
        def _():
            run(count)

        least = count


def layer_kernel(ks, own_ref, table, question, gain, *refs):
    n = len(ks)
    mine, theirs = refs[:n], refs[n : 2 * n]
    wq, wk, wv, wo = refs[2 * n : 2 * n + 4]
    out_own, out_other = refs[2 * n + 4 : 2 * n + 6]
    vq, vk, vv, vo, rows, query, key, value, attended, raw, made_out = refs[2 * n + 6 : -4]
    sems, sems_out, sems_rows, sems_made = refs[-4:]
    cols = query.shape[1]
    q_tokens = question.shape[1]
    _, p_tokens, half = mine[0].shape
    slots = CAPM * n
    total = q_tokens + p_tokens
    spans = (
        (p_tokens // 2, 3 * p_tokens // 4),
        (3 * p_tokens // 4, 3 * p_tokens // 4),
        (p_tokens, p_tokens),
    )
    c = own_ref[0, 0]
    q_len = own_ref[0, 2]
    copies = weight_copies(c, half, (wq, wk, wv), (vq, vk, vv), sems)
    out_copies = []
    for part, core in enumerate((1 - c, c)):
        start = pl.multiple_of(core * half, half)
        out_copies.append(
            pltpu.make_async_copy(wo.at[:, pl.ds(start, half)], vo.at[part], sems_out.at[part])
        )
    row_copies = []
    for part, sources in enumerate((mine, theirs)):
        for i, source in enumerate(sources):
            row_copies.append(
                pltpu.make_async_copy(source, raw.at[part, i], sems_rows.at[part, i])
            )
    for pieces in [row_copies] + copies + [out_copies]:
        for piece in pieces:
            piece.start()
    places, used_out = compact(table, ks, q_tokens)
    used = jnp.int32(0)
    for p_len, start, _ in places:
        used = jnp.where(p_len > 0, jnp.maximum(used, start + pick_span(p_len, spans)), used)
    g_own = gain[c].astype(jnp.float32)
    g_other = gain[1 - c].astype(jnp.float32)
    for piece in row_copies:
        piece.wait()
    for s, (p_len, start, _) in enumerate(places):

        @pl.when(p_len > 0)
        def _():
            first, second = normed_halves(
                raw[0, s // CAPM, s % CAPM], raw[1, s // CAPM, s % CAPM], g_own, g_other
            )
            rows[pl.ds(start, p_tokens), :half] = first
            rows[pl.ds(start, p_tokens), half:] = second

    for i, (weight, target) in enumerate(((vq, query), (vk, key), (vv, value))):
        for piece in copies[i]:
            piece.wait()

        def project(count):
            for left in range(0, cols, 256):
                span = slice(left, left + 256)
                made = jnp.dot(
                    rows[:count], weight[:, span], preferred_element_type=jnp.float32
                ).astype(jnp.bfloat16)
                if i == 0:
                    made = made * jnp.bfloat16(1.0 / 8.0)
                target[:count, span] = made

        for_rows(used, slots * p_tokens, project)

    lane = lax.broadcasted_iota(jnp.int32, (1, 2 * HS), 1)
    in_first = lane < HS

    def attend(p_len, start, start_out, queries, keys):
        both = q_tokens + queries
        room = -(-(q_tokens + keys) // LANES) * LANES
        spot = lax.broadcasted_iota(jnp.int32, (1, room), 1)
        end = jnp.where(spot < q_tokens, q_len, q_tokens + p_len)
        bias = jnp.where(spot < end, 0.0, MASKED)
        bias = jnp.concatenate([bias, bias], axis=1)
        one = jnp.ones((room, 2 * HS), jnp.bfloat16)

        def pair_rows(i, source, count, span):
            return jnp.concatenate(
                [question[i, :, span], source[pl.ds(start, count), span]], axis=0
            )

        def key_rows(i, source, span):
            found = pair_rows(i, source, keys, span)
            if room > found.shape[0]:
                fill = jnp.zeros((room - found.shape[0], 2 * HS), jnp.bfloat16)
                found = jnp.concatenate([found, fill], axis=0)
            return found

        def by_head(x):
            zero = jnp.zeros_like(x)
            return jnp.concatenate(
                [jnp.where(in_first, x, zero), jnp.where(in_first, zero, x)], axis=0
            )

        spans_here = [slice(left, left + 2 * HS) for left in range(0, cols, 2 * HS)]
        scores = [
            lax.dot_general(
                pair_rows(0, query, queries, span),
                by_head(key_rows(1, key, span)),
                (((1,), (1,)), ((), ())),
                preferred_element_type=jnp.float32,
            )
            + bias
            for span in spans_here
        ]
        raised = []
        for x in scores:
            halves = (x[:, :room], x[:, room:])
            raised.append(
                jnp.concatenate(
                    [
                        jnp.exp(y - jnp.max(y, axis=1, keepdims=True)).astype(jnp.bfloat16)
                        for y in halves
                    ],
                    axis=1,
                )
            )
        ones = by_head(one)
        with_sums = [
            jnp.dot(
                x,
                jnp.concatenate([by_head(key_rows(2, value, span)), ones], axis=1),
                preferred_element_type=jnp.float32,
            )
            for x, span in zip(raised, spans_here)
        ]
        for x, span in zip(with_sums, spans_here):
            attended[pl.ds(start_out, both), span] = (
                x[:, : 2 * HS] / x[:, 2 * HS :]
            ).astype(jnp.bfloat16)

    for s, (p_len, start, start_out) in enumerate(places):
        least = 0
        for queries, keys in spans:

            @pl.when(jnp.logical_and(p_len > least, p_len <= queries))
            def _():
                attend(p_len, start, start_out, queries, keys)

            least = queries

    sent = []
    for part, out in enumerate((out_other, out_own)):
        out_copies[part].wait()

        def put_out(count):
            for left in range(0, half, 256):
                span = slice(left, left + 256)
                made_out[part, :count, span] = jnp.dot(
                    attended[:count], vo[part, :, span], preferred_element_type=jnp.float32
                ).astype(jnp.bfloat16)

        for_rows(used_out, slots * total, put_out)
        sent.append(pltpu.make_async_copy(made_out.at[part], out, sems_made.at[part]))
        sent[-1].start()
    for piece in sent:
        piece.wait()


def layer(ks, own, table, question, gain, mine, theirs, wq, wk, wv, wo):
    _, p_tokens, half = mine[0].shape
    _, q_tokens, cols = question.shape
    width = wq.shape[0]
    slots = CAPM * len(ks)
    total = q_tokens + p_tokens
    weight = pltpu.VMEM((width, cols), jnp.bfloat16)
    packed = pltpu.VMEM((slots * p_tokens, cols), jnp.bfloat16)
    out = jax.ShapeDtypeStruct((slots * total, half), jnp.bfloat16)
    return pl.pallas_call(
        functools.partial(layer_kernel, ks),
        out_shape=[out, out],
        in_specs=[SMEM, SMEM, VMEM, VMEM] + [ANY] * (2 * len(ks)) + [HBM] * 4,
        out_specs=[ANY, ANY],
        scratch_shapes=[weight] * 3
        + [
            pltpu.VMEM((2, cols, half), jnp.bfloat16),
            pltpu.VMEM((slots * p_tokens, width), jnp.bfloat16),
            packed,
            packed,
            packed,
            pltpu.VMEM((slots * total, cols), jnp.bfloat16),
            pltpu.VMEM((2, len(ks), CAPM, p_tokens, half), jnp.bfloat16),
            pltpu.VMEM((2, slots * total, half), jnp.bfloat16),
            pltpu.SemaphoreType.DMA((3, 2)),
            pltpu.SemaphoreType.DMA((2,)),
            pltpu.SemaphoreType.DMA((2, len(ks))),
            pltpu.SemaphoreType.DMA((2,)),
        ],
        compiler_params=pltpu.CompilerParams(vmem_limit_bytes=VMEM_LAYER),
        cost_estimate=LITTLE,
        name="layer",
    )(own, table, question, gain, *mine, *theirs, wq, wk, wv, wo)


def combine_kernel(ks, first, own_ref, table, questions, *refs):
    n = len(ks)
    mine = refs[:n]
    ours, arrived = refs[n : n + 2]
    encoded, staged, sems = refs[n + 2 if first else n + 3 :]
    slots, total, _ = staged.shape
    q_tokens = questions.shape[1]
    q_len = own_ref[0, 2]
    places, _ = compact(table, ks, q_tokens)

    def copy(s, pair):
        return pltpu.make_async_copy(staged.at[s], encoded.at[0, pair], sems.at[s])

    for s, (p_len, _, start) in enumerate(places):
        pair = table[0, place_of(ks, s)]

        @pl.when(pair >= 0)
        def _():
            for rows, low, length in (
                (questions[0], 0, q_len),
                (mine[s // CAPM][s % CAPM], q_tokens, p_len),
            ):
                count = rows.shape[0]
                spot = lax.broadcasted_iota(jnp.int32, (count, 1), 0)
                at = pl.ds(pl.multiple_of(start + low, PACK), count)
                branch = ours[at].astype(jnp.float32) + arrived[at].astype(jnp.float32)
                made = rows.astype(jnp.float32) + branch
                staged[s, low : low + count] = jnp.where(spot < length, made, 0.0).astype(
                    jnp.bfloat16
                )
            copy(s, pair).start()

    for s in range(slots):

        @pl.when(table[0, place_of(ks, s)] >= 0)
        def _():
            copy(s, 0).wait()


def combine(ks, encoded, shape, own, table, questions, mine, ours, arrived):
    first = encoded is None
    slots = CAPM * len(ks)
    operands = [own, table, questions, *mine, ours, arrived] + ([] if first else [encoded])
    return pl.pallas_call(
        functools.partial(combine_kernel, ks, first),
        out_shape=jax.ShapeDtypeStruct(shape, jnp.bfloat16),
        in_specs=[SMEM, SMEM, VMEM] + [VMEM] * (len(ks) + 2) + ([] if first else [ANY]),
        out_specs=ANY,
        scratch_shapes=[
            pltpu.VMEM((slots, *shape[2:]), jnp.bfloat16),
            pltpu.SemaphoreType.DMA((slots,)),
        ],
        input_output_aliases={} if first else {len(operands) - 1: 0},
        compiler_params=pltpu.CompilerParams(vmem_limit_bytes=VMEM_LAYER),
        cost_estimate=LITTLE,
        name="combine",
    )(*operands)


def body(questions, memory, retrieved, q_len, p_len, norm_gain, w_query, w_key, w_value, w_out):
    shards = lax.axis_size("mem")
    cores = lax.axis_size("tp")
    _, q_tokens, half = questions.shape
    p_tokens = memory.shape[1]
    wants = retrieved.shape[1]

    def swap(x):
        return lax.ppermute(x, "tp", [(i, (i + 1) % cores) for i in range(cores)])

    def exchange(x, k):
        return lax.ppermute(x, "mem", [(i, i ^ k) for i in range(shards)])

    asked, own = ask(retrieved, p_len, q_len, shards)
    metas = lax.all_to_all(asked, "mem", 0, 0, tiled=True)
    gain = norm_gain.reshape(cores, 1, half)
    question = project_question(
        own, questions, swap(questions), gain, w_query, w_key, w_value
    )
    near = shards // 2
    chunks = [(0,)] + [(k, near - 1 + k) for k in range(1, near)] + [(shards - 1,)]
    come = [(0,), (1, 2, near)] + [
        (k, near - 2 + k) if k < near else (near - 2 + k,) for k in range(3, near + 2)
    ]
    first = (0, 1, 2, near)
    rest = tuple(k for k in range(shards) if k not in first)
    sends, (table,) = pick(first, True, own, asked, metas, memory)
    mine = {0: sends[0]}
    for k in first[1:]:
        mine[k] = exchange(sends[k], k)
    later, question = lax.optimization_barrier((metas, question))
    sends, _ = pick(rest, False, own, asked, later, memory)
    question, *held = lax.optimization_barrier((question, *sends.values()))
    for k, x in zip(rest, held):
        mine[k] = exchange(x, k)
    encoded = None
    shape = (1, wants, q_tokens + p_tokens, half)
    waiting = None
    for i, ks in enumerate(chunks):
        if waiting is not None:
            rows = [mine[k] for k in come[i]]
            *rows, ours, other = lax.optimization_barrier((*rows, *waiting[2:]))
            mine.update(zip(come[i], rows))
        rows = [mine[k] for k in ks]
        theirs = [swap(x) for x in rows]
        if waiting is not None:
            encoded = combine(
                waiting[0], encoded, shape, own, table, questions, waiting[1], ours, swap(other)
            )
            theirs[0], encoded = lax.optimization_barrier((theirs[0], encoded))
        made = layer(
            ks, own, table, question, gain, rows, theirs, w_query, w_key, w_value, w_out
        )
        waiting = (ks, rows, *made)
    ks, rows, ours, other = waiting
    encoded = combine(ks, encoded, shape, own, table, questions, rows, ours, swap(other))
    return encoded


def solution(mesh):
    in_specs = (
        P(("groups", "mem"), None, "tp"),
        P("mem", None, "tp"),
        P(("groups", "mem"), None),
        P(("groups", "mem")),
        P("mem"),
        P(),
        P(None, "tp"),
        P(None, "tp"),
        P(None, "tp"),
        P("tp", None),
    )
    out_specs = P(("groups", "mem"), None, None, "tp")
    return jax.shard_map(body, mesh=mesh, in_specs=in_specs, out_specs=out_specs, check_vma=False)
```

```python
import functools

import jax
import jax.numpy as jnp
from jax import lax
from jax.experimental import pallas as pl
from jax.experimental.pallas import tpu as pltpu
from jax.sharding import PartitionSpec as P

HS = 64
CAPM = 2
EPS = 1e-06
MASKED = -1e30
LANES = 128
PACK = 16
VMEM_ALL = 60 * 1024 * 1024
VMEM_LAYER = 48 * 1024 * 1024

ANY = pl.BlockSpec(memory_space=pl.ANY)
HBM = pl.BlockSpec(memory_space=pltpu.HBM)
SMEM = pl.BlockSpec(memory_space=pltpu.SMEM)
VMEM = pl.BlockSpec(memory_space=pltpu.VMEM)
LITTLE = pl.CostEstimate(flops=1, bytes_accessed=1, transcendentals=0)


def ask_kernel(pass_dev, wants, position, retrieved, p_len, q_len, metas, own_ref):
    shards = metas.shape[0]
    own_ref[0, 0] = position[0]
    own_ref[0, 1] = position[1]
    own_ref[0, 2] = q_len[0]
    for shard in range(shards):
        for r in range(CAPM):
            metas[shard, 0, r] = jnp.int32(-1)
            own_ref[1, CAPM * shard + r] = jnp.int32(-1)
        for i in range(pass_dev):
            metas[shard, 0, CAPM + i] = p_len[i]

    def place(j, carry):
        wanted = retrieved[0, j]
        shard = lax.div(wanted, pass_dev)
        taken = (metas[shard, 0, 0] >= 0).astype(jnp.int32)
        metas[shard, 0, taken] = wanted - shard * pass_dev
        own_ref[1, CAPM * shard + taken] = j
        return carry

    lax.fori_loop(0, wants, place, 0)


def ask(retrieved, p_len, q_len, shards):
    position = jnp.stack([lax.axis_index("tp"), lax.axis_index("mem")]).astype(jnp.int32)
    return pl.pallas_call(
        functools.partial(ask_kernel, p_len.shape[0], retrieved.shape[1]),
        out_shape=[
            jax.ShapeDtypeStruct((shards, 1, LANES), jnp.int32),
            jax.ShapeDtypeStruct((2, LANES), jnp.int32),
        ],
        in_specs=[SMEM] * 4,
        out_specs=[SMEM] * 2,
        cost_estimate=LITTLE,
        name="ask",
    )(position, retrieved, p_len, q_len)


def pick_kernel(ks, own_ref, asked, metas, memory, *refs):
    n = len(ks)
    outs = refs[:n]
    table = refs[n] if len(refs) > n + 2 else None
    staged, sems = refs[-2:]
    shards = metas.shape[0]
    me = own_ref[0, 1]
    found = []
    for i, k in enumerate(ks):
        partner = lax.bitwise_xor(me, k)
        for r in range(CAPM):
            local = metas[partner, 0, r]
            found.append(
                (
                    local,
                    pltpu.make_async_copy(
                        memory.at[jnp.maximum(local, 0)], staged.at[i, r], sems.at[0, i, r]
                    ),
                    pltpu.make_async_copy(staged.at[i, r], outs[i].at[r], sems.at[1, i, r]),
                )
            )

            @pl.when(local >= 0)
            def _():
                found[-1][1].start()

    if table is not None:
        for k in range(shards):
            partner = lax.bitwise_xor(me, k)
            for r in range(CAPM):
                pair = own_ref[1, CAPM * partner + r]
                local = jnp.maximum(asked[partner, 0, r], 0)
                table[0, CAPM * k + r] = pair
                table[1, CAPM * k + r] = jnp.where(
                    pair >= 0, metas[partner, 0, CAPM + local], 0
                )
    for local, come, go in found:

        @pl.when(local >= 0)
        def _():
            come.wait()
            go.start()

    for local, _, go in found:

        @pl.when(local >= 0)
        def _():
            go.wait()


def pick(ks, with_table, own, asked, metas, memory):
    n = len(ks)
    _, p_tokens, half = memory.shape
    slot = jax.ShapeDtypeStruct((CAPM, p_tokens, half), memory.dtype)
    result = pl.pallas_call(
        functools.partial(pick_kernel, ks),
        out_shape=[slot] * n + [jax.ShapeDtypeStruct((2, LANES), jnp.int32)] * with_table,
        in_specs=[SMEM, SMEM, SMEM, HBM],
        out_specs=[ANY] * n + [SMEM] * with_table,
        scratch_shapes=[
            pltpu.VMEM((n, CAPM, p_tokens, half), memory.dtype),
            pltpu.SemaphoreType.DMA((2, n, CAPM)),
        ],
        compiler_params=pltpu.CompilerParams(vmem_limit_bytes=VMEM_ALL),
        cost_estimate=LITTLE,
        name="pick",
    )(own, asked, metas, memory)
    return dict(zip(ks, result)), result[n:]


def normed_halves(own, other, gain_own, gain_other):
    own = own.astype(jnp.float32)
    other = other.astype(jnp.float32)
    total = jnp.sum(own * own + other * other, axis=-1, keepdims=True)
    scale = lax.rsqrt(total / (2 * own.shape[-1]) + EPS)
    return (
        (own * scale * gain_own).astype(jnp.bfloat16),
        (other * scale * gain_other).astype(jnp.bfloat16),
    )


def weight_copies(c, half, sources, targets, sems):
    copies = []
    for i, (source, target) in enumerate(zip(sources, targets)):
        pieces = []
        for part, core in enumerate((c, 1 - c)):
            start = pl.multiple_of(core * half, half)
            pieces.append(
                pltpu.make_async_copy(
                    source.at[pl.ds(start, half), :],
                    target.at[pl.ds(part * half, half), :],
                    sems.at[i, part],
                )
            )
        copies.append(pieces)
    return copies


def question_kernel(own_ref, mine, theirs, gain, wq, wk, wv, out, vq, vk, vv, sems):
    c = own_ref[0, 0]
    half = mine.shape[-1]
    copies = weight_copies(c, half, (wq, wk, wv), (vq, vk, vv), sems)
    for pieces in copies:
        for piece in pieces:
            piece.start()
    g_own = gain[c].astype(jnp.float32)
    g_other = gain[1 - c].astype(jnp.float32)
    first, second = normed_halves(mine[0], theirs[0], g_own, g_other)
    rows = jnp.concatenate([first, second], axis=1)
    for i, weight in enumerate((vq, vk, vv)):
        for piece in copies[i]:
            piece.wait()
        made = jnp.dot(rows, weight[...], preferred_element_type=jnp.float32)
        made = made.astype(jnp.bfloat16)
        if i == 0:
            made = made * jnp.bfloat16(1.0 / 8.0)
        out[i] = made


def project_question(own, mine, theirs, gain, wq, wk, wv):
    _, q_tokens, half = mine.shape
    width, cols = wq.shape
    weight = pltpu.VMEM((width, cols), jnp.bfloat16)
    return pl.pallas_call(
        question_kernel,
        out_shape=jax.ShapeDtypeStruct((3, q_tokens, cols), jnp.bfloat16),
        in_specs=[SMEM, VMEM, VMEM, VMEM, HBM, HBM, HBM],
        out_specs=VMEM,
        scratch_shapes=[weight] * 3 + [pltpu.SemaphoreType.DMA((3, 2))],
        compiler_params=pltpu.CompilerParams(vmem_limit_bytes=VMEM_ALL),
        cost_estimate=LITTLE,
        name="question_projections",
    )(own, mine, theirs, gain, wq, wk, wv)


def place_of(ks, s):
    return CAPM * ks[s // CAPM] + s % CAPM


def compact(table, ks, q_tokens):
    places = []
    start = jnp.int32(0)
    start_out = jnp.int32(0)
    for s in range(CAPM * len(ks)):
        p_len = table[1, place_of(ks, s)]
        room = lax.bitwise_and(p_len + (PACK - 1), ~(PACK - 1))
        places.append((p_len, pl.multiple_of(start, PACK), pl.multiple_of(start_out, PACK)))
        start = start + room
        start_out = start_out + jnp.where(p_len > 0, room + q_tokens, 0)
    return places, start_out


def pick_span(p_len, spans):
    span = jnp.int32(spans[-1][1])
    for queries, keys in reversed(spans[:-1]):
        span = jnp.where(p_len <= queries, keys, span)
    return span


def for_rows(needed, counts, run):
    least = 0
    for count in counts:

        @pl.when(jnp.logical_and(needed > least, needed <= count))
        def _():
            run(count)

        least = count


def layer_kernel(ks, own_ref, table, question, gain, *refs):
    n = len(ks)
    mine, theirs = refs[:n], refs[n : 2 * n]
    wq, wk, wv, wo = refs[2 * n : 2 * n + 4]
    out_own, out_other = refs[2 * n + 4 : 2 * n + 6]
    vq, vk, vv, vo, rows, query, key, value, attended, raw, made_out, listed = refs[
        2 * n + 6 : -4
    ]
    sems, sems_out, sems_rows, sems_made = refs[-4:]
    cols = query.shape[1]
    q_tokens = question.shape[1]
    _, p_tokens, half = mine[0].shape
    slots = CAPM * n
    total = q_tokens + p_tokens
    spans = ((3 * p_tokens // 4, 3 * p_tokens // 4), (p_tokens, p_tokens))
    c = own_ref[0, 0]
    q_len = own_ref[0, 2]
    copies = weight_copies(c, half, (wq, wk, wv), (vq, vk, vv), sems)
    out_copies = []
    for part, core in enumerate((1 - c, c)):
        start = pl.multiple_of(core * half, half)
        out_copies.append(
            pltpu.make_async_copy(wo.at[:, pl.ds(start, half)], vo.at[part], sems_out.at[part])
        )
    row_copies = []
    for part, sources in enumerate((mine, theirs)):
        for i, source in enumerate(sources):
            row_copies.append(
                pltpu.make_async_copy(source, raw.at[part, i], sems_rows.at[part, i])
            )
    for pieces in [row_copies] + copies + [out_copies]:
        for piece in pieces:
            piece.start()
    places, used_out = compact(table, ks, q_tokens)
    used = jnp.int32(0)
    valid = jnp.int32(0)
    for p_len, start, start_out in places:
        used = jnp.where(p_len > 0, jnp.maximum(used, start + pick_span(p_len, spans)), used)
        listed[0, valid] = p_len
        listed[1, valid] = start
        listed[2, valid] = start_out
        valid = valid + (p_len > 0).astype(jnp.int32)
    g_own = gain[c].astype(jnp.float32)
    g_other = gain[1 - c].astype(jnp.float32)
    for piece in row_copies:
        piece.wait()
    for s, (p_len, start, _) in enumerate(places):

        @pl.when(p_len > 0)
        def _():
            first, second = normed_halves(
                raw[0, s // CAPM, s % CAPM], raw[1, s // CAPM, s % CAPM], g_own, g_other
            )
            rows[pl.ds(start, p_tokens), :half] = first
            rows[pl.ds(start, p_tokens), half:] = second

    def project(count):
        for i, (weight, target) in enumerate(((vq, query), (vk, key), (vv, value))):
            for piece in copies[i]:
                piece.wait()
            for left in range(0, cols, 256):
                span = slice(left, left + 256)
                made = jnp.dot(
                    rows[:count], weight[:, span], preferred_element_type=jnp.float32
                ).astype(jnp.bfloat16)
                if i == 0:
                    made = made * jnp.bfloat16(1.0 / 8.0)
                target[:count, span] = made

    most = slots * p_tokens
    for_rows(used, [c for c in (128, 256, 384) if c < most and c > most // 4] + [most], project)

    @pl.when(used == 0)
    def _():
        for pieces in copies:
            for piece in pieces:
                piece.wait()

    lane = lax.broadcasted_iota(jnp.int32, (1, 2 * HS), 1)
    in_first = lane < HS

    def attend(p_len, start, start_out, queries, keys):
        both = q_tokens + queries
        room = -(-(q_tokens + keys) // LANES) * LANES
        spot = lax.broadcasted_iota(jnp.int32, (1, room), 1)
        end = jnp.where(spot < q_tokens, q_len, q_tokens + p_len)
        bias = jnp.where(spot < end, 0.0, MASKED)
        bias = jnp.concatenate([bias, bias], axis=1)
        one = jnp.ones((room, 2 * HS), jnp.bfloat16)

        def pair_rows(i, source, count, span):
            return jnp.concatenate(
                [question[i, :, span], source[pl.ds(start, count), span]], axis=0
            )

        def key_rows(i, source, span):
            found = pair_rows(i, source, keys, span)
            if room > found.shape[0]:
                fill = jnp.zeros((room - found.shape[0], 2 * HS), jnp.bfloat16)
                found = jnp.concatenate([found, fill], axis=0)
            return found

        def by_head(x):
            zero = jnp.zeros_like(x)
            return jnp.concatenate(
                [jnp.where(in_first, x, zero), jnp.where(in_first, zero, x)], axis=0
            )

        spans_here = [slice(left, left + 2 * HS) for left in range(0, cols, 2 * HS)]
        scores = [
            lax.dot_general(
                pair_rows(0, query, queries, span),
                by_head(key_rows(1, key, span)),
                (((1,), (1,)), ((), ())),
                preferred_element_type=jnp.float32,
            )
            + bias
            for span in spans_here
        ]
        raised = []
        for x in scores:
            halves = (x[:, :room], x[:, room:])
            raised.append(
                jnp.concatenate(
                    [
                        jnp.exp(y - jnp.max(y, axis=1, keepdims=True)).astype(jnp.bfloat16)
                        for y in halves
                    ],
                    axis=1,
                )
            )
        ones = by_head(one)
        with_sums = [
            jnp.dot(
                x,
                jnp.concatenate([by_head(key_rows(2, value, span)), ones], axis=1),
                preferred_element_type=jnp.float32,
            )
            for x, span in zip(raised, spans_here)
        ]
        for x, span in zip(with_sums, spans_here):
            attended[pl.ds(start_out, both), span] = (
                x[:, : 2 * HS] / x[:, 2 * HS :]
            ).astype(jnp.bfloat16)

    def attend_next(t, carry):
        p_len = listed[0, t]
        start = pl.multiple_of(listed[1, t], PACK)
        start_out = pl.multiple_of(listed[2, t], PACK)
        least = 0
        for queries, keys in spans:

            @pl.when(jnp.logical_and(p_len > least, p_len <= queries))
            def _():
                attend(p_len, start, start_out, queries, keys)

            least = queries
        return carry

    lax.fori_loop(0, valid, attend_next, 0)

    def put_out(count):
        for part, out in enumerate((out_other, out_own)):
            out_copies[part].wait()
            for left in range(0, half, 256):
                span = slice(left, left + 256)
                made_out[part, :count, span] = jnp.dot(
                    attended[:count], vo[part, :, span], preferred_element_type=jnp.float32
                ).astype(jnp.bfloat16)
            pltpu.make_async_copy(made_out.at[part], out, sems_made.at[part]).start()
        for part, out in enumerate((out_other, out_own)):
            pltpu.make_async_copy(made_out.at[part], out, sems_made.at[part]).wait()

    most = slots * total
    for_rows(
        used_out, [c for c in (192, 256, 384, 512) if c < most and c > most // 3] + [most], put_out
    )

    @pl.when(used_out == 0)
    def _():
        for piece in out_copies:
            piece.wait()


def layer(ks, own, table, question, gain, mine, theirs, wq, wk, wv, wo):
    _, p_tokens, half = mine[0].shape
    _, q_tokens, cols = question.shape
    width = wq.shape[0]
    slots = CAPM * len(ks)
    total = q_tokens + p_tokens
    weight = pltpu.VMEM((width, cols), jnp.bfloat16)
    packed = pltpu.VMEM((slots * p_tokens, cols), jnp.bfloat16)
    out = jax.ShapeDtypeStruct((slots * total, half), jnp.bfloat16)
    return pl.pallas_call(
        functools.partial(layer_kernel, ks),
        out_shape=[out, out],
        in_specs=[SMEM, SMEM, VMEM, VMEM] + [ANY] * (2 * len(ks)) + [HBM] * 4,
        out_specs=[ANY, ANY],
        scratch_shapes=[weight] * 3
        + [
            pltpu.VMEM((2, cols, half), jnp.bfloat16),
            pltpu.VMEM((slots * p_tokens, width), jnp.bfloat16),
            packed,
            packed,
            packed,
            pltpu.VMEM((slots * total, cols), jnp.bfloat16),
            pltpu.VMEM((2, len(ks), CAPM, p_tokens, half), jnp.bfloat16),
            pltpu.VMEM((2, slots * total, half), jnp.bfloat16),
            pltpu.SMEM((3, slots + 1), jnp.int32),
            pltpu.SemaphoreType.DMA((3, 2)),
            pltpu.SemaphoreType.DMA((2,)),
            pltpu.SemaphoreType.DMA((2, len(ks))),
            pltpu.SemaphoreType.DMA((2,)),
        ],
        compiler_params=pltpu.CompilerParams(vmem_limit_bytes=VMEM_LAYER),
        cost_estimate=LITTLE,
        name="layer",
    )(own, table, question, gain, *mine, *theirs, wq, wk, wv, wo)


def combine_kernel(ks, first, own_ref, table, questions, *refs):
    n = len(ks)
    mine = refs[:n]
    ours, arrived = refs[n : n + 2]
    encoded, staged, sems = refs[n + 2 if first else n + 3 :]
    slots, total, _ = staged.shape
    q_tokens = questions.shape[1]
    q_len = own_ref[0, 2]
    places, _ = compact(table, ks, q_tokens)

    def copy(s, pair):
        return pltpu.make_async_copy(staged.at[s], encoded.at[0, pair], sems.at[s])

    for s, (p_len, _, start) in enumerate(places):
        pair = table[0, place_of(ks, s)]

        @pl.when(pair >= 0)
        def _():
            for rows, low, length in (
                (questions[0], 0, q_len),
                (mine[s // CAPM][s % CAPM], q_tokens, p_len),
            ):
                count = rows.shape[0]
                spot = lax.broadcasted_iota(jnp.int32, (count, 1), 0)
                at = pl.ds(pl.multiple_of(start + low, PACK), count)
                branch = ours[at].astype(jnp.float32) + arrived[at].astype(jnp.float32)
                made = rows.astype(jnp.float32) + branch
                staged[s, low : low + count] = jnp.where(spot < length, made, 0.0).astype(
                    jnp.bfloat16
                )
            copy(s, pair).start()

    for s in range(slots):

        @pl.when(table[0, place_of(ks, s)] >= 0)
        def _():
            copy(s, 0).wait()


def combine(ks, encoded, shape, own, table, questions, mine, ours, arrived):
    first = encoded is None
    slots = CAPM * len(ks)
    operands = [own, table, questions, *mine, ours, arrived] + ([] if first else [encoded])
    return pl.pallas_call(
        functools.partial(combine_kernel, ks, first),
        out_shape=jax.ShapeDtypeStruct(shape, jnp.bfloat16),
        in_specs=[SMEM, SMEM, VMEM] + [VMEM] * (len(ks) + 2) + ([] if first else [ANY]),
        out_specs=ANY,
        scratch_shapes=[
            pltpu.VMEM((slots, *shape[2:]), jnp.bfloat16),
            pltpu.SemaphoreType.DMA((slots,)),
        ],
        input_output_aliases={} if first else {len(operands) - 1: 0},
        compiler_params=pltpu.CompilerParams(vmem_limit_bytes=VMEM_LAYER),
        cost_estimate=LITTLE,
        name="combine",
    )(*operands)


def body(questions, memory, retrieved, q_len, p_len, norm_gain, w_query, w_key, w_value, w_out):
    shards = lax.axis_size("mem")
    cores = lax.axis_size("tp")
    _, q_tokens, half = questions.shape
    p_tokens = memory.shape[1]
    wants = retrieved.shape[1]

    def swap(x):
        return lax.ppermute(x, "tp", [(i, (i + 1) % cores) for i in range(cores)])

    def exchange(x, k):
        return lax.ppermute(x, "mem", [(i, i ^ k) for i in range(shards)])

    asked, own = ask(retrieved, p_len, q_len, shards)
    metas = lax.all_to_all(asked, "mem", 0, 0, tiled=True)
    gain = norm_gain.reshape(cores, 1, half)
    question = project_question(
        own, questions, swap(questions), gain, w_query, w_key, w_value
    )
    near = shards // 2
    chunks = [(0,)] + [(k, near - 1 + k) for k in range(1, near)] + [(shards - 1,)]
    come = [(0,), (1, 2, near)] + [
        (k, near - 2 + k) if k < near else (near - 2 + k,) for k in range(3, near + 2)
    ]
    first = (0, 1, 2, near)
    rest = tuple(k for k in range(shards) if k not in first)
    sends, (table,) = pick(first, True, own, asked, metas, memory)
    mine = {0: sends[0]}
    for k in first[1:]:
        mine[k] = exchange(sends[k], k)
    later, question = lax.optimization_barrier((metas, question))
    sends, _ = pick(rest, False, own, asked, later, memory)
    question, *held = lax.optimization_barrier((question, *sends.values()))
    for k, x in zip(rest, held):
        mine[k] = exchange(x, k)
    encoded = None
    shape = (1, wants, q_tokens + p_tokens, half)
    waiting = None
    for i, ks in enumerate(chunks):
        if waiting is not None:
            rows = [mine[k] for k in come[i]]
            *rows, ours, other = lax.optimization_barrier((*rows, *waiting[2:]))
            mine.update(zip(come[i], rows))
        rows = [mine[k] for k in ks]
        theirs = [swap(x) for x in rows]
        if waiting is not None:
            encoded = combine(
                waiting[0], encoded, shape, own, table, questions, waiting[1], ours, swap(other)
            )
            theirs[0], encoded = lax.optimization_barrier((theirs[0], encoded))
        made = layer(
            ks, own, table, question, gain, rows, theirs, w_query, w_key, w_value, w_out
        )
        waiting = (ks, rows, *made)
    ks, rows, ours, other = waiting
    encoded = combine(ks, encoded, shape, own, table, questions, rows, ours, swap(other))
    return encoded


def solution(mesh):
    in_specs = (
        P(("groups", "mem"), None, "tp"),
        P("mem", None, "tp"),
        P(("groups", "mem"), None),
        P(("groups", "mem")),
        P("mem"),
        P(),
        P(None, "tp"),
        P(None, "tp"),
        P(None, "tp"),
        P("tp", None),
    )
    out_specs = P(("groups", "mem"), None, None, "tp")
    return jax.shard_map(body, mesh=mesh, in_specs=in_specs, out_specs=out_specs, check_vma=False)
```

```python
import functools

import jax
import jax.numpy as jnp
from jax import lax
from jax.experimental import pallas as pl
from jax.experimental.pallas import tpu as pltpu
from jax.sharding import PartitionSpec as P

HS = 64
CAPM = 2
EPS = 1e-06
MASKED = -1e30
LANES = 128
PACK = 16
VMEM_ALL = 60 * 1024 * 1024
VMEM_LAYER = 30 * 1024 * 1024
VMEM_SLOT = 5 * 512 * 1024

ANY = pl.BlockSpec(memory_space=pl.ANY)
HBM = pl.BlockSpec(memory_space=pltpu.HBM)
SMEM = pl.BlockSpec(memory_space=pltpu.SMEM)
VMEM = pl.BlockSpec(memory_space=pltpu.VMEM)
LITTLE = pl.CostEstimate(flops=1, bytes_accessed=1, transcendentals=0)


def ask_kernel(pass_dev, wants, position, retrieved, p_len, q_len, metas, own_ref):
    shards = metas.shape[0]
    own_ref[0, 0] = position[0]
    own_ref[0, 1] = position[1]
    own_ref[0, 2] = q_len[0]
    for shard in range(shards):
        for r in range(CAPM):
            metas[shard, 0, r] = jnp.int32(-1)
            own_ref[1, CAPM * shard + r] = jnp.int32(-1)
        for i in range(pass_dev):
            metas[shard, 0, CAPM + i] = p_len[i]

    def place(j, carry):
        wanted = retrieved[0, j]
        shard = lax.div(wanted, pass_dev)
        taken = (metas[shard, 0, 0] >= 0).astype(jnp.int32)
        metas[shard, 0, taken] = wanted - shard * pass_dev
        own_ref[1, CAPM * shard + taken] = j
        return carry

    lax.fori_loop(0, wants, place, 0)


def ask(retrieved, p_len, q_len, shards):
    position = jnp.stack([lax.axis_index("tp"), lax.axis_index("mem")]).astype(jnp.int32)
    return pl.pallas_call(
        functools.partial(ask_kernel, p_len.shape[0], retrieved.shape[1]),
        out_shape=[
            jax.ShapeDtypeStruct((shards, 1, LANES), jnp.int32),
            jax.ShapeDtypeStruct((2, LANES), jnp.int32),
        ],
        in_specs=[SMEM] * 4,
        out_specs=[SMEM] * 2,
        cost_estimate=LITTLE,
        name="ask",
    )(position, retrieved, p_len, q_len)


def pick_kernel(ks, own_ref, asked, metas, memory, *refs):
    n = len(ks)
    outs = refs[:n]
    table = refs[n] if len(refs) > n + 2 else None
    staged, sems = refs[-2:]
    shards = metas.shape[0]
    me = own_ref[0, 1]
    found = []
    for i, k in enumerate(ks):
        partner = lax.bitwise_xor(me, k)
        for r in range(CAPM):
            local = metas[partner, 0, r]
            found.append(
                (
                    local,
                    pltpu.make_async_copy(
                        memory.at[jnp.maximum(local, 0)], staged.at[i, r], sems.at[0, i, r]
                    ),
                    pltpu.make_async_copy(staged.at[i, r], outs[i].at[r], sems.at[1, i, r]),
                )
            )

            @pl.when(local >= 0)
            def _():
                found[-1][1].start()

    if table is not None:
        for k in range(shards):
            partner = lax.bitwise_xor(me, k)
            for r in range(CAPM):
                pair = own_ref[1, CAPM * partner + r]
                local = jnp.maximum(asked[partner, 0, r], 0)
                table[0, CAPM * k + r] = pair
                table[1, CAPM * k + r] = jnp.where(
                    pair >= 0, metas[partner, 0, CAPM + local], 0
                )
    for local, come, go in found:

        @pl.when(local >= 0)
        def _():
            come.wait()
            go.start()

    for local, _, go in found:

        @pl.when(local >= 0)
        def _():
            go.wait()


def pick(ks, with_table, own, asked, metas, memory):
    n = len(ks)
    _, p_tokens, half = memory.shape
    slot = jax.ShapeDtypeStruct((CAPM, p_tokens, half), memory.dtype)
    result = pl.pallas_call(
        functools.partial(pick_kernel, ks),
        out_shape=[slot] * n + [jax.ShapeDtypeStruct((2, LANES), jnp.int32)] * with_table,
        in_specs=[SMEM, SMEM, SMEM, HBM],
        out_specs=[ANY] * n + [SMEM] * with_table,
        scratch_shapes=[
            pltpu.VMEM((n, CAPM, p_tokens, half), memory.dtype),
            pltpu.SemaphoreType.DMA((2, n, CAPM)),
        ],
        compiler_params=pltpu.CompilerParams(vmem_limit_bytes=VMEM_ALL),
        cost_estimate=LITTLE,
        name="pick",
    )(own, asked, metas, memory)
    return dict(zip(ks, result)), result[n:]


def normed_halves(own, other, gain_own, gain_other):
    own = own.astype(jnp.float32)
    other = other.astype(jnp.float32)
    total = jnp.sum(own * own + other * other, axis=-1, keepdims=True)
    scale = lax.rsqrt(total / (2 * own.shape[-1]) + EPS)
    return (
        (own * scale * gain_own).astype(jnp.bfloat16),
        (other * scale * gain_other).astype(jnp.bfloat16),
    )


def weight_copies(c, half, sources, targets, sems):
    copies = []
    for i, (source, target) in enumerate(zip(sources, targets)):
        pieces = []
        for part, core in enumerate((c, 1 - c)):
            start = pl.multiple_of(core * half, half)
            pieces.append(
                pltpu.make_async_copy(
                    source.at[pl.ds(start, half), :],
                    target.at[pl.ds(part * half, half), :],
                    sems.at[i, part],
                )
            )
        copies.append(pieces)
    return copies


def question_kernel(own_ref, mine, theirs, gain, wq, wk, wv, out, vq, vk, vv, sems):
    c = own_ref[0, 0]
    half = mine.shape[-1]
    copies = weight_copies(c, half, (wq, wk, wv), (vq, vk, vv), sems)
    for piece in copies[0]:
        piece.start()
    g_own = gain[c].astype(jnp.float32)
    g_other = gain[1 - c].astype(jnp.float32)
    first, second = normed_halves(mine[0], theirs[0], g_own, g_other)
    rows = jnp.concatenate([first, second], axis=1)
    for i, weight in enumerate((vq, vk, vv)):
        for piece in copies[i + 1] if i < 2 else ():
            piece.start()
        for piece in copies[i]:
            piece.wait()
        made = jnp.dot(rows, weight[...], preferred_element_type=jnp.float32)
        made = made.astype(jnp.bfloat16)
        if i == 0:
            made = made * jnp.bfloat16(1.0 / 8.0)
        out[i] = made


def project_question(own, mine, theirs, gain, wq, wk, wv):
    _, q_tokens, half = mine.shape
    width, cols = wq.shape
    weight = pltpu.VMEM((width, cols), jnp.bfloat16)
    return pl.pallas_call(
        question_kernel,
        out_shape=jax.ShapeDtypeStruct((3, q_tokens, cols), jnp.bfloat16),
        in_specs=[SMEM, VMEM, VMEM, VMEM, HBM, HBM, HBM],
        out_specs=VMEM,
        scratch_shapes=[weight] * 3 + [pltpu.SemaphoreType.DMA((3, 2))],
        compiler_params=pltpu.CompilerParams(vmem_limit_bytes=VMEM_ALL),
        cost_estimate=LITTLE,
        name="question_projections",
    )(own, mine, theirs, gain, wq, wk, wv)


def place_of(ks, s):
    return CAPM * ks[s // CAPM] + s % CAPM


def compact(table, ks, q_tokens):
    places = []
    start = jnp.int32(0)
    start_out = jnp.int32(0)
    for s in range(CAPM * len(ks)):
        p_len = table[1, place_of(ks, s)]
        room = lax.bitwise_and(p_len + (PACK - 1), ~(PACK - 1))
        places.append((p_len, pl.multiple_of(start, PACK), pl.multiple_of(start_out, PACK)))
        start = start + room
        start_out = start_out + jnp.where(p_len > 0, room + q_tokens, 0)
    return places, start_out


def pick_span(p_len, spans):
    span = jnp.int32(spans[-1][1])
    for queries, keys in reversed(spans[:-1]):
        span = jnp.where(p_len <= queries, keys, span)
    return span


def for_rows(needed, counts, run):
    least = 0
    for count in counts:

        @pl.when(jnp.logical_and(needed > least, needed <= count))
        def _():
            run(count)

        least = count


def layer_kernel(ks, own_ref, table, question, gain, *refs):
    n = len(ks)
    mine, theirs = refs[:n], refs[n : 2 * n]
    wq, wk, wv, wo = refs[2 * n : 2 * n + 4]
    out_own, out_other = refs[2 * n + 4 : 2 * n + 6]
    vq, vk, vv, vo, rows, query, key, value, attended, raw, made_out, listed = refs[
        2 * n + 6 : -4
    ]
    sems, sems_out, sems_rows, sems_made = refs[-4:]
    cols = query.shape[1]
    q_tokens = question.shape[1]
    _, p_tokens, half = mine[0].shape
    slots = CAPM * n
    total = q_tokens + p_tokens
    spans = ((3 * p_tokens // 4, 3 * p_tokens // 4), (p_tokens, p_tokens))
    c = own_ref[0, 0]
    q_len = own_ref[0, 2]
    copies = weight_copies(c, half, (wq, wk, wv), (vq, vk, vv), sems)
    out_copies = []
    for part, core in enumerate((1 - c, c)):
        start = pl.multiple_of(core * half, half)
        out_copies.append(
            pltpu.make_async_copy(wo.at[:, pl.ds(start, half)], vo.at[part], sems_out.at[part])
        )
    row_copies = []
    for part, sources in enumerate((mine, theirs)):
        for i, source in enumerate(sources):
            row_copies.append(
                pltpu.make_async_copy(source, raw.at[part, i], sems_rows.at[part, i])
            )
    def launch(pieces):
        for piece in pieces:
            piece.start()

    launch(row_copies)
    launch(copies[0])
    places, used_out = compact(table, ks, q_tokens)
    used = jnp.int32(0)
    valid = jnp.int32(0)
    for p_len, start, start_out in places:
        used = jnp.where(p_len > 0, jnp.maximum(used, start + pick_span(p_len, spans)), used)
        listed[0, valid] = p_len
        listed[1, valid] = start
        listed[2, valid] = start_out
        valid = valid + (p_len > 0).astype(jnp.int32)
    g_own = gain[c].astype(jnp.float32)
    g_other = gain[1 - c].astype(jnp.float32)
    for piece in row_copies:
        piece.wait()
    for s, (p_len, start, _) in enumerate(places):

        @pl.when(p_len > 0)
        def _():
            first, second = normed_halves(
                raw[0, s // CAPM, s % CAPM], raw[1, s // CAPM, s % CAPM], g_own, g_other
            )
            rows[pl.ds(start, p_tokens), :half] = first
            rows[pl.ds(start, p_tokens), half:] = second

    def project(count):
        for i, (weight, target) in enumerate(((vq, query), (vk, key), (vv, value))):
            launch(copies[i + 1] if i < 2 else out_copies[:1])
            for piece in copies[i]:
                piece.wait()
            for left in range(0, cols, 256):
                span = slice(left, left + 256)
                made = jnp.dot(
                    rows[:count], weight[:, span], preferred_element_type=jnp.float32
                ).astype(jnp.bfloat16)
                if i == 0:
                    made = made * jnp.bfloat16(1.0 / 8.0)
                target[:count, span] = made
        launch(out_copies[1:])

    most = slots * p_tokens
    for_rows(
        used, [c for c in (128, 256, 384, 512, 640, 768) if most // 3 < c < most] + [most], project
    )

    @pl.when(used == 0)
    def _():
        for piece in copies[0]:
            piece.wait()

    lane = lax.broadcasted_iota(jnp.int32, (1, 2 * HS), 1)
    in_first = lane < HS

    def attend(p_len, start, start_out, queries, keys):
        both = q_tokens + queries
        room = -(-(q_tokens + keys) // LANES) * LANES
        spot = lax.broadcasted_iota(jnp.int32, (1, room), 1)
        end = jnp.where(spot < q_tokens, q_len, q_tokens + p_len)
        bias = jnp.where(spot < end, 0.0, MASKED)
        bias = jnp.concatenate([bias, bias], axis=1)
        one = jnp.ones((room, 2 * HS), jnp.bfloat16)

        def pair_rows(i, source, count, span):
            return jnp.concatenate(
                [question[i, :, span], source[pl.ds(start, count), span]], axis=0
            )

        def key_rows(i, source, span):
            found = pair_rows(i, source, keys, span)
            if room > found.shape[0]:
                fill = jnp.zeros((room - found.shape[0], 2 * HS), jnp.bfloat16)
                found = jnp.concatenate([found, fill], axis=0)
            return found

        def by_head(x):
            zero = jnp.zeros_like(x)
            return jnp.concatenate(
                [jnp.where(in_first, x, zero), jnp.where(in_first, zero, x)], axis=0
            )

        spans_here = [slice(left, left + 2 * HS) for left in range(0, cols, 2 * HS)]
        scores = [
            lax.dot_general(
                pair_rows(0, query, queries, span),
                by_head(key_rows(1, key, span)),
                (((1,), (1,)), ((), ())),
                preferred_element_type=jnp.float32,
            )
            + bias
            for span in spans_here
        ]
        raised = []
        for x in scores:
            halves = (x[:, :room], x[:, room:])
            raised.append(
                jnp.concatenate(
                    [
                        jnp.exp(y - jnp.max(y, axis=1, keepdims=True)).astype(jnp.bfloat16)
                        for y in halves
                    ],
                    axis=1,
                )
            )
        ones = by_head(one)
        with_sums = [
            jnp.dot(
                x,
                jnp.concatenate([by_head(key_rows(2, value, span)), ones], axis=1),
                preferred_element_type=jnp.float32,
            )
            for x, span in zip(raised, spans_here)
        ]
        for x, span in zip(with_sums, spans_here):
            attended[pl.ds(start_out, both), span] = (
                x[:, : 2 * HS] / x[:, 2 * HS :]
            ).astype(jnp.bfloat16)

    def attend_next(t, carry):
        p_len = listed[0, t]
        start = pl.multiple_of(listed[1, t], PACK)
        start_out = pl.multiple_of(listed[2, t], PACK)
        least = 0
        for queries, keys in spans:

            @pl.when(jnp.logical_and(p_len > least, p_len <= queries))
            def _():
                attend(p_len, start, start_out, queries, keys)

            least = queries
        return carry

    lax.fori_loop(0, valid, attend_next, 0)

    def put_out(count):
        for part, out in enumerate((out_other, out_own)):
            out_copies[part].wait()
            for left in range(0, half, 256):
                span = slice(left, left + 256)
                made_out[part, :count, span] = jnp.dot(
                    attended[:count], vo[part, :, span], preferred_element_type=jnp.float32
                ).astype(jnp.bfloat16)
            pltpu.make_async_copy(made_out.at[part], out, sems_made.at[part]).start()
        for part, out in enumerate((out_other, out_own)):
            pltpu.make_async_copy(made_out.at[part], out, sems_made.at[part]).wait()

    most = slots * total
    counts = (128, 192, 256, 384, 512, 640, 768, 896)
    for_rows(used_out, [c for c in counts if 3 * most // 8 < c < most] + [most], put_out)


def layer(ks, own, table, question, gain, mine, theirs, wq, wk, wv, wo):
    _, p_tokens, half = mine[0].shape
    _, q_tokens, cols = question.shape
    width = wq.shape[0]
    slots = CAPM * len(ks)
    total = q_tokens + p_tokens
    weight = pltpu.VMEM((width, cols), jnp.bfloat16)
    packed = pltpu.VMEM((slots * p_tokens, cols), jnp.bfloat16)
    out = jax.ShapeDtypeStruct((slots * total, half), jnp.bfloat16)
    return pl.pallas_call(
        functools.partial(layer_kernel, ks),
        out_shape=[out, out],
        in_specs=[SMEM, SMEM, VMEM, VMEM] + [ANY] * (2 * len(ks)) + [HBM] * 4,
        out_specs=[ANY, ANY],
        scratch_shapes=[weight] * 3
        + [
            pltpu.VMEM((2, cols, half), jnp.bfloat16),
            pltpu.VMEM((slots * p_tokens, width), jnp.bfloat16),
            packed,
            packed,
            packed,
            pltpu.VMEM((slots * total, cols), jnp.bfloat16),
            pltpu.VMEM((2, len(ks), CAPM, p_tokens, half), jnp.bfloat16),
            pltpu.VMEM((2, slots * total, half), jnp.bfloat16),
            pltpu.SMEM((3, slots + 1), jnp.int32),
            pltpu.SemaphoreType.DMA((3, 2)),
            pltpu.SemaphoreType.DMA((2,)),
            pltpu.SemaphoreType.DMA((2, len(ks))),
            pltpu.SemaphoreType.DMA((2,)),
        ],
        compiler_params=pltpu.CompilerParams(vmem_limit_bytes=VMEM_LAYER + slots * VMEM_SLOT),
        cost_estimate=LITTLE,
        name="layer",
    )(own, table, question, gain, *mine, *theirs, wq, wk, wv, wo)


def combine_kernel(ks, first, own_ref, table, questions, *refs):
    n = len(ks)
    mine = refs[:n]
    ours, arrived = refs[n : n + 2]
    encoded, staged, sems = refs[n + 2 if first else n + 3 :]
    slots, total, _ = staged.shape
    q_tokens = questions.shape[1]
    q_len = own_ref[0, 2]
    places, _ = compact(table, ks, q_tokens)

    def copy(s, pair):
        return pltpu.make_async_copy(staged.at[s], encoded.at[0, pair], sems.at[s])

    for s, (p_len, _, start) in enumerate(places):
        pair = table[0, place_of(ks, s)]

        @pl.when(pair >= 0)
        def _():
            for rows, low, length in (
                (questions[0], 0, q_len),
                (mine[s // CAPM][s % CAPM], q_tokens, p_len),
            ):
                count = rows.shape[0]
                spot = lax.broadcasted_iota(jnp.int32, (count, 1), 0)
                at = pl.ds(pl.multiple_of(start + low, PACK), count)
                branch = ours[at].astype(jnp.float32) + arrived[at].astype(jnp.float32)
                made = rows.astype(jnp.float32) + branch
                staged[s, low : low + count] = jnp.where(spot < length, made, 0.0).astype(
                    jnp.bfloat16
                )
            copy(s, pair).start()

    for s in range(slots):

        @pl.when(table[0, place_of(ks, s)] >= 0)
        def _():
            copy(s, 0).wait()


def combine(ks, encoded, shape, own, table, questions, mine, ours, arrived):
    first = encoded is None
    slots = CAPM * len(ks)
    operands = [own, table, questions, *mine, ours, arrived] + ([] if first else [encoded])
    return pl.pallas_call(
        functools.partial(combine_kernel, ks, first),
        out_shape=jax.ShapeDtypeStruct(shape, jnp.bfloat16),
        in_specs=[SMEM, SMEM, VMEM] + [VMEM] * (len(ks) + 2) + ([] if first else [ANY]),
        out_specs=ANY,
        scratch_shapes=[
            pltpu.VMEM((slots, *shape[2:]), jnp.bfloat16),
            pltpu.SemaphoreType.DMA((slots,)),
        ],
        input_output_aliases={} if first else {len(operands) - 1: 0},
        compiler_params=pltpu.CompilerParams(vmem_limit_bytes=VMEM_LAYER),
        cost_estimate=LITTLE,
        name="combine",
    )(*operands)


def body(questions, memory, retrieved, q_len, p_len, norm_gain, w_query, w_key, w_value, w_out):
    shards = lax.axis_size("mem")
    cores = lax.axis_size("tp")
    _, q_tokens, half = questions.shape
    p_tokens = memory.shape[1]
    wants = retrieved.shape[1]

    def swap(x):
        return lax.ppermute(x, "tp", [(i, (i + 1) % cores) for i in range(cores)])

    def exchange(x, k):
        return lax.ppermute(x, "mem", [(i, i ^ k) for i in range(shards)])

    asked, own = ask(retrieved, p_len, q_len, shards)
    metas = lax.all_to_all(asked, "mem", 0, 0, tiled=True)
    gain = norm_gain.reshape(cores, 1, half)
    near = shards // 2
    far = [*range(near + near // 2, shards), *range(near, near + near // 2)]
    steps = [(0,), (1, 2, *far[:2])] + [
        (k + 1, far[k]) if k + 1 < near else (far[k],) for k in range(2, near)
    ]
    first = steps[0] + steps[1]
    rest = tuple(k for k in range(shards) if k not in first)
    sends, (table,) = pick(first, True, own, asked, metas, memory)
    asked_rows, table = lax.optimization_barrier((questions, table))
    question = project_question(
        own, questions, swap(asked_rows), gain, w_query, w_key, w_value
    )
    mine = {0: sends[0]}
    for k in first[1:]:
        mine[k] = exchange(sends[k], k)
    later, question = lax.optimization_barrier((metas, question))
    sends, _ = pick(rest, False, own, asked, later, memory)
    question, *held = lax.optimization_barrier((question, *sends.values()))
    for k, x in zip(rest, held):
        mine[k] = exchange(x, k)
    encoded = None
    shape = (1, wants, q_tokens + p_tokens, half)
    waiting = None
    for ks in steps:
        rows = [mine[k] for k in ks]
        if waiting is not None:
            *rows, ours, other = lax.optimization_barrier((*rows, *waiting[2:]))
        theirs = [swap(x) for x in rows]
        if waiting is not None:
            encoded = combine(
                waiting[0], encoded, shape, own, table, questions, waiting[1], ours, swap(other)
            )
            theirs[0], encoded = lax.optimization_barrier((theirs[0], encoded))
        made = layer(
            ks, own, table, question, gain, rows, theirs, w_query, w_key, w_value, w_out
        )
        waiting = (ks, rows, *made)
    ks, rows, ours, other = waiting
    encoded = combine(ks, encoded, shape, own, table, questions, rows, ours, swap(other))
    return encoded


def solution(mesh):
    in_specs = (
        P(("groups", "mem"), None, "tp"),
        P("mem", None, "tp"),
        P(("groups", "mem"), None),
        P(("groups", "mem")),
        P("mem"),
        P(),
        P(None, "tp"),
        P(None, "tp"),
        P(None, "tp"),
        P("tp", None),
    )
    out_specs = P(("groups", "mem"), None, None, "tp")
    return jax.shard_map(body, mesh=mesh, in_specs=in_specs, out_specs=out_specs, check_vma=False)
```

```python
import functools

import jax
import jax.numpy as jnp
from jax import lax
from jax.experimental import pallas as pl
from jax.experimental.pallas import tpu as pltpu
from jax.sharding import PartitionSpec as P

HS = 64
CAPM = 2
EPS = 1e-06
MASKED = -1e30
LANES = 128
PACK = 16
VMEM_ALL = 60 * 1024 * 1024
VMEM_LAYER = 48 * 1024 * 1024

ANY = pl.BlockSpec(memory_space=pl.ANY)
HBM = pl.BlockSpec(memory_space=pltpu.HBM)
SMEM = pl.BlockSpec(memory_space=pltpu.SMEM)
VMEM = pl.BlockSpec(memory_space=pltpu.VMEM)
LITTLE = pl.CostEstimate(flops=1, bytes_accessed=1, transcendentals=0)


def ask_kernel(pass_dev, wants, position, retrieved, p_len, q_len, metas, own_ref):
    shards = metas.shape[0]
    own_ref[0, 0] = position[0]
    own_ref[0, 1] = position[1]
    own_ref[0, 2] = q_len[0]
    for shard in range(shards):
        for r in range(CAPM):
            metas[shard, 0, r] = jnp.int32(-1)
            own_ref[1, CAPM * shard + r] = jnp.int32(-1)
        for i in range(pass_dev):
            metas[shard, 0, CAPM + i] = p_len[i]

    def place(j, carry):
        wanted = retrieved[0, j]
        shard = lax.div(wanted, pass_dev)
        taken = (metas[shard, 0, 0] >= 0).astype(jnp.int32)
        metas[shard, 0, taken] = wanted - shard * pass_dev
        own_ref[1, CAPM * shard + taken] = j
        return carry

    lax.fori_loop(0, wants, place, 0)


def ask(retrieved, p_len, q_len, shards):
    position = jnp.stack([lax.axis_index("tp"), lax.axis_index("mem")]).astype(jnp.int32)
    return pl.pallas_call(
        functools.partial(ask_kernel, p_len.shape[0], retrieved.shape[1]),
        out_shape=[
            jax.ShapeDtypeStruct((shards, 1, LANES), jnp.int32),
            jax.ShapeDtypeStruct((2, LANES), jnp.int32),
        ],
        in_specs=[SMEM] * 4,
        out_specs=[SMEM] * 2,
        cost_estimate=LITTLE,
        name="ask",
    )(position, retrieved, p_len, q_len)


def pick_kernel(ks, own_ref, asked, metas, memory, *refs):
    n = len(ks)
    outs = refs[:n]
    table = refs[n] if len(refs) > n + 2 else None
    staged, sems = refs[-2:]
    shards = metas.shape[0]
    me = own_ref[0, 1]
    found = []
    for i, k in enumerate(ks):
        partner = lax.bitwise_xor(me, k)
        for r in range(CAPM):
            local = metas[partner, 0, r]
            found.append(
                (
                    local,
                    pltpu.make_async_copy(
                        memory.at[jnp.maximum(local, 0)], staged.at[i, r], sems.at[0, i, r]
                    ),
                    pltpu.make_async_copy(staged.at[i, r], outs[i].at[r], sems.at[1, i, r]),
                )
            )

            @pl.when(local >= 0)
            def _():
                found[-1][1].start()

    if table is not None:
        for k in range(shards):
            partner = lax.bitwise_xor(me, k)
            for r in range(CAPM):
                pair = own_ref[1, CAPM * partner + r]
                local = jnp.maximum(asked[partner, 0, r], 0)
                table[0, CAPM * k + r] = pair
                table[1, CAPM * k + r] = jnp.where(
                    pair >= 0, metas[partner, 0, CAPM + local], 0
                )
    for local, come, go in found:

        @pl.when(local >= 0)
        def _():
            come.wait()
            go.start()

    for local, _, go in found:

        @pl.when(local >= 0)
        def _():
            go.wait()


def pick(ks, with_table, own, asked, metas, memory):
    n = len(ks)
    _, p_tokens, half = memory.shape
    slot = jax.ShapeDtypeStruct((CAPM, p_tokens, half), memory.dtype)
    result = pl.pallas_call(
        functools.partial(pick_kernel, ks),
        out_shape=[slot] * n + [jax.ShapeDtypeStruct((2, LANES), jnp.int32)] * with_table,
        in_specs=[SMEM, SMEM, SMEM, HBM],
        out_specs=[ANY] * n + [SMEM] * with_table,
        scratch_shapes=[
            pltpu.VMEM((n, CAPM, p_tokens, half), memory.dtype),
            pltpu.SemaphoreType.DMA((2, n, CAPM)),
        ],
        compiler_params=pltpu.CompilerParams(vmem_limit_bytes=VMEM_ALL),
        cost_estimate=LITTLE,
        name="pick",
    )(own, asked, metas, memory)
    return dict(zip(ks, result)), result[n:]


def normed_halves(own, other, gain_own, gain_other):
    own = own.astype(jnp.float32)
    other = other.astype(jnp.float32)
    total = jnp.sum(own * own + other * other, axis=-1, keepdims=True)
    scale = lax.rsqrt(total / (2 * own.shape[-1]) + EPS)
    return (
        (own * scale * gain_own).astype(jnp.bfloat16),
        (other * scale * gain_other).astype(jnp.bfloat16),
    )


def weight_copies(c, half, sources, targets, sems):
    copies = []
    for i, (source, target) in enumerate(zip(sources, targets)):
        pieces = []
        for part, core in enumerate((c, 1 - c)):
            start = pl.multiple_of(core * half, half)
            pieces.append(
                pltpu.make_async_copy(
                    source.at[pl.ds(start, half), :],
                    target.at[pl.ds(part * half, half), :],
                    sems.at[i, part],
                )
            )
        copies.append(pieces)
    return copies


def question_kernel(own_ref, mine, theirs, gain, wq, wk, wv, out, vq, vk, vv, sems):
    c = own_ref[0, 0]
    half = mine.shape[-1]
    copies = weight_copies(c, half, (wq, wk, wv), (vq, vk, vv), sems)
    for pieces in copies:
        for piece in pieces:
            piece.start()
    g_own = gain[c].astype(jnp.float32)
    g_other = gain[1 - c].astype(jnp.float32)
    first, second = normed_halves(mine[0], theirs[0], g_own, g_other)
    rows = jnp.concatenate([first, second], axis=1)
    for i, weight in enumerate((vq, vk, vv)):
        for piece in copies[i]:
            piece.wait()
        made = jnp.dot(rows, weight[...], preferred_element_type=jnp.float32)
        made = made.astype(jnp.bfloat16)
        if i == 0:
            made = made * jnp.bfloat16(1.0 / 8.0)
        out[i] = made


def project_question(own, mine, theirs, gain, wq, wk, wv):
    _, q_tokens, half = mine.shape
    width, cols = wq.shape
    weight = pltpu.VMEM((width, cols), jnp.bfloat16)
    return pl.pallas_call(
        question_kernel,
        out_shape=jax.ShapeDtypeStruct((3, q_tokens, cols), jnp.bfloat16),
        in_specs=[SMEM, VMEM, VMEM, VMEM, HBM, HBM, HBM],
        out_specs=VMEM,
        scratch_shapes=[weight] * 3 + [pltpu.SemaphoreType.DMA((3, 2))],
        compiler_params=pltpu.CompilerParams(vmem_limit_bytes=VMEM_ALL),
        cost_estimate=LITTLE,
        name="question_projections",
    )(own, mine, theirs, gain, wq, wk, wv)


def place_of(ks, s):
    return CAPM * ks[s // CAPM] + s % CAPM


def compact(table, ks, q_tokens):
    places = []
    start = jnp.int32(0)
    start_out = jnp.int32(0)
    for s in range(CAPM * len(ks)):
        p_len = table[1, place_of(ks, s)]
        room = lax.bitwise_and(p_len + (PACK - 1), ~(PACK - 1))
        places.append((p_len, pl.multiple_of(start, PACK), pl.multiple_of(start_out, PACK)))
        start = start + room
        start_out = start_out + jnp.where(p_len > 0, room + q_tokens, 0)
    return places, start_out


def pick_span(p_len, spans):
    span = jnp.int32(spans[-1][1])
    for queries, keys in reversed(spans[:-1]):
        span = jnp.where(p_len <= queries, keys, span)
    return span


def for_rows(needed, counts, run):
    least = 0
    for count in counts:

        @pl.when(jnp.logical_and(needed > least, needed <= count))
        def _():
            run(count)

        least = count


def layer_kernel(ks, own_ref, table, question, gain, *refs):
    n = len(ks)
    mine, theirs = refs[:n], refs[n : 2 * n]
    wq, wk, wv, wo = refs[2 * n : 2 * n + 4]
    out_own, out_other = refs[2 * n + 4 : 2 * n + 6]
    vq, vk, vv, vo, rows, query, key, value, attended, raw, made_out, listed = refs[
        2 * n + 6 : -4
    ]
    sems, sems_out, sems_rows, sems_made = refs[-4:]
    cols = query.shape[1]
    q_tokens = question.shape[1]
    _, p_tokens, half = mine[0].shape
    slots = CAPM * n
    total = q_tokens + p_tokens
    spans = ((3 * p_tokens // 4, 3 * p_tokens // 4), (p_tokens, p_tokens))
    c = own_ref[0, 0]
    q_len = own_ref[0, 2]
    copies = weight_copies(c, half, (wq, wk, wv), (vq, vk, vv), sems)
    out_copies = []
    for part, core in enumerate((1 - c, c)):
        start = pl.multiple_of(core * half, half)
        out_copies.append(
            pltpu.make_async_copy(wo.at[:, pl.ds(start, half)], vo.at[part], sems_out.at[part])
        )
    row_copies = []
    for part, sources in enumerate((mine, theirs)):
        for i, source in enumerate(sources):
            row_copies.append(
                pltpu.make_async_copy(source, raw.at[part, i], sems_rows.at[part, i])
            )
    def launch(pieces):
        for piece in pieces:
            piece.start()

    launch(row_copies)
    launch(copies[0])
    launch(copies[1])
    places, used_out = compact(table, ks, q_tokens)
    used = jnp.int32(0)
    valid = jnp.int32(0)
    for p_len, start, start_out in places:
        used = jnp.where(p_len > 0, jnp.maximum(used, start + pick_span(p_len, spans)), used)
        listed[0, valid] = p_len
        listed[1, valid] = start
        listed[2, valid] = start_out
        valid = valid + (p_len > 0).astype(jnp.int32)
    g_own = gain[c].astype(jnp.float32)
    g_other = gain[1 - c].astype(jnp.float32)
    for piece in row_copies:
        piece.wait()
    for s, (p_len, start, _) in enumerate(places):

        @pl.when(p_len > 0)
        def _():
            first, second = normed_halves(
                raw[0, s // CAPM, s % CAPM], raw[1, s // CAPM, s % CAPM], g_own, g_other
            )
            rows[pl.ds(start, p_tokens), :half] = first
            rows[pl.ds(start, p_tokens), half:] = second

    def project(count):
        for i, (weight, target) in enumerate(((vq, query), (vk, key), (vv, value))):
            for piece in copies[i]:
                piece.wait()
            launch((copies[2], out_copies[:1], out_copies[1:])[i])
            for left in range(0, cols, 256):
                span = slice(left, left + 256)
                made = jnp.dot(
                    rows[:count], weight[:, span], preferred_element_type=jnp.float32
                ).astype(jnp.bfloat16)
                if i == 0:
                    made = made * jnp.bfloat16(1.0 / 8.0)
                target[:count, span] = made

    most = slots * p_tokens
    for_rows(used, [c for c in (128, 256, 384) if c < most and c > most // 4] + [most], project)

    @pl.when(used == 0)
    def _():
        for piece in copies[0] + copies[1]:
            piece.wait()

    lane = lax.broadcasted_iota(jnp.int32, (1, 2 * HS), 1)
    in_first = lane < HS
    row_in_first = lax.broadcasted_iota(jnp.int32, (2 * HS, 1), 0) < HS

    def attend(p_len, start, start_out, queries, keys):
        both = q_tokens + queries
        room = -(-(q_tokens + keys) // LANES) * LANES
        spot = lax.broadcasted_iota(jnp.int32, (1, room), 1)
        end = jnp.where(spot < q_tokens, q_len, q_tokens + p_len)
        bias = jnp.where(spot < end, 0.0, MASKED)
        bias = jnp.concatenate([bias, bias], axis=1)
        one = jnp.ones((room, 2 * HS), jnp.bfloat16)

        def pair_rows(i, source, count, span):
            return jnp.concatenate(
                [question[i, :, span], source[pl.ds(start, count), span]], axis=0
            )

        def key_rows(i, source, span):
            found = pair_rows(i, source, keys, span)
            if room > found.shape[0]:
                fill = jnp.zeros((room - found.shape[0], 2 * HS), jnp.bfloat16)
                found = jnp.concatenate([found, fill], axis=0)
            return found

        def by_head(x, first, axis):
            zero = jnp.zeros_like(x)
            return jnp.concatenate(
                [jnp.where(first, x, zero), jnp.where(first, zero, x)], axis=axis
            )

        spans_here = [slice(left, left + 2 * HS) for left in range(0, cols, 2 * HS)]
        scores = [
            jnp.dot(
                pair_rows(0, query, queries, span),
                by_head(key_rows(1, key, span).T, row_in_first, 1),
                preferred_element_type=jnp.float32,
            )
            + bias
            for span in spans_here
        ]
        raised = []
        for x in scores:
            halves = (x[:, :room], x[:, room:])
            raised.append(
                jnp.concatenate(
                    [
                        jnp.exp(y - jnp.max(y, axis=1, keepdims=True)).astype(jnp.bfloat16)
                        for y in halves
                    ],
                    axis=1,
                )
            )
        ones = by_head(one, in_first, 0)
        with_sums = [
            jnp.dot(
                x,
                jnp.concatenate([by_head(key_rows(2, value, span), in_first, 0), ones], axis=1),
                preferred_element_type=jnp.float32,
            )
            for x, span in zip(raised, spans_here)
        ]
        for x, span in zip(with_sums, spans_here):
            attended[pl.ds(start_out, both), span] = (
                x[:, : 2 * HS] / x[:, 2 * HS :]
            ).astype(jnp.bfloat16)

    def attend_next(t, carry):
        p_len = listed[0, t]
        start = pl.multiple_of(listed[1, t], PACK)
        start_out = pl.multiple_of(listed[2, t], PACK)
        least = 0
        for queries, keys in spans:

            @pl.when(jnp.logical_and(p_len > least, p_len <= queries))
            def _():
                attend(p_len, start, start_out, queries, keys)

            least = queries
        return carry

    lax.fori_loop(0, valid, attend_next, 0)

    def put_out(count):
        for part, out in enumerate((out_other, out_own)):
            out_copies[part].wait()
            for left in range(0, half, 256):
                span = slice(left, left + 256)
                made_out[part, :count, span] = jnp.dot(
                    attended[:count], vo[part, :, span], preferred_element_type=jnp.float32
                ).astype(jnp.bfloat16)
            pltpu.make_async_copy(made_out.at[part], out, sems_made.at[part]).start()
        for part, out in enumerate((out_other, out_own)):
            pltpu.make_async_copy(made_out.at[part], out, sems_made.at[part]).wait()

    most = slots * total
    for_rows(
        used_out, [c for c in (192, 256, 384, 512) if c < most and c > most // 3] + [most], put_out
    )


def layer(ks, own, table, question, gain, mine, theirs, wq, wk, wv, wo):
    _, p_tokens, half = mine[0].shape
    _, q_tokens, cols = question.shape
    width = wq.shape[0]
    slots = CAPM * len(ks)
    total = q_tokens + p_tokens
    weight = pltpu.VMEM((width, cols), jnp.bfloat16)
    packed = pltpu.VMEM((slots * p_tokens, cols), jnp.bfloat16)
    out = jax.ShapeDtypeStruct((slots * total, half), jnp.bfloat16)
    return pl.pallas_call(
        functools.partial(layer_kernel, ks),
        out_shape=[out, out],
        in_specs=[SMEM, SMEM, VMEM, VMEM] + [ANY] * (2 * len(ks)) + [HBM] * 4,
        out_specs=[ANY, ANY],
        scratch_shapes=[weight] * 3
        + [
            pltpu.VMEM((2, cols, half), jnp.bfloat16),
            pltpu.VMEM((slots * p_tokens, width), jnp.bfloat16),
            packed,
            packed,
            packed,
            pltpu.VMEM((slots * total, cols), jnp.bfloat16),
            pltpu.VMEM((2, len(ks), CAPM, p_tokens, half), jnp.bfloat16),
            pltpu.VMEM((2, slots * total, half), jnp.bfloat16),
            pltpu.SMEM((3, slots + 1), jnp.int32),
            pltpu.SemaphoreType.DMA((3, 2)),
            pltpu.SemaphoreType.DMA((2,)),
            pltpu.SemaphoreType.DMA((2, len(ks))),
            pltpu.SemaphoreType.DMA((2,)),
        ],
        compiler_params=pltpu.CompilerParams(vmem_limit_bytes=VMEM_LAYER),
        cost_estimate=LITTLE,
        name="layer",
    )(own, table, question, gain, *mine, *theirs, wq, wk, wv, wo)


def combine_kernel(ks, first, own_ref, table, questions, *refs):
    n = len(ks)
    mine = refs[:n]
    ours, arrived = refs[n : n + 2]
    encoded, staged, sems = refs[n + 2 if first else n + 3 :]
    slots, total, _ = staged.shape
    q_tokens = questions.shape[1]
    q_len = own_ref[0, 2]
    places, _ = compact(table, ks, q_tokens)

    def copy(s, pair):
        return pltpu.make_async_copy(staged.at[s], encoded.at[0, pair], sems.at[s])

    for s, (p_len, _, start) in enumerate(places):
        pair = table[0, place_of(ks, s)]

        @pl.when(pair >= 0)
        def _():
            for rows, low, length in (
                (questions[0], 0, q_len),
                (mine[s // CAPM][s % CAPM], q_tokens, p_len),
            ):
                count = rows.shape[0]
                spot = lax.broadcasted_iota(jnp.int32, (count, 1), 0)
                at = pl.ds(pl.multiple_of(start + low, PACK), count)
                branch = ours[at].astype(jnp.float32) + arrived[at].astype(jnp.float32)
                made = rows.astype(jnp.float32) + branch
                staged[s, low : low + count] = jnp.where(spot < length, made, 0.0).astype(
                    jnp.bfloat16
                )
            copy(s, pair).start()

    for s in range(slots):

        @pl.when(table[0, place_of(ks, s)] >= 0)
        def _():
            copy(s, 0).wait()


def combine(ks, encoded, shape, own, table, questions, mine, ours, arrived):
    first = encoded is None
    slots = CAPM * len(ks)
    operands = [own, table, questions, *mine, ours, arrived] + ([] if first else [encoded])
    return pl.pallas_call(
        functools.partial(combine_kernel, ks, first),
        out_shape=jax.ShapeDtypeStruct(shape, jnp.bfloat16),
        in_specs=[SMEM, SMEM, VMEM] + [VMEM] * (len(ks) + 2) + ([] if first else [ANY]),
        out_specs=ANY,
        scratch_shapes=[
            pltpu.VMEM((slots, *shape[2:]), jnp.bfloat16),
            pltpu.SemaphoreType.DMA((slots,)),
        ],
        input_output_aliases={} if first else {len(operands) - 1: 0},
        compiler_params=pltpu.CompilerParams(vmem_limit_bytes=VMEM_LAYER),
        cost_estimate=LITTLE,
        name="combine",
    )(*operands)


def body(questions, memory, retrieved, q_len, p_len, norm_gain, w_query, w_key, w_value, w_out):
    shards = lax.axis_size("mem")
    cores = lax.axis_size("tp")
    _, q_tokens, half = questions.shape
    p_tokens = memory.shape[1]
    wants = retrieved.shape[1]

    def swap(x):
        return lax.ppermute(x, "tp", [(i, (i + 1) % cores) for i in range(cores)])

    def exchange(x, k):
        return lax.ppermute(x, "mem", [(i, i ^ k) for i in range(shards)])

    asked, own = ask(retrieved, p_len, q_len, shards)
    metas = lax.all_to_all(asked, "mem", 0, 0, tiled=True)
    gain = norm_gain.reshape(cores, 1, half)
    near = shards // 2
    far = [*range(near + near // 2, shards), *range(near, near + near // 2)]
    chunks = [(0,)] + [(k, far[k - 1]) for k in range(1, near)] + [(far[-1],)]
    come = [(0,), (1, 2, far[0])] + [
        (k, far[k - 2]) if k < near else (far[k - 2],) for k in range(3, near + 2)
    ]
    first = (0, 1, 2, far[0])
    rest = tuple(k for k in range(shards) if k not in first)
    sends, (table,) = pick(first, True, own, asked, metas, memory)
    asked_rows, table = lax.optimization_barrier((questions, table))
    question = project_question(
        own, questions, swap(asked_rows), gain, w_query, w_key, w_value
    )
    mine = {0: sends[0]}
    for k in first[1:]:
        mine[k] = exchange(sends[k], k)
    later, question = lax.optimization_barrier((metas, question))
    sends, _ = pick(rest, False, own, asked, later, memory)
    question, *held = lax.optimization_barrier((question, *sends.values()))
    for k, x in zip(rest, held):
        mine[k] = exchange(x, k)
    encoded = None
    shape = (1, wants, q_tokens + p_tokens, half)
    waiting = None
    for i, ks in enumerate(chunks):
        if waiting is not None:
            rows = [mine[k] for k in come[i]]
            *rows, ours, other = lax.optimization_barrier((*rows, *waiting[2:]))
            mine.update(zip(come[i], rows))
        rows = [mine[k] for k in ks]
        theirs = [swap(x) for x in rows]
        if waiting is not None:
            encoded = combine(
                waiting[0], encoded, shape, own, table, questions, waiting[1], ours, swap(other)
            )
            theirs[0], encoded = lax.optimization_barrier((theirs[0], encoded))
        made = layer(
            ks, own, table, question, gain, rows, theirs, w_query, w_key, w_value, w_out
        )
        waiting = (ks, rows, *made)
    ks, rows, ours, other = waiting
    encoded = combine(ks, encoded, shape, own, table, questions, rows, ours, swap(other))
    return encoded


def solution(mesh):
    in_specs = (
        P(("groups", "mem"), None, "tp"),
        P("mem", None, "tp"),
        P(("groups", "mem"), None),
        P(("groups", "mem")),
        P("mem"),
        P(),
        P(None, "tp"),
        P(None, "tp"),
        P(None, "tp"),
        P("tp", None),
    )
    out_specs = P(("groups", "mem"), None, None, "tp")
    return jax.shard_map(body, mesh=mesh, in_specs=in_specs, out_specs=out_specs, check_vma=False)
```

```python
import functools

import jax
import jax.numpy as jnp
from jax import lax
from jax.experimental import pallas as pl
from jax.experimental.pallas import tpu as pltpu
from jax.sharding import PartitionSpec as P

HS = 64
CAPM = 2
EPS = 1e-06
MASKED = -1e30
LANES = 128
PACK = 16
VMEM_ALL = 60 * 1024 * 1024
VMEM_LAYER = 48 * 1024 * 1024

ANY = pl.BlockSpec(memory_space=pl.ANY)
HBM = pl.BlockSpec(memory_space=pltpu.HBM)
SMEM = pl.BlockSpec(memory_space=pltpu.SMEM)
VMEM = pl.BlockSpec(memory_space=pltpu.VMEM)
LITTLE = pl.CostEstimate(flops=1, bytes_accessed=1, transcendentals=0)


def ask_kernel(pass_dev, wants, position, retrieved, p_len, q_len, metas, own_ref):
    shards = metas.shape[0]
    own_ref[0, 0] = position[0]
    own_ref[0, 1] = position[1]
    own_ref[0, 2] = q_len[0]
    for shard in range(shards):
        for r in range(CAPM):
            metas[shard, 0, r] = jnp.int32(-1)
            own_ref[1, CAPM * shard + r] = jnp.int32(-1)
        for i in range(pass_dev):
            metas[shard, 0, CAPM + i] = p_len[i]

    def place(j, carry):
        wanted = retrieved[0, j]
        shard = lax.div(wanted, pass_dev)
        taken = (metas[shard, 0, 0] >= 0).astype(jnp.int32)
        metas[shard, 0, taken] = wanted - shard * pass_dev
        own_ref[1, CAPM * shard + taken] = j
        return carry

    lax.fori_loop(0, wants, place, 0)


def ask(retrieved, p_len, q_len, shards):
    position = jnp.stack([lax.axis_index("tp"), lax.axis_index("mem")]).astype(jnp.int32)
    return pl.pallas_call(
        functools.partial(ask_kernel, p_len.shape[0], retrieved.shape[1]),
        out_shape=[
            jax.ShapeDtypeStruct((shards, 1, LANES), jnp.int32),
            jax.ShapeDtypeStruct((2, LANES), jnp.int32),
        ],
        in_specs=[SMEM] * 4,
        out_specs=[SMEM] * 2,
        cost_estimate=LITTLE,
        name="ask",
    )(position, retrieved, p_len, q_len)


def pick_kernel(ks, own_ref, asked, metas, memory, *refs):
    n = len(ks)
    outs = refs[:n]
    table = refs[n] if len(refs) > n + 2 else None
    staged, sems = refs[-2:]
    shards = metas.shape[0]
    me = own_ref[0, 1]
    found = []
    for i, k in enumerate(ks):
        partner = lax.bitwise_xor(me, k)
        for r in range(CAPM):
            local = metas[partner, 0, r]
            found.append(
                (
                    local,
                    pltpu.make_async_copy(
                        memory.at[jnp.maximum(local, 0)], staged.at[i, r], sems.at[0, i, r]
                    ),
                    pltpu.make_async_copy(staged.at[i, r], outs[i].at[r], sems.at[1, i, r]),
                )
            )

            @pl.when(local >= 0)
            def _():
                found[-1][1].start()

    if table is not None:
        for k in range(shards):
            partner = lax.bitwise_xor(me, k)
            for r in range(CAPM):
                pair = own_ref[1, CAPM * partner + r]
                local = jnp.maximum(asked[partner, 0, r], 0)
                table[0, CAPM * k + r] = pair
                table[1, CAPM * k + r] = jnp.where(
                    pair >= 0, metas[partner, 0, CAPM + local], 0
                )
    for local, come, go in found:

        @pl.when(local >= 0)
        def _():
            come.wait()
            go.start()

    for local, _, go in found:

        @pl.when(local >= 0)
        def _():
            go.wait()


def pick(ks, with_table, own, asked, metas, memory):
    n = len(ks)
    _, p_tokens, half = memory.shape
    slot = jax.ShapeDtypeStruct((CAPM, p_tokens, half), memory.dtype)
    result = pl.pallas_call(
        functools.partial(pick_kernel, ks),
        out_shape=[slot] * n + [jax.ShapeDtypeStruct((2, LANES), jnp.int32)] * with_table,
        in_specs=[SMEM, SMEM, SMEM, HBM],
        out_specs=[ANY] * n + [SMEM] * with_table,
        scratch_shapes=[
            pltpu.VMEM((n, CAPM, p_tokens, half), memory.dtype),
            pltpu.SemaphoreType.DMA((2, n, CAPM)),
        ],
        compiler_params=pltpu.CompilerParams(vmem_limit_bytes=VMEM_ALL),
        cost_estimate=LITTLE,
        name="pick",
    )(own, asked, metas, memory)
    return dict(zip(ks, result)), result[n:]


def normed_halves(own, other, gain_own, gain_other):
    own = own.astype(jnp.float32)
    other = other.astype(jnp.float32)
    total = jnp.sum(own * own + other * other, axis=-1, keepdims=True)
    scale = lax.rsqrt(total / (2 * own.shape[-1]) + EPS)
    return (
        (own * scale * gain_own).astype(jnp.bfloat16),
        (other * scale * gain_other).astype(jnp.bfloat16),
    )


def weight_copies(c, half, sources, targets, sems):
    copies = []
    for i, (source, target) in enumerate(zip(sources, targets)):
        pieces = []
        for part, core in enumerate((c, 1 - c)):
            start = pl.multiple_of(core * half, half)
            pieces.append(
                pltpu.make_async_copy(
                    source.at[pl.ds(start, half), :],
                    target.at[pl.ds(part * half, half), :],
                    sems.at[i, part],
                )
            )
        copies.append(pieces)
    return copies


def question_kernel(own_ref, mine, theirs, gain, wq, wk, wv, out, vq, vk, vv, sems):
    c = own_ref[0, 0]
    half = mine.shape[-1]
    copies = weight_copies(c, half, (wq, wk, wv), (vq, vk, vv), sems)
    for pieces in copies:
        for piece in pieces:
            piece.start()
    g_own = gain[c].astype(jnp.float32)
    g_other = gain[1 - c].astype(jnp.float32)
    first, second = normed_halves(mine[0], theirs[0], g_own, g_other)
    rows = jnp.concatenate([first, second], axis=1)
    for i, weight in enumerate((vq, vk, vv)):
        for piece in copies[i]:
            piece.wait()
        made = jnp.dot(rows, weight[...], preferred_element_type=jnp.float32)
        made = made.astype(jnp.bfloat16)
        if i == 0:
            made = made * jnp.bfloat16(1.0 / 8.0)
        out[i] = made


def project_question(own, mine, theirs, gain, wq, wk, wv):
    _, q_tokens, half = mine.shape
    width, cols = wq.shape
    weight = pltpu.VMEM((width, cols), jnp.bfloat16)
    return pl.pallas_call(
        question_kernel,
        out_shape=jax.ShapeDtypeStruct((3, q_tokens, cols), jnp.bfloat16),
        in_specs=[SMEM, VMEM, VMEM, VMEM, HBM, HBM, HBM],
        out_specs=VMEM,
        scratch_shapes=[weight] * 3 + [pltpu.SemaphoreType.DMA((3, 2))],
        compiler_params=pltpu.CompilerParams(vmem_limit_bytes=VMEM_ALL),
        cost_estimate=LITTLE,
        name="question_projections",
    )(own, mine, theirs, gain, wq, wk, wv)


def place_of(ks, s):
    return CAPM * ks[s // CAPM] + s % CAPM


def compact(table, ks, q_tokens):
    places = []
    start = jnp.int32(0)
    start_out = jnp.int32(0)
    for s in range(CAPM * len(ks)):
        p_len = table[1, place_of(ks, s)]
        room = lax.bitwise_and(p_len + (PACK - 1), ~(PACK - 1))
        places.append((p_len, pl.multiple_of(start, PACK), pl.multiple_of(start_out, PACK)))
        start = start + room
        start_out = start_out + jnp.where(p_len > 0, room + q_tokens, 0)
    return places, start_out


def pick_span(p_len, spans):
    span = jnp.int32(spans[-1][1])
    for queries, keys in reversed(spans[:-1]):
        span = jnp.where(p_len <= queries, keys, span)
    return span


def for_rows(needed, counts, run):
    least = 0
    for count in counts:

        @pl.when(jnp.logical_and(needed > least, needed <= count))
        def _():
            run(count)

        least = count


def layer_kernel(ks, own_ref, table, question, gain, *refs):
    n = len(ks)
    mine, theirs = refs[:n], refs[n : 2 * n]
    wq, wk, wv, wo = refs[2 * n : 2 * n + 4]
    out_own, out_other = refs[2 * n + 4 : 2 * n + 6]
    vq, vk, vv, vo, rows, query, key, value, attended, raw, made_out, listed = refs[
        2 * n + 6 : -4
    ]
    sems, sems_out, sems_rows, sems_made = refs[-4:]
    cols = query.shape[1]
    q_tokens = question.shape[1]
    _, p_tokens, half = mine[0].shape
    slots = CAPM * n
    total = q_tokens + p_tokens
    spans = ((3 * p_tokens // 4, 3 * p_tokens // 4), (p_tokens, p_tokens))
    c = own_ref[0, 0]
    q_len = own_ref[0, 2]
    copies = weight_copies(c, half, (wq, wk, wv), (vq, vk, vv), sems)
    out_copies = []
    for part, core in enumerate((1 - c, c)):
        start = pl.multiple_of(core * half, half)
        out_copies.append(
            pltpu.make_async_copy(wo.at[:, pl.ds(start, half)], vo.at[part], sems_out.at[part])
        )
    row_copies = []
    for part, sources in enumerate((mine, theirs)):
        for i, source in enumerate(sources):
            row_copies.append(
                pltpu.make_async_copy(source, raw.at[part, i], sems_rows.at[part, i])
            )
    for pieces in [row_copies] + copies + [out_copies]:
        for piece in pieces:
            piece.start()
    places, used_out = compact(table, ks, q_tokens)
    used = jnp.int32(0)
    valid = jnp.int32(0)
    for p_len, start, start_out in places:
        used = jnp.where(p_len > 0, jnp.maximum(used, start + pick_span(p_len, spans)), used)
        listed[0, valid] = p_len
        listed[1, valid] = start
        listed[2, valid] = start_out
        valid = valid + (p_len > 0).astype(jnp.int32)
    g_own = gain[c].astype(jnp.float32)
    g_other = gain[1 - c].astype(jnp.float32)
    for piece in row_copies:
        piece.wait()
    for s, (p_len, start, _) in enumerate(places):

        @pl.when(p_len > 0)
        def _():
            first, second = normed_halves(
                raw[0, s // CAPM, s % CAPM], raw[1, s // CAPM, s % CAPM], g_own, g_other
            )
            rows[pl.ds(start, p_tokens), :half] = first
            rows[pl.ds(start, p_tokens), half:] = second

    def project(count):
        for i, (weight, target) in enumerate(((vq, query), (vk, key), (vv, value))):
            for piece in copies[i]:
                piece.wait()
            for left in range(0, cols, 256):
                span = slice(left, left + 256)
                made = jnp.dot(
                    rows[:count], weight[:, span], preferred_element_type=jnp.float32
                ).astype(jnp.bfloat16)
                if i == 0:
                    made = made * jnp.bfloat16(1.0 / 8.0)
                target[:count, span] = made

    most = slots * p_tokens
    for_rows(used, [c for c in (128, 256, 384, 512) if most // 3 < c < most] + [most], project)

    @pl.when(used == 0)
    def _():
        for pieces in copies:
            for piece in pieces:
                piece.wait()

    lane = lax.broadcasted_iota(jnp.int32, (1, 2 * HS), 1)
    in_first = lane < HS

    def attend(p_len, start, start_out, queries, keys):
        both = q_tokens + queries
        room = -(-(q_tokens + keys) // LANES) * LANES
        spot = lax.broadcasted_iota(jnp.int32, (1, room), 1)
        end = jnp.where(spot < q_tokens, q_len, q_tokens + p_len)
        bias = jnp.where(spot < end, 0.0, MASKED)
        bias = jnp.concatenate([bias, bias], axis=1)
        one = jnp.ones((room, 2 * HS), jnp.bfloat16)

        def pair_rows(i, source, count, span):
            return jnp.concatenate(
                [question[i, :, span], source[pl.ds(start, count), span]], axis=0
            )

        def key_rows(i, source, span):
            found = pair_rows(i, source, keys, span)
            if room > found.shape[0]:
                fill = jnp.zeros((room - found.shape[0], 2 * HS), jnp.bfloat16)
                found = jnp.concatenate([found, fill], axis=0)
            return found

        def by_head(x):
            zero = jnp.zeros_like(x)
            return jnp.concatenate(
                [jnp.where(in_first, x, zero), jnp.where(in_first, zero, x)], axis=0
            )

        spans_here = [slice(left, left + 2 * HS) for left in range(0, cols, 2 * HS)]
        scores = [
            lax.dot_general(
                pair_rows(0, query, queries, span),
                by_head(key_rows(1, key, span)),
                (((1,), (1,)), ((), ())),
                preferred_element_type=jnp.float32,
            )
            + bias
            for span in spans_here
        ]
        raised = []
        for x in scores:
            halves = (x[:, :room], x[:, room:])
            raised.append(
                jnp.concatenate(
                    [
                        jnp.exp(y - jnp.max(y, axis=1, keepdims=True)).astype(jnp.bfloat16)
                        for y in halves
                    ],
                    axis=1,
                )
            )
        ones = by_head(one)
        with_sums = [
            jnp.dot(
                x,
                jnp.concatenate([by_head(key_rows(2, value, span)), ones], axis=1),
                preferred_element_type=jnp.float32,
            )
            for x, span in zip(raised, spans_here)
        ]
        for x, span in zip(with_sums, spans_here):
            attended[pl.ds(start_out, both), span] = (
                x[:, : 2 * HS] / x[:, 2 * HS :]
            ).astype(jnp.bfloat16)

    def attend_next(t, carry):
        p_len = listed[0, t]
        start = pl.multiple_of(listed[1, t], PACK)
        start_out = pl.multiple_of(listed[2, t], PACK)
        least = 0
        for queries, keys in spans:

            @pl.when(jnp.logical_and(p_len > least, p_len <= queries))
            def _():
                attend(p_len, start, start_out, queries, keys)

            least = queries
        return carry

    lax.fori_loop(0, valid, attend_next, 0)

    def put_out(count):
        for part, out in enumerate((out_other, out_own)):
            out_copies[part].wait()
            for left in range(0, half, 256):
                span = slice(left, left + 256)
                made_out[part, :count, span] = jnp.dot(
                    attended[:count], vo[part, :, span], preferred_element_type=jnp.float32
                ).astype(jnp.bfloat16)
            pltpu.make_async_copy(made_out.at[part], out, sems_made.at[part]).start()
        for part, out in enumerate((out_other, out_own)):
            pltpu.make_async_copy(made_out.at[part], out, sems_made.at[part]).wait()

    most = slots * total
    for_rows(
        used_out, [c for c in (192, 256, 384, 512, 640) if 3 * most // 8 < c < most] + [most], put_out
    )

    @pl.when(used_out == 0)
    def _():
        for piece in out_copies:
            piece.wait()


def layer(ks, own, table, question, gain, mine, theirs, wq, wk, wv, wo):
    _, p_tokens, half = mine[0].shape
    _, q_tokens, cols = question.shape
    width = wq.shape[0]
    slots = CAPM * len(ks)
    total = q_tokens + p_tokens
    weight = pltpu.VMEM((width, cols), jnp.bfloat16)
    packed = pltpu.VMEM((slots * p_tokens, cols), jnp.bfloat16)
    out = jax.ShapeDtypeStruct((slots * total, half), jnp.bfloat16)
    return pl.pallas_call(
        functools.partial(layer_kernel, ks),
        out_shape=[out, out],
        in_specs=[SMEM, SMEM, VMEM, VMEM] + [ANY] * (2 * len(ks)) + [HBM] * 4,
        out_specs=[ANY, ANY],
        scratch_shapes=[weight] * 3
        + [
            pltpu.VMEM((2, cols, half), jnp.bfloat16),
            pltpu.VMEM((slots * p_tokens, width), jnp.bfloat16),
            packed,
            packed,
            packed,
            pltpu.VMEM((slots * total, cols), jnp.bfloat16),
            pltpu.VMEM((2, len(ks), CAPM, p_tokens, half), jnp.bfloat16),
            pltpu.VMEM((2, slots * total, half), jnp.bfloat16),
            pltpu.SMEM((3, slots + 1), jnp.int32),
            pltpu.SemaphoreType.DMA((3, 2)),
            pltpu.SemaphoreType.DMA((2,)),
            pltpu.SemaphoreType.DMA((2, len(ks))),
            pltpu.SemaphoreType.DMA((2,)),
        ],
        compiler_params=pltpu.CompilerParams(vmem_limit_bytes=VMEM_LAYER),
        cost_estimate=LITTLE,
        name="layer",
    )(own, table, question, gain, *mine, *theirs, wq, wk, wv, wo)


def combine_kernel(ks, first, own_ref, table, questions, *refs):
    n = len(ks)
    mine = refs[:n]
    ours, arrived = refs[n : n + 2]
    encoded, staged, sems = refs[n + 2 if first else n + 3 :]
    slots, total, _ = staged.shape
    q_tokens = questions.shape[1]
    q_len = own_ref[0, 2]
    places, _ = compact(table, ks, q_tokens)

    def copy(s, pair):
        return pltpu.make_async_copy(staged.at[s], encoded.at[0, pair], sems.at[s])

    for s, (p_len, _, start) in enumerate(places):
        pair = table[0, place_of(ks, s)]

        @pl.when(pair >= 0)
        def _():
            for rows, low, length in (
                (questions[0], 0, q_len),
                (mine[s // CAPM][s % CAPM], q_tokens, p_len),
            ):
                count = rows.shape[0]
                spot = lax.broadcasted_iota(jnp.int32, (count, 1), 0)
                at = pl.ds(pl.multiple_of(start + low, PACK), count)
                branch = ours[at].astype(jnp.float32) + arrived[at].astype(jnp.float32)
                made = rows.astype(jnp.float32) + branch
                staged[s, low : low + count] = jnp.where(spot < length, made, 0.0).astype(
                    jnp.bfloat16
                )
            copy(s, pair).start()

    for s in range(slots):

        @pl.when(table[0, place_of(ks, s)] >= 0)
        def _():
            copy(s, 0).wait()


def combine(ks, encoded, shape, own, table, questions, mine, ours, arrived):
    first = encoded is None
    slots = CAPM * len(ks)
    operands = [own, table, questions, *mine, ours, arrived] + ([] if first else [encoded])
    return pl.pallas_call(
        functools.partial(combine_kernel, ks, first),
        out_shape=jax.ShapeDtypeStruct(shape, jnp.bfloat16),
        in_specs=[SMEM, SMEM, VMEM] + [VMEM] * (len(ks) + 2) + ([] if first else [ANY]),
        out_specs=ANY,
        scratch_shapes=[
            pltpu.VMEM((slots, *shape[2:]), jnp.bfloat16),
            pltpu.SemaphoreType.DMA((slots,)),
        ],
        input_output_aliases={} if first else {len(operands) - 1: 0},
        compiler_params=pltpu.CompilerParams(vmem_limit_bytes=VMEM_LAYER),
        cost_estimate=LITTLE,
        name="combine",
    )(*operands)


def body(questions, memory, retrieved, q_len, p_len, norm_gain, w_query, w_key, w_value, w_out):
    shards = lax.axis_size("mem")
    cores = lax.axis_size("tp")
    _, q_tokens, half = questions.shape
    p_tokens = memory.shape[1]
    wants = retrieved.shape[1]

    def swap(x):
        return lax.ppermute(x, "tp", [(i, (i + 1) % cores) for i in range(cores)])

    def exchange(x, k):
        return lax.ppermute(x, "mem", [(i, i ^ k) for i in range(shards)])

    asked, own = ask(retrieved, p_len, q_len, shards)
    metas = lax.all_to_all(asked, "mem", 0, 0, tiled=True)
    gain = norm_gain.reshape(cores, 1, half)
    near = shards // 2
    steps = [(0,), (1, 2, near)] + [
        (k, near - 2 + k) if k < near else (near - 2 + k,) for k in range(3, near + 2)
    ]
    first = steps[0] + steps[1]
    rest = tuple(k for k in range(shards) if k not in first)
    sends, (table,) = pick(first, True, own, asked, metas, memory)
    asked_rows, table = lax.optimization_barrier((questions, table))
    question = project_question(
        own, questions, swap(asked_rows), gain, w_query, w_key, w_value
    )
    mine = {0: sends[0]}
    for k in first[1:]:
        mine[k] = exchange(sends[k], k)
    later, question = lax.optimization_barrier((metas, question))
    sends, _ = pick(rest, False, own, asked, later, memory)
    question, *held = lax.optimization_barrier((question, *sends.values()))
    for k, x in zip(rest, held):
        mine[k] = exchange(x, k)
    encoded = None
    shape = (1, wants, q_tokens + p_tokens, half)
    waiting = None
    for ks in steps:
        rows = [mine[k] for k in ks]
        if waiting is not None:
            *rows, ours, other = lax.optimization_barrier((*rows, *waiting[2:]))
        theirs = [swap(x) for x in rows]
        if waiting is not None:
            encoded = combine(
                waiting[0], encoded, shape, own, table, questions, waiting[1], ours, swap(other)
            )
            theirs[0], encoded = lax.optimization_barrier((theirs[0], encoded))
        made = layer(
            ks, own, table, question, gain, rows, theirs, w_query, w_key, w_value, w_out
        )
        waiting = (ks, rows, *made)
    ks, rows, ours, other = waiting
    encoded = combine(ks, encoded, shape, own, table, questions, rows, ours, swap(other))
    return encoded


def solution(mesh):
    in_specs = (
        P(("groups", "mem"), None, "tp"),
        P("mem", None, "tp"),
        P(("groups", "mem"), None),
        P(("groups", "mem")),
        P("mem"),
        P(),
        P(None, "tp"),
        P(None, "tp"),
        P(None, "tp"),
        P("tp", None),
    )
    out_specs = P(("groups", "mem"), None, None, "tp")
    return jax.shard_map(body, mesh=mesh, in_specs=in_specs, out_specs=out_specs, check_vma=False)
```

```python
import functools

import jax
import jax.numpy as jnp
from jax import lax
from jax.experimental import pallas as pl
from jax.experimental.pallas import tpu as pltpu
from jax.sharding import PartitionSpec as P

HS = 64
CAPM = 2
EPS = 1e-06
MASKED = -1e30
LANES = 128
PACK = 16
VMEM_ALL = 60 * 1024 * 1024
VMEM_LAYER = 48 * 1024 * 1024

ANY = pl.BlockSpec(memory_space=pl.ANY)
HBM = pl.BlockSpec(memory_space=pltpu.HBM)
SMEM = pl.BlockSpec(memory_space=pltpu.SMEM)
VMEM = pl.BlockSpec(memory_space=pltpu.VMEM)
LITTLE = pl.CostEstimate(flops=1, bytes_accessed=1, transcendentals=0)


def ask_kernel(pass_dev, wants, position, retrieved, p_len, q_len, metas, own_ref):
    shards = metas.shape[0]
    own_ref[0, 0] = position[0]
    own_ref[0, 1] = position[1]
    own_ref[0, 2] = q_len[0]
    for shard in range(shards):
        for r in range(CAPM):
            metas[shard, 0, r] = jnp.int32(-1)
            own_ref[1, CAPM * shard + r] = jnp.int32(-1)
        for i in range(pass_dev):
            metas[shard, 0, CAPM + i] = p_len[i]

    def place(j, carry):
        wanted = retrieved[0, j]
        shard = lax.div(wanted, pass_dev)
        taken = (metas[shard, 0, 0] >= 0).astype(jnp.int32)
        metas[shard, 0, taken] = wanted - shard * pass_dev
        own_ref[1, CAPM * shard + taken] = j
        return carry

    lax.fori_loop(0, wants, place, 0)


def ask(retrieved, p_len, q_len, shards):
    position = jnp.stack([lax.axis_index("tp"), lax.axis_index("mem")]).astype(jnp.int32)
    return pl.pallas_call(
        functools.partial(ask_kernel, p_len.shape[0], retrieved.shape[1]),
        out_shape=[
            jax.ShapeDtypeStruct((shards, 1, LANES), jnp.int32),
            jax.ShapeDtypeStruct((2, LANES), jnp.int32),
        ],
        in_specs=[SMEM] * 4,
        out_specs=[SMEM] * 2,
        cost_estimate=LITTLE,
        name="ask",
    )(position, retrieved, p_len, q_len)


def pick_kernel(ks, own_ref, asked, metas, memory, *refs):
    n = len(ks)
    outs = refs[:n]
    table = refs[n] if len(refs) > n + 2 else None
    staged, sems = refs[-2:]
    shards = metas.shape[0]
    me = own_ref[0, 1]
    found = []
    for i, k in enumerate(ks):
        partner = lax.bitwise_xor(me, k)
        for r in range(CAPM):
            local = metas[partner, 0, r]
            found.append(
                (
                    local,
                    pltpu.make_async_copy(
                        memory.at[jnp.maximum(local, 0)], staged.at[i, r], sems.at[0, i, r]
                    ),
                    pltpu.make_async_copy(staged.at[i, r], outs[i].at[r], sems.at[1, i, r]),
                )
            )

            @pl.when(local >= 0)
            def _():
                found[-1][1].start()

    if table is not None:
        for k in range(shards):
            partner = lax.bitwise_xor(me, k)
            for r in range(CAPM):
                pair = own_ref[1, CAPM * partner + r]
                local = jnp.maximum(asked[partner, 0, r], 0)
                table[0, CAPM * k + r] = pair
                table[1, CAPM * k + r] = jnp.where(
                    pair >= 0, metas[partner, 0, CAPM + local], 0
                )
    for local, come, go in found:

        @pl.when(local >= 0)
        def _():
            come.wait()
            go.start()

    for local, _, go in found:

        @pl.when(local >= 0)
        def _():
            go.wait()


def pick(ks, with_table, own, asked, metas, memory):
    n = len(ks)
    _, p_tokens, half = memory.shape
    slot = jax.ShapeDtypeStruct((CAPM, p_tokens, half), memory.dtype)
    result = pl.pallas_call(
        functools.partial(pick_kernel, ks),
        out_shape=[slot] * n + [jax.ShapeDtypeStruct((2, LANES), jnp.int32)] * with_table,
        in_specs=[SMEM, SMEM, SMEM, HBM],
        out_specs=[ANY] * n + [SMEM] * with_table,
        scratch_shapes=[
            pltpu.VMEM((n, CAPM, p_tokens, half), memory.dtype),
            pltpu.SemaphoreType.DMA((2, n, CAPM)),
        ],
        compiler_params=pltpu.CompilerParams(vmem_limit_bytes=VMEM_ALL),
        cost_estimate=LITTLE,
        name="pick",
    )(own, asked, metas, memory)
    return dict(zip(ks, result)), result[n:]


def normed_halves(own, other, gain_own, gain_other):
    own = own.astype(jnp.float32)
    other = other.astype(jnp.float32)
    total = jnp.sum(own * own + other * other, axis=-1, keepdims=True)
    scale = lax.rsqrt(total / (2 * own.shape[-1]) + EPS)
    return (
        (own * scale * gain_own).astype(jnp.bfloat16),
        (other * scale * gain_other).astype(jnp.bfloat16),
    )


def weight_copies(c, half, sources, targets, sems):
    copies = []
    for i, (source, target) in enumerate(zip(sources, targets)):
        pieces = []
        for part, core in enumerate((c, 1 - c)):
            start = pl.multiple_of(core * half, half)
            pieces.append(
                pltpu.make_async_copy(
                    source.at[pl.ds(start, half), :],
                    target.at[pl.ds(part * half, half), :],
                    sems.at[i, part],
                )
            )
        copies.append(pieces)
    return copies


def question_kernel(own_ref, mine, theirs, gain, wq, wk, wv, out, vq, vk, vv, sems):
    c = own_ref[0, 0]
    half = mine.shape[-1]
    copies = weight_copies(c, half, (wq, wk, wv), (vq, vk, vv), sems)
    for pieces in copies:
        for piece in pieces:
            piece.start()
    g_own = gain[c].astype(jnp.float32)
    g_other = gain[1 - c].astype(jnp.float32)
    first, second = normed_halves(mine[0], theirs[0], g_own, g_other)
    rows = jnp.concatenate([first, second], axis=1)
    for i, weight in enumerate((vq, vk, vv)):
        for piece in copies[i]:
            piece.wait()
        made = jnp.dot(rows, weight[...], preferred_element_type=jnp.float32)
        made = made.astype(jnp.bfloat16)
        if i == 0:
            made = made * jnp.bfloat16(1.0 / 8.0)
        out[i] = made


def project_question(own, mine, theirs, gain, wq, wk, wv):
    _, q_tokens, half = mine.shape
    width, cols = wq.shape
    weight = pltpu.VMEM((width, cols), jnp.bfloat16)
    return pl.pallas_call(
        question_kernel,
        out_shape=jax.ShapeDtypeStruct((3, q_tokens, cols), jnp.bfloat16),
        in_specs=[SMEM, VMEM, VMEM, VMEM, HBM, HBM, HBM],
        out_specs=VMEM,
        scratch_shapes=[weight] * 3 + [pltpu.SemaphoreType.DMA((3, 2))],
        compiler_params=pltpu.CompilerParams(vmem_limit_bytes=VMEM_ALL),
        cost_estimate=LITTLE,
        name="question_projections",
    )(own, mine, theirs, gain, wq, wk, wv)


def place_of(ks, s):
    return CAPM * ks[s // CAPM] + s % CAPM


def compact(table, ks, q_tokens):
    places = []
    start = jnp.int32(0)
    start_out = jnp.int32(0)
    for s in range(CAPM * len(ks)):
        p_len = table[1, place_of(ks, s)]
        room = lax.bitwise_and(p_len + (PACK - 1), ~(PACK - 1))
        places.append((p_len, pl.multiple_of(start, PACK), pl.multiple_of(start_out, PACK)))
        start = start + room
        start_out = start_out + jnp.where(p_len > 0, room + q_tokens, 0)
    return places, start_out


def pick_span(p_len, spans):
    span = jnp.int32(spans[-1][1])
    for queries, keys in reversed(spans[:-1]):
        span = jnp.where(p_len <= queries, keys, span)
    return span


def for_rows(needed, counts, run):
    least = 0
    for count in counts:

        @pl.when(jnp.logical_and(needed > least, needed <= count))
        def _():
            run(count)

        least = count


def layer_kernel(ks, own_ref, table, question, gain, *refs):
    n = len(ks)
    mine, theirs = refs[:n], refs[n : 2 * n]
    wq, wk, wv, wo = refs[2 * n : 2 * n + 4]
    out_own, out_other = refs[2 * n + 4 : 2 * n + 6]
    vq, vk, vv, vo, rows, query, key, value, attended, raw, made_out, listed = refs[
        2 * n + 6 : -4
    ]
    sems, sems_out, sems_rows, sems_made = refs[-4:]
    cols = query.shape[1]
    q_tokens = question.shape[1]
    _, p_tokens, half = mine[0].shape
    slots = CAPM * n
    total = q_tokens + p_tokens
    spans = ((3 * p_tokens // 4, 3 * p_tokens // 4), (p_tokens, p_tokens))
    c = own_ref[0, 0]
    q_len = own_ref[0, 2]
    copies = weight_copies(c, half, (wq, wk, wv), (vq, vk, vv), sems)
    out_copies = []
    for part, core in enumerate((1 - c, c)):
        start = pl.multiple_of(core * half, half)
        out_copies.append(
            pltpu.make_async_copy(wo.at[:, pl.ds(start, half)], vo.at[part], sems_out.at[part])
        )
    row_copies = []
    for part, sources in enumerate((mine, theirs)):
        for i, source in enumerate(sources):
            row_copies.append(
                pltpu.make_async_copy(source, raw.at[part, i], sems_rows.at[part, i])
            )
    for pieces in [row_copies] + copies + [out_copies]:
        for piece in pieces:
            piece.start()
    places, used_out = compact(table, ks, q_tokens)
    used = jnp.int32(0)
    valid = jnp.int32(0)
    for p_len, start, start_out in places:
        used = jnp.where(p_len > 0, jnp.maximum(used, start + pick_span(p_len, spans)), used)
        listed[0, valid] = p_len
        listed[1, valid] = start
        listed[2, valid] = start_out
        valid = valid + (p_len > 0).astype(jnp.int32)
    g_own = gain[c].astype(jnp.float32)
    g_other = gain[1 - c].astype(jnp.float32)
    for piece in row_copies:
        piece.wait()
    for s, (p_len, start, _) in enumerate(places):

        @pl.when(p_len > 0)
        def _():
            first, second = normed_halves(
                raw[0, s // CAPM, s % CAPM], raw[1, s // CAPM, s % CAPM], g_own, g_other
            )
            rows[pl.ds(start, p_tokens), :half] = first
            rows[pl.ds(start, p_tokens), half:] = second

    def project(count):
        for i, (weight, target) in enumerate(((vq, query), (vk, key), (vv, value))):
            for piece in copies[i]:
                piece.wait()
            for left in range(0, cols, 256):
                span = slice(left, left + 256)
                made = jnp.dot(
                    rows[:count], weight[:, span], preferred_element_type=jnp.float32
                ).astype(jnp.bfloat16)
                if i == 0:
                    made = made * jnp.bfloat16(1.0 / 8.0)
                target[:count, span] = made

    most = slots * p_tokens
    for_rows(used, [c for c in (128, 256, 384, 512) if most // 3 < c < most] + [most], project)

    @pl.when(used == 0)
    def _():
        for pieces in copies:
            for piece in pieces:
                piece.wait()

    lane = lax.broadcasted_iota(jnp.int32, (1, 2 * HS), 1)
    in_first = lane < HS

    def attend(p_len, start, start_out, queries, keys):
        both = q_tokens + queries
        room = -(-(q_tokens + keys) // LANES) * LANES
        spot = lax.broadcasted_iota(jnp.int32, (1, room), 1)
        end = jnp.where(spot < q_tokens, q_len, q_tokens + p_len)
        bias = jnp.where(spot < end, 0.0, MASKED)
        bias = jnp.concatenate([bias, bias], axis=1)
        one = jnp.ones((room, 2 * HS), jnp.bfloat16)

        def pair_rows(i, source, count, span):
            return jnp.concatenate(
                [question[i, :, span], source[pl.ds(start, count), span]], axis=0
            )

        def key_rows(i, source, span):
            found = pair_rows(i, source, keys, span)
            if room > found.shape[0]:
                fill = jnp.zeros((room - found.shape[0], 2 * HS), jnp.bfloat16)
                found = jnp.concatenate([found, fill], axis=0)
            return found

        def by_head(x):
            zero = jnp.zeros_like(x)
            return jnp.concatenate(
                [jnp.where(in_first, x, zero), jnp.where(in_first, zero, x)], axis=0
            )

        spans_here = [slice(left, left + 2 * HS) for left in range(0, cols, 2 * HS)]
        scores = [
            lax.dot_general(
                pair_rows(0, query, queries, span),
                by_head(key_rows(1, key, span)),
                (((1,), (1,)), ((), ())),
                preferred_element_type=jnp.float32,
            )
            + bias
            for span in spans_here
        ]
        raised = []
        for x in scores:
            halves = (x[:, :room], x[:, room:])
            raised.append(
                jnp.concatenate(
                    [
                        jnp.exp(y - jnp.max(y, axis=1, keepdims=True)).astype(jnp.bfloat16)
                        for y in halves
                    ],
                    axis=1,
                )
            )
        ones = by_head(one)
        with_sums = [
            jnp.dot(
                x,
                jnp.concatenate([by_head(key_rows(2, value, span)), ones], axis=1),
                preferred_element_type=jnp.float32,
            )
            for x, span in zip(raised, spans_here)
        ]
        for x, span in zip(with_sums, spans_here):
            attended[pl.ds(start_out, both), span] = (
                x[:, : 2 * HS] / x[:, 2 * HS :]
            ).astype(jnp.bfloat16)

    def attend_next(t, carry):
        p_len = listed[0, t]
        start = pl.multiple_of(listed[1, t], PACK)
        start_out = pl.multiple_of(listed[2, t], PACK)
        least = 0
        for queries, keys in spans:

            @pl.when(jnp.logical_and(p_len > least, p_len <= queries))
            def _():
                attend(p_len, start, start_out, queries, keys)

            least = queries
        return carry

    lax.fori_loop(0, valid, attend_next, 0)

    def put_out(count):
        for part, out in enumerate((out_other, out_own)):
            out_copies[part].wait()
            for left in range(0, half, 256):
                span = slice(left, left + 256)
                made_out[part, :count, span] = jnp.dot(
                    attended[:count], vo[part, :, span], preferred_element_type=jnp.float32
                ).astype(jnp.bfloat16)
            pltpu.make_async_copy(made_out.at[part], out, sems_made.at[part]).start()
        for part, out in enumerate((out_other, out_own)):
            pltpu.make_async_copy(made_out.at[part], out, sems_made.at[part]).wait()

    most = slots * total
    for_rows(
        used_out, [c for c in (192, 256, 384, 512, 640) if 3 * most // 8 < c < most] + [most], put_out
    )

    @pl.when(used_out == 0)
    def _():
        for piece in out_copies:
            piece.wait()


def layer(ks, own, table, question, gain, mine, theirs, wq, wk, wv, wo):
    _, p_tokens, half = mine[0].shape
    _, q_tokens, cols = question.shape
    width = wq.shape[0]
    slots = CAPM * len(ks)
    total = q_tokens + p_tokens
    weight = pltpu.VMEM((width, cols), jnp.bfloat16)
    packed = pltpu.VMEM((slots * p_tokens, cols), jnp.bfloat16)
    out = jax.ShapeDtypeStruct((slots * total, half), jnp.bfloat16)
    return pl.pallas_call(
        functools.partial(layer_kernel, ks),
        out_shape=[out, out],
        in_specs=[SMEM, SMEM, VMEM, VMEM] + [ANY] * (2 * len(ks)) + [HBM] * 4,
        out_specs=[ANY, ANY],
        scratch_shapes=[weight] * 3
        + [
            pltpu.VMEM((2, cols, half), jnp.bfloat16),
            pltpu.VMEM((slots * p_tokens, width), jnp.bfloat16),
            packed,
            packed,
            packed,
            pltpu.VMEM((slots * total, cols), jnp.bfloat16),
            pltpu.VMEM((2, len(ks), CAPM, p_tokens, half), jnp.bfloat16),
            pltpu.VMEM((2, slots * total, half), jnp.bfloat16),
            pltpu.SMEM((3, slots + 1), jnp.int32),
            pltpu.SemaphoreType.DMA((3, 2)),
            pltpu.SemaphoreType.DMA((2,)),
            pltpu.SemaphoreType.DMA((2, len(ks))),
            pltpu.SemaphoreType.DMA((2,)),
        ],
        compiler_params=pltpu.CompilerParams(vmem_limit_bytes=VMEM_LAYER),
        cost_estimate=LITTLE,
        name="layer",
    )(own, table, question, gain, *mine, *theirs, wq, wk, wv, wo)


def combine_kernel(ks, first, own_ref, table, questions, *refs):
    n = len(ks)
    mine = refs[:n]
    ours, arrived = refs[n : n + 2]
    encoded, staged, sems = refs[n + 2 if first else n + 3 :]
    slots, total, _ = staged.shape
    q_tokens = questions.shape[1]
    q_len = own_ref[0, 2]
    places, _ = compact(table, ks, q_tokens)

    def copy(s, pair):
        return pltpu.make_async_copy(staged.at[s], encoded.at[0, pair], sems.at[s])

    for s, (p_len, _, start) in enumerate(places):
        pair = table[0, place_of(ks, s)]

        @pl.when(pair >= 0)
        def _():
            for rows, low, length in (
                (questions[0], 0, q_len),
                (mine[s // CAPM][s % CAPM], q_tokens, p_len),
            ):
                count = rows.shape[0]
                spot = lax.broadcasted_iota(jnp.int32, (count, 1), 0)
                at = pl.ds(pl.multiple_of(start + low, PACK), count)
                branch = ours[at].astype(jnp.float32) + arrived[at].astype(jnp.float32)
                made = rows.astype(jnp.float32) + branch
                staged[s, low : low + count] = jnp.where(spot < length, made, 0.0).astype(
                    jnp.bfloat16
                )
            copy(s, pair).start()

    for s in range(slots):

        @pl.when(table[0, place_of(ks, s)] >= 0)
        def _():
            copy(s, 0).wait()


def combine(ks, encoded, shape, own, table, questions, mine, ours, arrived):
    first = encoded is None
    slots = CAPM * len(ks)
    operands = [own, table, questions, *mine, ours, arrived] + ([] if first else [encoded])
    return pl.pallas_call(
        functools.partial(combine_kernel, ks, first),
        out_shape=jax.ShapeDtypeStruct(shape, jnp.bfloat16),
        in_specs=[SMEM, SMEM, VMEM] + [VMEM] * (len(ks) + 2) + ([] if first else [ANY]),
        out_specs=ANY,
        scratch_shapes=[
            pltpu.VMEM((slots, *shape[2:]), jnp.bfloat16),
            pltpu.SemaphoreType.DMA((slots,)),
        ],
        input_output_aliases={} if first else {len(operands) - 1: 0},
        compiler_params=pltpu.CompilerParams(vmem_limit_bytes=VMEM_LAYER),
        cost_estimate=LITTLE,
        name="combine",
    )(*operands)


def body(questions, memory, retrieved, q_len, p_len, norm_gain, w_query, w_key, w_value, w_out):
    shards = lax.axis_size("mem")
    cores = lax.axis_size("tp")
    _, q_tokens, half = questions.shape
    p_tokens = memory.shape[1]
    wants = retrieved.shape[1]

    def swap(x):
        return lax.ppermute(x, "tp", [(i, (i + 1) % cores) for i in range(cores)])

    def exchange(x, k):
        return lax.ppermute(x, "mem", [(i, i ^ k) for i in range(shards)])

    asked, own = ask(retrieved, p_len, q_len, shards)
    metas = lax.all_to_all(asked, "mem", 0, 0, tiled=True)
    gain = norm_gain.reshape(cores, 1, half)
    near = shards // 2
    steps = [(0,), (near, 1, 2)] + [
        (near - 2 + k, k) if k < near else (near - 2 + k,) for k in range(3, near + 2)
    ]
    first = steps[0] + steps[1]
    rest = tuple(k for k in range(shards) if k not in first)
    sends, (table,) = pick(first, True, own, asked, metas, memory)
    asked_rows, table = lax.optimization_barrier((questions, table))
    question = project_question(
        own, questions, swap(asked_rows), gain, w_query, w_key, w_value
    )
    mine = {0: sends[0]}
    for k in first[1:]:
        mine[k] = exchange(sends[k], k)
    later, question = lax.optimization_barrier((metas, question))
    sends, _ = pick(rest, False, own, asked, later, memory)
    question, *held = lax.optimization_barrier((question, *sends.values()))
    for k, x in zip(rest, held):
        mine[k] = exchange(x, k)
    encoded = None
    shape = (1, wants, q_tokens + p_tokens, half)
    waiting = None
    for ks in steps:
        rows = [mine[k] for k in ks]
        if waiting is not None:
            *rows, ours, other = lax.optimization_barrier((*rows, *waiting[2:]))
            if ks == steps[-1]:
                ours, other = waiting[2:]
        theirs = [swap(x) for x in rows]
        if waiting is not None:
            encoded = combine(
                waiting[0], encoded, shape, own, table, questions, waiting[1], ours, swap(other)
            )
            theirs[0], encoded = lax.optimization_barrier((theirs[0], encoded))
        made = layer(
            ks, own, table, question, gain, rows, theirs, w_query, w_key, w_value, w_out
        )
        waiting = (ks, rows, *made)
    ks, rows, ours, other = waiting
    encoded = combine(ks, encoded, shape, own, table, questions, rows, ours, swap(other))
    return encoded


def solution(mesh):
    in_specs = (
        P(("groups", "mem"), None, "tp"),
        P("mem", None, "tp"),
        P(("groups", "mem"), None),
        P(("groups", "mem")),
        P("mem"),
        P(),
        P(None, "tp"),
        P(None, "tp"),
        P(None, "tp"),
        P("tp", None),
    )
    out_specs = P(("groups", "mem"), None, None, "tp")
    return jax.shard_map(body, mesh=mesh, in_specs=in_specs, out_specs=out_specs, check_vma=False)
```

```python
import functools

import jax
import jax.numpy as jnp
from jax import lax
from jax.experimental import pallas as pl
from jax.experimental.pallas import tpu as pltpu
from jax.sharding import PartitionSpec as P

HS = 64
CAPM = 2
EPS = 1e-06
MASKED = -1e30
LANES = 128
PACK = 16
VMEM_ALL = 60 * 1024 * 1024
VMEM_LAYER = 48 * 1024 * 1024

ANY = pl.BlockSpec(memory_space=pl.ANY)
HBM = pl.BlockSpec(memory_space=pltpu.HBM)
SMEM = pl.BlockSpec(memory_space=pltpu.SMEM)
VMEM = pl.BlockSpec(memory_space=pltpu.VMEM)
LITTLE = pl.CostEstimate(flops=1, bytes_accessed=1, transcendentals=0)


def ask_kernel(pass_dev, wants, position, retrieved, p_len, q_len, metas, own_ref):
    shards = metas.shape[0]
    own_ref[0, 0] = position[0]
    own_ref[0, 1] = position[1]
    own_ref[0, 2] = q_len[0]
    for shard in range(shards):
        for r in range(CAPM):
            metas[shard, 0, r] = jnp.int32(-1)
            own_ref[1, CAPM * shard + r] = jnp.int32(-1)
        for i in range(pass_dev):
            metas[shard, 0, CAPM + i] = p_len[i]

    def place(j, carry):
        wanted = retrieved[0, j]
        shard = lax.div(wanted, pass_dev)
        taken = (metas[shard, 0, 0] >= 0).astype(jnp.int32)
        metas[shard, 0, taken] = wanted - shard * pass_dev
        own_ref[1, CAPM * shard + taken] = j
        return carry

    lax.fori_loop(0, wants, place, 0)


def ask(retrieved, p_len, q_len, shards):
    position = jnp.stack([lax.axis_index("tp"), lax.axis_index("mem")]).astype(jnp.int32)
    return pl.pallas_call(
        functools.partial(ask_kernel, p_len.shape[0], retrieved.shape[1]),
        out_shape=[
            jax.ShapeDtypeStruct((shards, 1, LANES), jnp.int32),
            jax.ShapeDtypeStruct((2, LANES), jnp.int32),
        ],
        in_specs=[SMEM] * 4,
        out_specs=[SMEM] * 2,
        cost_estimate=LITTLE,
        name="ask",
    )(position, retrieved, p_len, q_len)


def pick_kernel(ks, own_ref, asked, metas, memory, *refs):
    n = len(ks)
    outs = refs[:n]
    table = refs[n] if len(refs) > n + 2 else None
    staged, sems = refs[-2:]
    shards = metas.shape[0]
    me = own_ref[0, 1]
    found = []
    for i, k in enumerate(ks):
        partner = lax.bitwise_xor(me, k)
        for r in range(CAPM):
            local = metas[partner, 0, r]
            found.append(
                (
                    local,
                    pltpu.make_async_copy(
                        memory.at[jnp.maximum(local, 0)], staged.at[i, r], sems.at[0, i, r]
                    ),
                    pltpu.make_async_copy(staged.at[i, r], outs[i].at[r], sems.at[1, i, r]),
                )
            )

            @pl.when(local >= 0)
            def _():
                found[-1][1].start()

    if table is not None:
        for k in range(shards):
            partner = lax.bitwise_xor(me, k)
            for r in range(CAPM):
                pair = own_ref[1, CAPM * partner + r]
                local = jnp.maximum(asked[partner, 0, r], 0)
                table[0, CAPM * k + r] = pair
                table[1, CAPM * k + r] = jnp.where(
                    pair >= 0, metas[partner, 0, CAPM + local], 0
                )
    for local, come, go in found:

        @pl.when(local >= 0)
        def _():
            come.wait()
            go.start()

    for local, _, go in found:

        @pl.when(local >= 0)
        def _():
            go.wait()


def pick(ks, with_table, own, asked, metas, memory):
    n = len(ks)
    _, p_tokens, half = memory.shape
    slot = jax.ShapeDtypeStruct((CAPM, p_tokens, half), memory.dtype)
    result = pl.pallas_call(
        functools.partial(pick_kernel, ks),
        out_shape=[slot] * n + [jax.ShapeDtypeStruct((2, LANES), jnp.int32)] * with_table,
        in_specs=[SMEM, SMEM, SMEM, HBM],
        out_specs=[ANY] * n + [SMEM] * with_table,
        scratch_shapes=[
            pltpu.VMEM((n, CAPM, p_tokens, half), memory.dtype),
            pltpu.SemaphoreType.DMA((2, n, CAPM)),
        ],
        compiler_params=pltpu.CompilerParams(vmem_limit_bytes=VMEM_ALL),
        cost_estimate=LITTLE,
        name="pick",
    )(own, asked, metas, memory)
    return dict(zip(ks, result)), result[n:]


def normed_halves(own, other, gain_own, gain_other):
    own = own.astype(jnp.float32)
    other = other.astype(jnp.float32)
    total = jnp.sum(own * own + other * other, axis=-1, keepdims=True)
    scale = lax.rsqrt(total / (2 * own.shape[-1]) + EPS)
    return (
        (own * scale * gain_own).astype(jnp.bfloat16),
        (other * scale * gain_other).astype(jnp.bfloat16),
    )


def weight_copies(c, half, sources, targets, sems):
    copies = []
    for i, (source, target) in enumerate(zip(sources, targets)):
        pieces = []
        for part, core in enumerate((c, 1 - c)):
            start = pl.multiple_of(core * half, half)
            pieces.append(
                pltpu.make_async_copy(
                    source.at[pl.ds(start, half), :],
                    target.at[pl.ds(part * half, half), :],
                    sems.at[i, part],
                )
            )
        copies.append(pieces)
    return copies


def question_kernel(own_ref, mine, theirs, gain, wq, wk, wv, out, vq, vk, vv, sems):
    c = own_ref[0, 0]
    half = mine.shape[-1]
    copies = weight_copies(c, half, (wq, wk, wv), (vq, vk, vv), sems)
    for pieces in copies:
        for piece in pieces:
            piece.start()
    g_own = gain[c].astype(jnp.float32)
    g_other = gain[1 - c].astype(jnp.float32)
    first, second = normed_halves(mine[0], theirs[0], g_own, g_other)
    rows = jnp.concatenate([first, second], axis=1)
    for i, weight in enumerate((vq, vk, vv)):
        for piece in copies[i]:
            piece.wait()
        made = jnp.dot(rows, weight[...], preferred_element_type=jnp.float32)
        made = made.astype(jnp.bfloat16)
        if i == 0:
            made = made * jnp.bfloat16(1.0 / 8.0)
        out[i] = made


def project_question(own, mine, theirs, gain, wq, wk, wv):
    _, q_tokens, half = mine.shape
    width, cols = wq.shape
    weight = pltpu.VMEM((width, cols), jnp.bfloat16)
    return pl.pallas_call(
        question_kernel,
        out_shape=jax.ShapeDtypeStruct((3, q_tokens, cols), jnp.bfloat16),
        in_specs=[SMEM, VMEM, VMEM, VMEM, HBM, HBM, HBM],
        out_specs=VMEM,
        scratch_shapes=[weight] * 3 + [pltpu.SemaphoreType.DMA((3, 2))],
        compiler_params=pltpu.CompilerParams(vmem_limit_bytes=VMEM_ALL),
        cost_estimate=LITTLE,
        name="question_projections",
    )(own, mine, theirs, gain, wq, wk, wv)


def place_of(ks, s):
    return CAPM * ks[s // CAPM] + s % CAPM


def compact(table, ks, q_tokens):
    places = []
    start = jnp.int32(0)
    start_out = jnp.int32(0)
    for s in range(CAPM * len(ks)):
        p_len = table[1, place_of(ks, s)]
        room = lax.bitwise_and(p_len + (PACK - 1), ~(PACK - 1))
        places.append((p_len, pl.multiple_of(start, PACK), pl.multiple_of(start_out, PACK)))
        start = start + room
        start_out = start_out + jnp.where(p_len > 0, room + q_tokens, 0)
    return places, start_out


def pick_span(p_len, spans):
    span = jnp.int32(spans[-1][1])
    for queries, keys in reversed(spans[:-1]):
        span = jnp.where(p_len <= queries, keys, span)
    return span


def for_rows(needed, counts, run):
    least = 0
    for count in counts:

        @pl.when(jnp.logical_and(needed > least, needed <= count))
        def _():
            run(count)

        least = count


def layer_kernel(ks, own_ref, table, question, gain, *refs):
    n = len(ks)
    mine, theirs = refs[:n], refs[n : 2 * n]
    wq, wk, wv, wo = refs[2 * n : 2 * n + 4]
    out_own, out_other = refs[2 * n + 4 : 2 * n + 6]
    vq, vk, vv, vo, rows, query, key, value, attended, raw, made_out, listed = refs[
        2 * n + 6 : -4
    ]
    sems, sems_out, sems_rows, sems_made = refs[-4:]
    cols = query.shape[1]
    q_tokens = question.shape[1]
    _, p_tokens, half = mine[0].shape
    slots = CAPM * n
    total = q_tokens + p_tokens
    spans = ((3 * p_tokens // 4, 3 * p_tokens // 4), (p_tokens, p_tokens))
    c = own_ref[0, 0]
    q_len = own_ref[0, 2]
    copies = weight_copies(c, half, (wq, wk, wv), (vq, vk, vv), sems)
    out_copies = []
    for part, core in enumerate((1 - c, c)):
        start = pl.multiple_of(core * half, half)
        out_copies.append(
            pltpu.make_async_copy(wo.at[:, pl.ds(start, half)], vo.at[part], sems_out.at[part])
        )
    row_copies = []
    for part, sources in enumerate((mine, theirs)):
        for i, source in enumerate(sources):
            row_copies.append(
                pltpu.make_async_copy(source, raw.at[part, i], sems_rows.at[part, i])
            )
    for pieces in [row_copies] + copies + [out_copies]:
        for piece in pieces:
            piece.start()
    places, used_out = compact(table, ks, q_tokens)
    used = jnp.int32(0)
    valid = jnp.int32(0)
    for p_len, start, start_out in places:
        used = jnp.where(p_len > 0, jnp.maximum(used, start + pick_span(p_len, spans)), used)
        listed[0, valid] = p_len
        listed[1, valid] = start
        listed[2, valid] = start_out
        valid = valid + (p_len > 0).astype(jnp.int32)
    g_own = gain[c].astype(jnp.float32)
    g_other = gain[1 - c].astype(jnp.float32)
    for piece in row_copies:
        piece.wait()
    for s, (p_len, start, _) in enumerate(places):

        @pl.when(p_len > 0)
        def _():
            first, second = normed_halves(
                raw[0, s // CAPM, s % CAPM], raw[1, s // CAPM, s % CAPM], g_own, g_other
            )
            rows[pl.ds(start, p_tokens), :half] = first
            rows[pl.ds(start, p_tokens), half:] = second

    def project(count):
        for i, (weight, target) in enumerate(((vq, query), (vk, key), (vv, value))):
            for piece in copies[i]:
                piece.wait()
            for left in range(0, cols, 256):
                span = slice(left, left + 256)
                made = jnp.dot(
                    rows[:count], weight[:, span], preferred_element_type=jnp.float32
                ).astype(jnp.bfloat16)
                if i == 0:
                    made = made * jnp.bfloat16(1.0 / 8.0)
                target[:count, span] = made

    most = slots * p_tokens
    for_rows(used, [c for c in (128, 256, 384, 512) if most // 3 < c < most] + [most], project)

    @pl.when(used == 0)
    def _():
        for pieces in copies:
            for piece in pieces:
                piece.wait()

    lane = lax.broadcasted_iota(jnp.int32, (1, 2 * HS), 1)
    in_first = lane < HS

    def attend(p_len, start, start_out, queries, keys):
        both = q_tokens + queries
        room = -(-(q_tokens + keys) // LANES) * LANES
        spot = lax.broadcasted_iota(jnp.int32, (1, room), 1)
        end = jnp.where(spot < q_tokens, q_len, q_tokens + p_len)
        bias = jnp.where(spot < end, 0.0, MASKED)
        bias = jnp.concatenate([bias, bias], axis=1)
        one = jnp.ones((room, 2 * HS), jnp.bfloat16)

        def pair_rows(i, source, count, span):
            return jnp.concatenate(
                [question[i, :, span], source[pl.ds(start, count), span]], axis=0
            )

        def key_rows(i, source, span):
            found = pair_rows(i, source, keys, span)
            if room > found.shape[0]:
                fill = jnp.zeros((room - found.shape[0], 2 * HS), jnp.bfloat16)
                found = jnp.concatenate([found, fill], axis=0)
            return found

        def by_head(x):
            zero = jnp.zeros_like(x)
            return jnp.concatenate(
                [jnp.where(in_first, x, zero), jnp.where(in_first, zero, x)], axis=0
            )

        spans_here = [slice(left, left + 2 * HS) for left in range(0, cols, 2 * HS)]
        scores = [
            lax.dot_general(
                pair_rows(0, query, queries, span),
                by_head(key_rows(1, key, span)),
                (((1,), (1,)), ((), ())),
                preferred_element_type=jnp.float32,
            )
            + bias
            for span in spans_here
        ]
        raised = []
        for x in scores:
            halves = (x[:, :room], x[:, room:])
            raised.append(
                jnp.concatenate(
                    [
                        jnp.exp(y - jnp.max(y, axis=1, keepdims=True)).astype(jnp.bfloat16)
                        for y in halves
                    ],
                    axis=1,
                )
            )
        ones = by_head(one)
        with_sums = [
            jnp.dot(
                x,
                jnp.concatenate([by_head(key_rows(2, value, span)), ones], axis=1),
                preferred_element_type=jnp.float32,
            )
            for x, span in zip(raised, spans_here)
        ]
        for x, span in zip(with_sums, spans_here):
            attended[pl.ds(start_out, both), span] = (
                x[:, : 2 * HS] / x[:, 2 * HS :]
            ).astype(jnp.bfloat16)

    def attend_next(t, carry):
        p_len = listed[0, t]
        start = pl.multiple_of(listed[1, t], PACK)
        start_out = pl.multiple_of(listed[2, t], PACK)
        least = 0
        for queries, keys in spans:

            @pl.when(jnp.logical_and(p_len > least, p_len <= queries))
            def _():
                attend(p_len, start, start_out, queries, keys)

            least = queries
        return carry

    lax.fori_loop(0, valid, attend_next, 0)

    def put_out(count):
        for part, out in enumerate((out_other, out_own)):
            out_copies[part].wait()
            for left in range(0, half, 256):
                span = slice(left, left + 256)
                made_out[part, :count, span] = jnp.dot(
                    attended[:count], vo[part, :, span], preferred_element_type=jnp.float32
                ).astype(jnp.bfloat16)
            pltpu.make_async_copy(made_out.at[part], out, sems_made.at[part]).start()
        for part, out in enumerate((out_other, out_own)):
            pltpu.make_async_copy(made_out.at[part], out, sems_made.at[part]).wait()

    most = slots * total
    for_rows(
        used_out, [c for c in (192, 256, 384, 512, 640) if 3 * most // 8 < c < most] + [most], put_out
    )

    @pl.when(used_out == 0)
    def _():
        for piece in out_copies:
            piece.wait()


def layer(ks, own, table, question, gain, mine, theirs, wq, wk, wv, wo):
    _, p_tokens, half = mine[0].shape
    _, q_tokens, cols = question.shape
    width = wq.shape[0]
    slots = CAPM * len(ks)
    total = q_tokens + p_tokens
    weight = pltpu.VMEM((width, cols), jnp.bfloat16)
    packed = pltpu.VMEM((slots * p_tokens, cols), jnp.bfloat16)
    out = jax.ShapeDtypeStruct((slots * total, half), jnp.bfloat16)
    return pl.pallas_call(
        functools.partial(layer_kernel, ks),
        out_shape=[out, out],
        in_specs=[SMEM, SMEM, VMEM, VMEM] + [ANY] * (2 * len(ks)) + [HBM] * 4,
        out_specs=[ANY, ANY],
        scratch_shapes=[weight] * 3
        + [
            pltpu.VMEM((2, cols, half), jnp.bfloat16),
            pltpu.VMEM((slots * p_tokens, width), jnp.bfloat16),
            packed,
            packed,
            packed,
            pltpu.VMEM((slots * total, cols), jnp.bfloat16),
            pltpu.VMEM((2, len(ks), CAPM, p_tokens, half), jnp.bfloat16),
            pltpu.VMEM((2, slots * total, half), jnp.bfloat16),
            pltpu.SMEM((3, slots + 1), jnp.int32),
            pltpu.SemaphoreType.DMA((3, 2)),
            pltpu.SemaphoreType.DMA((2,)),
            pltpu.SemaphoreType.DMA((2, len(ks))),
            pltpu.SemaphoreType.DMA((2,)),
        ],
        compiler_params=pltpu.CompilerParams(vmem_limit_bytes=VMEM_LAYER),
        cost_estimate=LITTLE,
        name="layer",
    )(own, table, question, gain, *mine, *theirs, wq, wk, wv, wo)


def combine_kernel(ks, first, own_ref, table, questions, *refs):
    n = len(ks)
    mine = refs[:n]
    ours, arrived = refs[n : n + 2]
    encoded, staged, sems = refs[n + 2 if first else n + 3 :]
    slots, total, _ = staged.shape
    q_tokens = questions.shape[1]
    q_len = own_ref[0, 2]
    places, _ = compact(table, ks, q_tokens)

    def copy(s, pair):
        return pltpu.make_async_copy(staged.at[s], encoded.at[0, pair], sems.at[s])

    for s, (p_len, _, start) in enumerate(places):
        pair = table[0, place_of(ks, s)]

        @pl.when(pair >= 0)
        def _():
            for rows, low, length in (
                (questions[0], 0, q_len),
                (mine[s // CAPM][s % CAPM], q_tokens, p_len),
            ):
                count = rows.shape[0]
                spot = lax.broadcasted_iota(jnp.int32, (count, 1), 0)
                at = pl.ds(pl.multiple_of(start + low, PACK), count)
                branch = ours[at].astype(jnp.float32) + arrived[at].astype(jnp.float32)
                made = rows.astype(jnp.float32) + branch
                staged[s, low : low + count] = jnp.where(spot < length, made, 0.0).astype(
                    jnp.bfloat16
                )
            copy(s, pair).start()

    for s in range(slots):

        @pl.when(table[0, place_of(ks, s)] >= 0)
        def _():
            copy(s, 0).wait()


def combine(ks, encoded, shape, own, table, questions, mine, ours, arrived):
    first = encoded is None
    slots = CAPM * len(ks)
    operands = [own, table, questions, *mine, ours, arrived] + ([] if first else [encoded])
    return pl.pallas_call(
        functools.partial(combine_kernel, ks, first),
        out_shape=jax.ShapeDtypeStruct(shape, jnp.bfloat16),
        in_specs=[SMEM, SMEM, VMEM] + [VMEM] * (len(ks) + 2) + ([] if first else [ANY]),
        out_specs=ANY,
        scratch_shapes=[
            pltpu.VMEM((slots, *shape[2:]), jnp.bfloat16),
            pltpu.SemaphoreType.DMA((slots,)),
        ],
        input_output_aliases={} if first else {len(operands) - 1: 0},
        compiler_params=pltpu.CompilerParams(vmem_limit_bytes=VMEM_LAYER),
        cost_estimate=LITTLE,
        name="combine",
    )(*operands)


def body(questions, memory, retrieved, q_len, p_len, norm_gain, w_query, w_key, w_value, w_out):
    shards = lax.axis_size("mem")
    cores = lax.axis_size("tp")
    _, q_tokens, half = questions.shape
    p_tokens = memory.shape[1]
    wants = retrieved.shape[1]

    def swap(x):
        return lax.ppermute(x, "tp", [(i, (i + 1) % cores) for i in range(cores)])

    def exchange(x, k):
        return lax.ppermute(x, "mem", [(i, i ^ k) for i in range(shards)])

    asked, own = ask(retrieved, p_len, q_len, shards)
    metas = lax.all_to_all(asked, "mem", 0, 0, tiled=True)
    gain = norm_gain.reshape(cores, 1, half)
    near = shards // 2
    pairs = (near - 2) // 2
    steps = (
        [(0,), (near, 1, 2)]
        + [(near + 1 + 2 * i, near + 2 + 2 * i, 3 + i) for i in range(pairs)]
        + [(shards - 1, *range(3 + pairs, near))]
    )
    first = steps[0] + steps[1]
    rest = tuple(k for k in range(shards) if k not in first)
    sends, (table,) = pick(first, True, own, asked, metas, memory)
    asked_rows, table = lax.optimization_barrier((questions, table))
    question = project_question(
        own, questions, swap(asked_rows), gain, w_query, w_key, w_value
    )
    mine = {0: sends[0]}
    for k in first[1:]:
        mine[k] = exchange(sends[k], k)
    later, question = lax.optimization_barrier((metas, question))
    sends, _ = pick(rest, False, own, asked, later, memory)
    question, *held = lax.optimization_barrier((question, *sends.values()))
    for k, x in zip(rest, held):
        mine[k] = exchange(x, k)
    encoded = None
    shape = (1, wants, q_tokens + p_tokens, half)
    waiting = None
    for ks in steps:
        rows = [mine[k] for k in ks]
        if waiting is not None:
            *rows, ours, other = lax.optimization_barrier((*rows, *waiting[2:]))
        theirs = [swap(x) for x in rows]
        if waiting is not None:
            encoded = combine(
                waiting[0], encoded, shape, own, table, questions, waiting[1], ours, swap(other)
            )
            theirs[0], encoded = lax.optimization_barrier((theirs[0], encoded))
        made = layer(
            ks, own, table, question, gain, rows, theirs, w_query, w_key, w_value, w_out
        )
        waiting = (ks, rows, *made)
    ks, rows, ours, other = waiting
    encoded = combine(ks, encoded, shape, own, table, questions, rows, ours, swap(other))
    return encoded


def solution(mesh):
    in_specs = (
        P(("groups", "mem"), None, "tp"),
        P("mem", None, "tp"),
        P(("groups", "mem"), None),
        P(("groups", "mem")),
        P("mem"),
        P(),
        P(None, "tp"),
        P(None, "tp"),
        P(None, "tp"),
        P("tp", None),
    )
    out_specs = P(("groups", "mem"), None, None, "tp")
    return jax.shard_map(body, mesh=mesh, in_specs=in_specs, out_specs=out_specs, check_vma=False)
```

```python
import functools

import jax
import jax.numpy as jnp
from jax import lax
from jax.experimental import pallas as pl
from jax.experimental.pallas import tpu as pltpu
from jax.sharding import PartitionSpec as P

HS = 64
CAPM = 2
EPS = 1e-06
MASKED = -1e30
LANES = 128
PACK = 16
VMEM_ALL = 60 * 1024 * 1024
VMEM_LAYER = 48 * 1024 * 1024

ANY = pl.BlockSpec(memory_space=pl.ANY)
HBM = pl.BlockSpec(memory_space=pltpu.HBM)
SMEM = pl.BlockSpec(memory_space=pltpu.SMEM)
VMEM = pl.BlockSpec(memory_space=pltpu.VMEM)
LITTLE = pl.CostEstimate(flops=1, bytes_accessed=1, transcendentals=0)


def ask_kernel(pass_dev, wants, position, retrieved, p_len, q_len, metas, own_ref):
    shards = metas.shape[0]
    own_ref[0, 0] = position[0]
    own_ref[0, 1] = position[1]
    own_ref[0, 2] = q_len[0]
    for shard in range(shards):
        for r in range(CAPM):
            metas[shard, 0, r] = jnp.int32(-1)
            own_ref[1, CAPM * shard + r] = jnp.int32(-1)
        for i in range(pass_dev):
            metas[shard, 0, CAPM + i] = p_len[i]

    def place(j, carry):
        wanted = retrieved[0, j]
        shard = lax.div(wanted, pass_dev)
        taken = (metas[shard, 0, 0] >= 0).astype(jnp.int32)
        metas[shard, 0, taken] = wanted - shard * pass_dev
        own_ref[1, CAPM * shard + taken] = j
        return carry

    lax.fori_loop(0, wants, place, 0)


def ask(retrieved, p_len, q_len, shards):
    position = jnp.stack([lax.axis_index("tp"), lax.axis_index("mem")]).astype(jnp.int32)
    return pl.pallas_call(
        functools.partial(ask_kernel, p_len.shape[0], retrieved.shape[1]),
        out_shape=[
            jax.ShapeDtypeStruct((shards, 1, LANES), jnp.int32),
            jax.ShapeDtypeStruct((2, LANES), jnp.int32),
        ],
        in_specs=[SMEM] * 4,
        out_specs=[SMEM] * 2,
        cost_estimate=LITTLE,
        name="ask",
    )(position, retrieved, p_len, q_len)


def pick_kernel(ks, own_ref, asked, metas, memory, *refs):
    n = len(ks)
    outs = refs[:n]
    table = refs[n] if len(refs) > n + 2 else None
    staged, sems = refs[-2:]
    shards = metas.shape[0]
    me = own_ref[0, 1]
    found = []
    for i, k in enumerate(ks):
        partner = lax.bitwise_xor(me, k)
        for r in range(CAPM):
            local = metas[partner, 0, r]
            found.append(
                (
                    local,
                    pltpu.make_async_copy(
                        memory.at[jnp.maximum(local, 0)], staged.at[i, r], sems.at[0, i, r]
                    ),
                    pltpu.make_async_copy(staged.at[i, r], outs[i].at[r], sems.at[1, i, r]),
                )
            )

            @pl.when(local >= 0)
            def _():
                found[-1][1].start()

    if table is not None:
        for k in range(shards):
            partner = lax.bitwise_xor(me, k)
            for r in range(CAPM):
                pair = own_ref[1, CAPM * partner + r]
                local = jnp.maximum(asked[partner, 0, r], 0)
                table[0, CAPM * k + r] = pair
                table[1, CAPM * k + r] = jnp.where(
                    pair >= 0, metas[partner, 0, CAPM + local], 0
                )
    for local, come, go in found:

        @pl.when(local >= 0)
        def _():
            come.wait()
            go.start()

    for local, _, go in found:

        @pl.when(local >= 0)
        def _():
            go.wait()


def pick(ks, with_table, own, asked, metas, memory):
    n = len(ks)
    _, p_tokens, half = memory.shape
    slot = jax.ShapeDtypeStruct((CAPM, p_tokens, half), memory.dtype)
    result = pl.pallas_call(
        functools.partial(pick_kernel, ks),
        out_shape=[slot] * n + [jax.ShapeDtypeStruct((2, LANES), jnp.int32)] * with_table,
        in_specs=[SMEM, SMEM, SMEM, HBM],
        out_specs=[ANY] * n + [SMEM] * with_table,
        scratch_shapes=[
            pltpu.VMEM((n, CAPM, p_tokens, half), memory.dtype),
            pltpu.SemaphoreType.DMA((2, n, CAPM)),
        ],
        compiler_params=pltpu.CompilerParams(vmem_limit_bytes=VMEM_ALL),
        cost_estimate=LITTLE,
        name="pick",
    )(own, asked, metas, memory)
    return dict(zip(ks, result)), result[n:]


def normed_halves(own, other, gain_own, gain_other):
    own = own.astype(jnp.float32)
    other = other.astype(jnp.float32)
    total = jnp.sum(own * own + other * other, axis=-1, keepdims=True)
    scale = lax.rsqrt(total / (2 * own.shape[-1]) + EPS)
    return (
        (own * scale * gain_own).astype(jnp.bfloat16),
        (other * scale * gain_other).astype(jnp.bfloat16),
    )


def weight_copies(c, half, sources, targets, sems):
    copies = []
    for i, (source, target) in enumerate(zip(sources, targets)):
        pieces = []
        for part, core in enumerate((c, 1 - c)):
            start = pl.multiple_of(core * half, half)
            pieces.append(
                pltpu.make_async_copy(
                    source.at[pl.ds(start, half), :],
                    target.at[pl.ds(part * half, half), :],
                    sems.at[i, part],
                )
            )
        copies.append(pieces)
    return copies


def question_kernel(own_ref, mine, theirs, gain, wq, wk, wv, out, vq, vk, vv, sems):
    c = own_ref[0, 0]
    half = mine.shape[-1]
    copies = weight_copies(c, half, (wq, wk, wv), (vq, vk, vv), sems)
    for pieces in copies:
        for piece in pieces:
            piece.start()
    g_own = gain[c].astype(jnp.float32)
    g_other = gain[1 - c].astype(jnp.float32)
    first, second = normed_halves(mine[0], theirs[0], g_own, g_other)
    rows = jnp.concatenate([first, second], axis=1)
    for i, weight in enumerate((vq, vk, vv)):
        for piece in copies[i]:
            piece.wait()
        made = jnp.dot(rows, weight[...], preferred_element_type=jnp.float32)
        made = made.astype(jnp.bfloat16)
        if i == 0:
            made = made * jnp.bfloat16(1.0 / 8.0)
        out[i] = made


def project_question(own, mine, theirs, gain, wq, wk, wv):
    _, q_tokens, half = mine.shape
    width, cols = wq.shape
    weight = pltpu.VMEM((width, cols), jnp.bfloat16)
    return pl.pallas_call(
        question_kernel,
        out_shape=jax.ShapeDtypeStruct((3, q_tokens, cols), jnp.bfloat16),
        in_specs=[SMEM, VMEM, VMEM, VMEM, HBM, HBM, HBM],
        out_specs=VMEM,
        scratch_shapes=[weight] * 3 + [pltpu.SemaphoreType.DMA((3, 2))],
        compiler_params=pltpu.CompilerParams(vmem_limit_bytes=VMEM_ALL),
        cost_estimate=LITTLE,
        name="question_projections",
    )(own, mine, theirs, gain, wq, wk, wv)


def place_of(ks, s):
    return CAPM * ks[s // CAPM] + s % CAPM


def compact(table, ks, q_tokens):
    places = []
    start = jnp.int32(0)
    start_out = jnp.int32(0)
    for s in range(CAPM * len(ks)):
        p_len = table[1, place_of(ks, s)]
        room = lax.bitwise_and(p_len + (PACK - 1), ~(PACK - 1))
        places.append((p_len, pl.multiple_of(start, PACK), pl.multiple_of(start_out, PACK)))
        start = start + room
        start_out = start_out + jnp.where(p_len > 0, room + q_tokens, 0)
    return places, start_out


def pick_span(p_len, spans):
    span = jnp.int32(spans[-1][1])
    for queries, keys in reversed(spans[:-1]):
        span = jnp.where(p_len <= queries, keys, span)
    return span


def for_rows(needed, counts, run):
    least = 0
    for count in counts:

        @pl.when(jnp.logical_and(needed > least, needed <= count))
        def _():
            run(count)

        least = count


def layer_kernel(ks, own_ref, table, question, gain, *refs):
    n = len(ks)
    mine, theirs = refs[:n], refs[n : 2 * n]
    wq, wk, wv, wo = refs[2 * n : 2 * n + 4]
    out_own, out_other = refs[2 * n + 4 : 2 * n + 6]
    vq, vk, vv, vo, rows, query, key, value, attended, raw, made_out, listed = refs[
        2 * n + 6 : -4
    ]
    sems, sems_out, sems_rows, sems_made = refs[-4:]
    cols = query.shape[1]
    q_tokens = question.shape[1]
    _, p_tokens, half = mine[0].shape
    slots = CAPM * n
    total = q_tokens + p_tokens
    spans = ((3 * p_tokens // 4, 3 * p_tokens // 4), (p_tokens, p_tokens))
    c = own_ref[0, 0]
    q_len = own_ref[0, 2]
    copies = weight_copies(c, half, (wq, wk, wv), (vq, vk, vv), sems)
    out_copies = []
    for part, core in enumerate((1 - c, c)):
        start = pl.multiple_of(core * half, half)
        out_copies.append(
            pltpu.make_async_copy(wo.at[:, pl.ds(start, half)], vo.at[part], sems_out.at[part])
        )
    row_copies = []
    for part, sources in enumerate((mine, theirs)):
        for i, source in enumerate(sources):
            row_copies.append(
                pltpu.make_async_copy(source, raw.at[part, i], sems_rows.at[part, i])
            )
    for pieces in [row_copies] + copies + [out_copies]:
        for piece in pieces:
            piece.start()
    places, used_out = compact(table, ks, q_tokens)
    used = jnp.int32(0)
    valid = jnp.int32(0)
    for p_len, start, start_out in places:
        used = jnp.where(p_len > 0, jnp.maximum(used, start + pick_span(p_len, spans)), used)
        listed[0, valid] = p_len
        listed[1, valid] = start
        listed[2, valid] = start_out
        valid = valid + (p_len > 0).astype(jnp.int32)
    g_own = gain[c].astype(jnp.float32)
    g_other = gain[1 - c].astype(jnp.float32)
    for piece in row_copies:
        piece.wait()
    for s, (p_len, start, _) in enumerate(places):

        @pl.when(p_len > 0)
        def _():
            first, second = normed_halves(
                raw[0, s // CAPM, s % CAPM], raw[1, s // CAPM, s % CAPM], g_own, g_other
            )
            rows[pl.ds(start, p_tokens), :half] = first
            rows[pl.ds(start, p_tokens), half:] = second

    def project(count):
        for i, (weight, target) in enumerate(((vq, query), (vk, key), (vv, value))):
            for piece in copies[i]:
                piece.wait()
            for left in range(0, cols, 256):
                span = slice(left, left + 256)
                made = jnp.dot(
                    rows[:count], weight[:, span], preferred_element_type=jnp.float32
                ).astype(jnp.bfloat16)
                if i == 0:
                    made = made * jnp.bfloat16(1.0 / 8.0)
                target[:count, span] = made

    most = slots * p_tokens
    for_rows(used, [c for c in (128, 256, 384, 512) if most // 3 < c < most] + [most], project)

    @pl.when(used == 0)
    def _():
        for pieces in copies:
            for piece in pieces:
                piece.wait()

    lane = lax.broadcasted_iota(jnp.int32, (1, 2 * HS), 1)
    in_first = lane < HS

    def attend(p_len, start, start_out, queries, keys):
        both = q_tokens + queries
        room = -(-(q_tokens + keys) // LANES) * LANES
        spot = lax.broadcasted_iota(jnp.int32, (1, room), 1)
        end = jnp.where(spot < q_tokens, q_len, q_tokens + p_len)
        bias = jnp.where(spot < end, 0.0, MASKED)
        bias = jnp.concatenate([bias, bias], axis=1)
        one = jnp.ones((room, 2 * HS), jnp.bfloat16)

        def pair_rows(i, source, count, span):
            return jnp.concatenate(
                [question[i, :, span], source[pl.ds(start, count), span]], axis=0
            )

        def key_rows(i, source, span):
            found = pair_rows(i, source, keys, span)
            if room > found.shape[0]:
                fill = jnp.zeros((room - found.shape[0], 2 * HS), jnp.bfloat16)
                found = jnp.concatenate([found, fill], axis=0)
            return found

        def by_head(x):
            zero = jnp.zeros_like(x)
            return jnp.concatenate(
                [jnp.where(in_first, x, zero), jnp.where(in_first, zero, x)], axis=0
            )

        spans_here = [slice(left, left + 2 * HS) for left in range(0, cols, 2 * HS)]
        scores = [
            lax.dot_general(
                pair_rows(0, query, queries, span),
                by_head(key_rows(1, key, span)),
                (((1,), (1,)), ((), ())),
                preferred_element_type=jnp.float32,
            )
            + bias
            for span in spans_here
        ]
        raised = []
        for x in scores:
            halves = (x[:, :room], x[:, room:])
            raised.append(
                jnp.concatenate(
                    [
                        jnp.exp(y - jnp.max(y, axis=1, keepdims=True)).astype(jnp.bfloat16)
                        for y in halves
                    ],
                    axis=1,
                )
            )
        ones = by_head(one)
        with_sums = [
            jnp.dot(
                x,
                jnp.concatenate([by_head(key_rows(2, value, span)), ones], axis=1),
                preferred_element_type=jnp.float32,
            )
            for x, span in zip(raised, spans_here)
        ]
        for x, span in zip(with_sums, spans_here):
            attended[pl.ds(start_out, both), span] = (
                x[:, : 2 * HS] / x[:, 2 * HS :]
            ).astype(jnp.bfloat16)

    def attend_next(t, carry):
        p_len = listed[0, t]
        start = pl.multiple_of(listed[1, t], PACK)
        start_out = pl.multiple_of(listed[2, t], PACK)
        least = 0
        for queries, keys in spans:

            @pl.when(jnp.logical_and(p_len > least, p_len <= queries))
            def _():
                attend(p_len, start, start_out, queries, keys)

            least = queries
        return carry

    lax.fori_loop(0, valid, attend_next, 0)

    def put_out(count):
        for part, out in enumerate((out_other, out_own)):
            out_copies[part].wait()
            for left in range(0, half, 256):
                span = slice(left, left + 256)
                made_out[part, :count, span] = jnp.dot(
                    attended[:count], vo[part, :, span], preferred_element_type=jnp.float32
                ).astype(jnp.bfloat16)
            pltpu.make_async_copy(made_out.at[part], out, sems_made.at[part]).start()
        for part, out in enumerate((out_other, out_own)):
            pltpu.make_async_copy(made_out.at[part], out, sems_made.at[part]).wait()

    most = slots * total
    for_rows(
        used_out, [c for c in (192, 256, 384, 512, 640) if 3 * most // 8 < c < most] + [most], put_out
    )

    @pl.when(used_out == 0)
    def _():
        for piece in out_copies:
            piece.wait()


def layer(ks, own, table, question, gain, mine, theirs, wq, wk, wv, wo):
    _, p_tokens, half = mine[0].shape
    _, q_tokens, cols = question.shape
    width = wq.shape[0]
    slots = CAPM * len(ks)
    total = q_tokens + p_tokens
    weight = pltpu.VMEM((width, cols), jnp.bfloat16)
    packed = pltpu.VMEM((slots * p_tokens, cols), jnp.bfloat16)
    out = jax.ShapeDtypeStruct((slots * total, half), jnp.bfloat16)
    return pl.pallas_call(
        functools.partial(layer_kernel, ks),
        out_shape=[out, out],
        in_specs=[SMEM, SMEM, VMEM, VMEM] + [ANY] * (2 * len(ks)) + [HBM] * 4,
        out_specs=[ANY, ANY],
        scratch_shapes=[weight] * 3
        + [
            pltpu.VMEM((2, cols, half), jnp.bfloat16),
            pltpu.VMEM((slots * p_tokens, width), jnp.bfloat16),
            packed,
            packed,
            packed,
            pltpu.VMEM((slots * total, cols), jnp.bfloat16),
            pltpu.VMEM((2, len(ks), CAPM, p_tokens, half), jnp.bfloat16),
            pltpu.VMEM((2, slots * total, half), jnp.bfloat16),
            pltpu.SMEM((3, slots + 1), jnp.int32),
            pltpu.SemaphoreType.DMA((3, 2)),
            pltpu.SemaphoreType.DMA((2,)),
            pltpu.SemaphoreType.DMA((2, len(ks))),
            pltpu.SemaphoreType.DMA((2,)),
        ],
        compiler_params=pltpu.CompilerParams(vmem_limit_bytes=VMEM_LAYER),
        cost_estimate=LITTLE,
        name="layer",
    )(own, table, question, gain, *mine, *theirs, wq, wk, wv, wo)


def combine_kernel(ks, first, own_ref, table, questions, *refs):
    n = len(ks)
    mine = refs[:n]
    ours, arrived = refs[n : n + 2]
    encoded, staged, sems = refs[n + 2 if first else n + 3 :]
    slots, total, _ = staged.shape
    q_tokens = questions.shape[1]
    q_len = own_ref[0, 2]
    places, _ = compact(table, ks, q_tokens)

    def copy(s, pair):
        return pltpu.make_async_copy(staged.at[s], encoded.at[0, pair], sems.at[s])

    for s, (p_len, _, start) in enumerate(places):
        pair = table[0, place_of(ks, s)]

        @pl.when(pair >= 0)
        def _():
            for rows, low, length in (
                (questions[0], 0, q_len),
                (mine[s // CAPM][s % CAPM], q_tokens, p_len),
            ):
                count = rows.shape[0]
                spot = lax.broadcasted_iota(jnp.int32, (count, 1), 0)
                at = pl.ds(pl.multiple_of(start + low, PACK), count)
                branch = ours[at].astype(jnp.float32) + arrived[at].astype(jnp.float32)
                made = rows.astype(jnp.float32) + branch
                staged[s, low : low + count] = jnp.where(spot < length, made, 0.0).astype(
                    jnp.bfloat16
                )
            copy(s, pair).start()

    for s in range(slots):

        @pl.when(table[0, place_of(ks, s)] >= 0)
        def _():
            copy(s, 0).wait()


def combine(ks, encoded, shape, own, table, questions, mine, ours, arrived):
    first = encoded is None
    slots = CAPM * len(ks)
    operands = [own, table, questions, *mine, ours, arrived] + ([] if first else [encoded])
    return pl.pallas_call(
        functools.partial(combine_kernel, ks, first),
        out_shape=jax.ShapeDtypeStruct(shape, jnp.bfloat16),
        in_specs=[SMEM, SMEM, VMEM] + [VMEM] * (len(ks) + 2) + ([] if first else [ANY]),
        out_specs=ANY,
        scratch_shapes=[
            pltpu.VMEM((slots, *shape[2:]), jnp.bfloat16),
            pltpu.SemaphoreType.DMA((slots,)),
        ],
        input_output_aliases={} if first else {len(operands) - 1: 0},
        compiler_params=pltpu.CompilerParams(vmem_limit_bytes=VMEM_LAYER),
        cost_estimate=LITTLE,
        name="combine",
    )(*operands)


def body(questions, memory, retrieved, q_len, p_len, norm_gain, w_query, w_key, w_value, w_out):
    shards = lax.axis_size("mem")
    cores = lax.axis_size("tp")
    _, q_tokens, half = questions.shape
    p_tokens = memory.shape[1]
    wants = retrieved.shape[1]

    def swap(x):
        return lax.ppermute(x, "tp", [(i, (i + 1) % cores) for i in range(cores)])

    def exchange(x, k):
        return lax.ppermute(x, "mem", [(i, i ^ k) for i in range(shards)])

    asked, own = ask(retrieved, p_len, q_len, shards)
    metas = lax.all_to_all(asked, "mem", 0, 0, tiled=True)
    gain = norm_gain.reshape(cores, 1, half)
    near = shards // 2
    far = [*range(near, shards - 2), shards - 1, shards - 2]
    steps = [(0,), (1, 2, far[0])] + [
        (k, far[k - 2]) if k < near else (far[k - 2],) for k in range(3, near + 2)
    ]
    first = steps[0] + steps[1]
    rest = tuple(k for k in range(shards) if k not in first)
    sends, (table,) = pick(first, True, own, asked, metas, memory)
    asked_rows, table = lax.optimization_barrier((questions, table))
    question = project_question(
        own, questions, swap(asked_rows), gain, w_query, w_key, w_value
    )
    mine = {0: sends[0]}
    for k in first[1:]:
        mine[k] = exchange(sends[k], k)
    later, question = lax.optimization_barrier((metas, question))
    sends, _ = pick(rest, False, own, asked, later, memory)
    question, *held = lax.optimization_barrier((question, *sends.values()))
    for k, x in zip(rest, held):
        mine[k] = exchange(x, k)
    encoded = None
    shape = (1, wants, q_tokens + p_tokens, half)
    waiting = None
    for ks in steps:
        rows = [mine[k] for k in ks]
        if waiting is not None:
            *rows, ours, other = lax.optimization_barrier((*rows, *waiting[2:]))
        theirs = [swap(x) for x in rows]
        if waiting is not None:
            encoded = combine(
                waiting[0], encoded, shape, own, table, questions, waiting[1], ours, swap(other)
            )
            theirs[0], encoded = lax.optimization_barrier((theirs[0], encoded))
        made = layer(
            ks, own, table, question, gain, rows, theirs, w_query, w_key, w_value, w_out
        )
        waiting = (ks, rows, *made)
    ks, rows, ours, other = waiting
    encoded = combine(ks, encoded, shape, own, table, questions, rows, ours, swap(other))
    return encoded


def solution(mesh):
    in_specs = (
        P(("groups", "mem"), None, "tp"),
        P("mem", None, "tp"),
        P(("groups", "mem"), None),
        P(("groups", "mem")),
        P("mem"),
        P(),
        P(None, "tp"),
        P(None, "tp"),
        P(None, "tp"),
        P("tp", None),
    )
    out_specs = P(("groups", "mem"), None, None, "tp")
    return jax.shard_map(body, mesh=mesh, in_specs=in_specs, out_specs=out_specs, check_vma=False)
```
